32 devices in a mesh: dp: 2 (over y), expert: 16 (over z, x, core).
Axes of the slice: x: 2, y: 2, z: 4, core: 2. Of those that a mesh axis runs over, the one named last changes fastest.
Arguments:
- tokens: bfloat16 [12288, 1280], P(('dp', 'expert')), may hold values from -6 to 6
- lengths: int32 [32, 4], P(('dp', 'expert')), may hold values from 1 to 288, 384 in all within a row
- routes: int32 [12288, 6], P(('dp', 'expert')), may hold values from 0 to 15, all different within a row; in each aligned block of 384 rows (0 to 383, 384 to 767, ...) at most 184 rows name the same one
- cotangent: bfloat16 [12288, 1280], P(('dp', 'expert')), may hold values from -6 to 6
- norm_gains: float32 [2, 1280], P(None, ('dp', 'expert')), may hold values from 0.5 to 1.5
- gains_m: float32 [2, 1280], P(None, ('dp', 'expert')), as said below
- gains_v: float32 [2, 1280], P(None, ('dp', 'expert')), as said below
- w_qkv: float32 [1280, 3840], P(('dp', 'expert')), may hold values from -0.15625 to 0.15625
- m_qkv: float32 [1280, 3840], P(('dp', 'expert')), as said below
- v_qkv: float32 [1280, 3840], P(('dp', 'expert')), as said below
- w_out: float32 [1280, 1280], P(('dp', 'expert')), may hold values from -1.25 to 1.25
- m_out: float32 [1280, 1280], P(('dp', 'expert')), as said below
- v_out: float32 [1280, 1280], P(('dp', 'expert')), as said below
- w_shared_in: float32 [1280, 1792], P(('dp', 'expert')), may hold values from -0.15625 to 0.15625
- m_shared_in: float32 [1280, 1792], P(('dp', 'expert')), as said below
- v_shared_in: float32 [1280, 1792], P(('dp', 'expert')), as said below
- w_shared_down: float32 [896, 1280], P(('dp', 'expert')), may hold values from -0.1875 to 0.1875
- m_shared_down: float32 [896, 1280], P(('dp', 'expert')), as said below
- v_shared_down: float32 [896, 1280], P(('dp', 'expert')), as said below
- w_router: float32 [1280, 16], P(('dp', 'expert')), may hold values from -0.078125 to 0.078125
- m_router: float32 [1280, 16], P(('dp', 'expert')), as said below
- v_router: float32 [1280, 16], P(('dp', 'expert')), as said below
- w_expert_in: float32 [16, 1280, 1792], P('expert', 'dp'), may hold values from -0.15625 to 0.15625
- m_expert_in: float32 [16, 1280, 1792], P('expert', 'dp'), as said below
- v_expert_in: float32 [16, 1280, 1792], P('expert', 'dp'), as said below
- w_expert_down: float32 [16, 896, 1280], P('expert', 'dp'), may hold values from -1.5 to 1.5
- m_expert_down: float32 [16, 896, 1280], P('expert', 'dp'), as said below
- v_expert_down: float32 [16, 896, 1280], P('expert', 'dp'), as said below
Outputs:
- mixed: bfloat16 [12288, 1280], P(('dp', 'expert'))
- input_grad: float32 [12288, 1280], P(('dp', 'expert'))
- gains_new: float32 [2, 1280], P(None, ('dp', 'expert'))
- gains_m_new: float32 [2, 1280], P(None, ('dp', 'expert'))
- gains_v_new: float32 [2, 1280], P(None, ('dp', 'expert'))
- w_qkv_new: float32 [1280, 3840], P(('dp', 'expert'))
- m_qkv_new: float32 [1280, 3840], P(('dp', 'expert'))
- v_qkv_new: float32 [1280, 3840], P(('dp', 'expert'))
- w_out_new: float32 [1280, 1280], P(('dp', 'expert'))
- m_out_new: float32 [1280, 1280], P(('dp', 'expert'))
- v_out_new: float32 [1280, 1280], P(('dp', 'expert'))
- w_shared_in_new: float32 [1280, 1792], P(('dp', 'expert'))
- m_shared_in_new: float32 [1280, 1792], P(('dp', 'expert'))
- v_shared_in_new: float32 [1280, 1792], P(('dp', 'expert'))
- w_shared_down_new: float32 [896, 1280], P(('dp', 'expert'))
- m_shared_down_new: float32 [896, 1280], P(('dp', 'expert'))
- v_shared_down_new: float32 [896, 1280], P(('dp', 'expert'))
- w_router_new: float32 [1280, 16], P(('dp', 'expert'))
- m_router_new: float32 [1280, 16], P(('dp', 'expert'))
- v_router_new: float32 [1280, 16], P(('dp', 'expert'))
- w_expert_in_new: float32 [16, 1280, 1792], P('expert', 'dp')
- m_expert_in_new: float32 [16, 1280, 1792], P('expert', 'dp')
- v_expert_in_new: float32 [16, 1280, 1792], P('expert', 'dp')
- w_expert_down_new: float32 [16, 896, 1280], P('expert', 'dp')
- m_expert_down_new: float32 [16, 896, 1280], P('expert', 'dp')
- v_expert_down_new: float32 [16, 896, 1280], P('expert', 'dp')
- grad_norm: float32 [], replicated
The draws below stay inside these ranges and needn't reach their ends.
Inputs may be any that keep to these rules, and one draw needn't show every extreme that they name: `lengths`: each row sums to 384, and its largest entry is 288. `routes`: each token names 6 different experts; of one device's tokens at most 184 name one expert, and exactly 184 in some device's tokens. `gains_m`: first moments of both signs. `gains_v`: positive. `m_qkv`: first moments of both signs. `v_qkv`: positive. `m_out`: first moments of both signs. `v_out`: positive. `m_shared_in`: first moments of both signs. `v_shared_in`: positive. `m_shared_down`: first moments of both signs. `v_shared_down`: positive. `m_router`: first moments of both signs. `v_router`: positive. `m_expert_in`: first moments of both signs. `v_expert_in`: positive. `m_expert_down`: first moments of both signs. `v_expert_down`: positive.
All inputs are finite; a program needn't handle non-finite values.
Results may differ from the reference program's by a relative error of at most 0.014.
Values may be sent and summed in bfloat16 or wider, within the bound.
A program may use at most 320 MiB of HBM per device.

```python
import math
import jax
import jax.numpy as jnp
import numpy as np
from jax import lax

D = 1280
H = 10
HD = 128
FF = 896
TOP = 6
SEQ_SLOTS = 4
ADAM_STEP = 5
TOK_DEV = 384
MAX_LEN = 288
EXPERTS = 16
CAP = 184
TOKENS = 12288
DEVICES = 32


def kind_scales():
    route_share = math.sqrt(TOP / EXPERTS)
    attend_share = math.sqrt(math.log(MAX_LEN) / MAX_LEN)
    qkv_level = 12.0 * math.sqrt(D / (H * HD)) * attend_share
    gain_level = math.sqrt((3.0 * H * HD / D * qkv_level * qkv_level + 1.44) / 2.0)
    out_level = 1.5 * attend_share
    shared_in_level = 0.55 * math.sqrt(D / FF)
    shared_down_level = 0.6
    router_level = 4.8 * math.sqrt(D) / EXPERTS * route_share
    expert_in_level = 0.55 * math.sqrt(64.0 * D / FF) / EXPERTS * route_share
    expert_down_level = 0.6 / EXPERTS * route_share
    levels = (gain_level, qkv_level, out_level, shared_in_level, shared_down_level, router_level, expert_in_level, expert_down_level)
    entry_counts = (2.0 * D, 3.0 * D * H * HD, 1.0 * H * HD * D, 2.0 * D * FF, 1.0 * FF * D, 1.0 * D * EXPERTS, 2.0 * EXPERTS * D * FF, 1.0 * EXPERTS * FF * D)
    total = 0.0
    for amount, level_value in zip(entry_counts, levels):
        total = total + amount * level_value * level_value
    whole_norm = math.sqrt(total)
    return tuple((level_value / whole_norm for level_value in levels))


def first_draw(key, array_shape, grad_scale):
    noise_draw = jax.random.normal(key, array_shape, jnp.float32)
    return 0.111 * grad_scale * noise_draw


def second_draw(key, array_shape, grad_scale):
    spread_draw = jnp.exp(jax.random.uniform(key, array_shape, jnp.float32, jnp.log(0.5), jnp.log(2.0)))
    return 0.0526 * grad_scale * grad_scale * spread_draw


def draw_gains_m(key, part):
    return first_draw(jax.random.fold_in(key, 101), (2, D), kind_scales()[0])


def draw_gains_v(key, part):
    return second_draw(jax.random.fold_in(key, 102), (2, D), kind_scales()[0])


def draw_m_qkv(key, part):
    return first_draw(jax.random.fold_in(key, 201), (D, 3 * H * HD), kind_scales()[1])


def draw_v_qkv(key, part):
    return second_draw(jax.random.fold_in(key, 202), (D, 3 * H * HD), kind_scales()[1])


def draw_m_out(key, part):
    return first_draw(jax.random.fold_in(key, 301), (H * HD, D), kind_scales()[2])


def draw_v_out(key, part):
    return second_draw(jax.random.fold_in(key, 302), (H * HD, D), kind_scales()[2])


def draw_m_shared_in(key, part):
    return first_draw(jax.random.fold_in(key, 401), (D, 2 * FF), kind_scales()[3])


def draw_v_shared_in(key, part):
    return second_draw(jax.random.fold_in(key, 402), (D, 2 * FF), kind_scales()[3])


def draw_m_shared_down(key, part):
    return first_draw(jax.random.fold_in(key, 501), (FF, D), kind_scales()[4])


def draw_v_shared_down(key, part):
    return second_draw(jax.random.fold_in(key, 502), (FF, D), kind_scales()[4])


def draw_m_router(key, part):
    return first_draw(jax.random.fold_in(key, 601), (D, EXPERTS), kind_scales()[5])


def draw_v_router(key, part):
    return second_draw(jax.random.fold_in(key, 602), (D, EXPERTS), kind_scales()[5])


def draw_m_expert_in(key, part):
    return first_draw(jax.random.fold_in(key, 701), (EXPERTS, D, 2 * FF), kind_scales()[6])


def draw_v_expert_in(key, part):
    return second_draw(jax.random.fold_in(key, 702), (EXPERTS, D, 2 * FF), kind_scales()[6])


def draw_m_expert_down(key, part):
    return first_draw(jax.random.fold_in(key, 801), (EXPERTS, FF, D), kind_scales()[7])


def draw_v_expert_down(key, part):
    return second_draw(jax.random.fold_in(key, 802), (EXPERTS, FF, D), kind_scales()[7])


def level_of(rng, dims, shards, low, high):
    gain = 1.0
    for axis_at, blocks in shards:
        steps = jax.random.uniform(jax.random.fold_in(jax.random.fold_in(rng, 6), axis_at), (blocks,), jnp.float32, low / len(shards), high / len(shards))
        gain = gain * jnp.repeat(jnp.exp(steps), dims[axis_at] // blocks).reshape((-1,) + (1,) * (len(dims) - 1 - axis_at))
    return gain


def split_up(count, total, limit, slope):
    weights = [(1 << 20) // math.isqrt(grade ** slope) + 1 for grade in range(2, count + 1)]
    surplus, counts = total - limit - (count - 1), [1] * (count - 1)
    while surplus > 0:
        movable = [i for i in range(count - 1) if counts[i] < limit]
        whole, budget = sum([weights[i] for i in movable]), surplus
        for i in movable:
            addition = min(limit - counts[i], max(1, budget * weights[i] // whole), surplus)
            counts[i] = counts[i] + addition
            surplus = surplus - addition
    return np.array([limit] + counts)


def ragged(own_key, number_of, total, bound, slope):
    if number_of == 2:
        one = jax.random.randint(own_key, (), max(1, total - bound), min(bound, total - 1) + 1)
        return jnp.stack([one, total - one])
    sizes = jnp.asarray(split_up(number_of, total, bound, slope), jnp.int32)
    twos = (number_of - 1) // 2
    source_of, taker = sizes[1:1 + 2 * twos:2], sizes[2:2 + 2 * twos:2]
    slack = jnp.minimum(source_of - 1, bound - taker)
    moved = jax.random.randint(jax.random.fold_in(own_key, 1), (twos,), 0, 1 << 20) % (slack + 1)
    sizes = sizes.at[1:1 + 2 * twos:2].set(source_of - moved).at[2:2 + 2 * twos:2].set(taker + moved)
    return sizes[jax.random.permutation(jax.random.fold_in(own_key, 2), number_of)]


def assign_block(key, own, number, rows, count, top, limit, skew):
    sequence = jax.random.permutation(key, count)
    crowded, usual = shares(count, rows * top, limit, skew, True), shares(count, rows * top, limit, skew, False)
    places = jnp.arange(count)

    def named(tallies, offset_by):
        used = int((tallies > 0).sum())
        fixed = max(1, used // 4)
        shifted = fixed + (places - fixed + offset_by * (used - fixed)) % max(1, count - fixed)
        return jnp.zeros((count,), jnp.int32).at[sequence[jnp.where(places < fixed, places, shifted)]].set(jnp.asarray(tallies, jnp.int32))

    tallies = jnp.where(number % 4 == 0, named(crowded, number // 4), named(usual, number - number // 4 - 1))
    mixed = jax.random.permutation(jax.random.fold_in(own, 3), count)
    source_of, receiver = mixed[0:count // 2 * 2:2], mixed[1:count // 2 * 2:2]
    margin = jnp.minimum(tallies[source_of] - 1, limit - tallies[receiver]) // 2
    margin = jnp.where((source_of == sequence[0]) | (receiver == sequence[0]) | (tallies[receiver] == 0), 0, jnp.maximum(margin, 0))
    shifted = jax.random.randint(jax.random.fold_in(own, 4), (count // 2,), 0, 1 << 20) % (margin + 1)
    tallies = tallies.at[source_of].add(-shifted).at[receiver].add(shifted)
    items = jnp.searchsorted(jnp.cumsum(tallies), jnp.arange(rows * top), side="right").astype(jnp.int32)
    grid = items.reshape(top, rows).T
    grid = grid[jax.random.permutation(jax.random.fold_in(own, 1), rows)]
    offset_by = jax.random.randint(jax.random.fold_in(own, 2), (rows, 1), 0, top)
    return jnp.take_along_axis(grid, (jnp.arange(top)[None, :] + offset_by) % top, axis=1)


def shares(count, total, bound, lean, full):
    loads = [(1 << 20) // math.isqrt(standing ** lean) + 1 for standing in range(1, count + 1)]
    largest = bound if full else min(bound, max(-(-total // count), total * loads[0] // sum(loads)))
    least = 1 if total - largest >= count - 1 else 0
    given, spare = [largest] + [least] * (count - 1), total - largest - least * (count - 1)
    while spare > 0:
        candidates = [i for i in range(1, count) if given[i] < largest] or [i for i in range(1, count) if given[i] < bound]
        mass, left = sum([loads[i] for i in candidates]), spare
        for i in candidates:
            addition = min(bound - given[i], max(1, left * loads[i] // mass), spare)
            given[i] = given[i] + addition
            spare = spare - addition
    return np.array(given)


def bell_draw(stream_key, shape, width, bound, cuts=(), kind=jnp.bfloat16):
    result = width * jax.random.normal(stream_key, shape, jnp.float32)
    if cuts:
        result = result * level_of(stream_key, shape, cuts, -0.22, 0.18)
    return jnp.clip(result, -bound, bound).astype(kind)


def setup_inputs(seed: int = 0) -> dict:
    key_list = jax.random.split(jax.random.key(seed), 29)
    tokens = bell_draw(key_list[0], (TOKENS, D), 1.0, 6.0, ((0, 32),))
    lengths = jax.vmap(lambda own: ragged(own, SEQ_SLOTS, TOK_DEV, MAX_LEN, 2))(jax.random.split(key_list[1], DEVICES)).reshape((DEVICES, SEQ_SLOTS)).astype(jnp.int32)
    routes_keys = jax.random.split(jax.random.fold_in(key_list[2], 1), TOKENS // TOK_DEV)
    routes_turns = jax.random.permutation(jax.random.fold_in(key_list[2], 3), TOKENS // TOK_DEV)
    routes = jax.vmap(lambda own, number: assign_block(jax.random.fold_in(key_list[2], 2), own, number, TOK_DEV, EXPERTS, TOP, CAP, 1))(routes_keys, routes_turns).reshape((TOKENS, TOP))
    cotangent = bell_draw(key_list[3], (TOKENS, D), 1.0, 6.0, ((0, 32),))
    norm_gains = jnp.clip(1.0 + 0.1 * jax.random.normal(key_list[4], (2, D), jnp.float32), 0.5, 1.5)
    gains_m = draw_gains_m(jax.random.fold_in(key_list[28], 71), 0)
    gains_v = draw_gains_v(jax.random.fold_in(key_list[28], 71), 0)
    w_qkv = bell_draw(key_list[7], (D, 3 * H * HD), D ** -0.5, 0.15625, ((0, 32),), jnp.float32)
    m_qkv = draw_m_qkv(jax.random.fold_in(key_list[28], 71), 0)
    v_qkv = draw_v_qkv(jax.random.fold_in(key_list[28], 71), 0)
    w_out = bell_draw(key_list[10], (H * HD, D), (H * HD // 64) ** -0.5, 1.25, ((0, 32),), jnp.float32)
    m_out = draw_m_out(jax.random.fold_in(key_list[28], 71), 0)
    v_out = draw_v_out(jax.random.fold_in(key_list[28], 71), 0)
    w_shared_in = bell_draw(key_list[13], (D, 2 * FF), D ** -0.5, 0.15625, ((0, 32),), jnp.float32)
    m_shared_in = draw_m_shared_in(jax.random.fold_in(key_list[28], 71), 0)
    v_shared_in = draw_v_shared_in(jax.random.fold_in(key_list[28], 71), 0)
    w_shared_down = bell_draw(key_list[16], (FF, D), FF ** -0.5, 0.1875, ((0, 32),), jnp.float32)
    m_shared_down = draw_m_shared_down(jax.random.fold_in(key_list[28], 71), 0)
    v_shared_down = draw_v_shared_down(jax.random.fold_in(key_list[28], 71), 0)
    w_router = bell_draw(key_list[19], (D, EXPERTS), (4 * D) ** -0.5, 0.078125, ((0, 32),), jnp.float32)
    m_router = draw_m_router(jax.random.fold_in(key_list[28], 71), 0)
    v_router = draw_v_router(jax.random.fold_in(key_list[28], 71), 0)
    w_expert_in = bell_draw(key_list[22], (EXPERTS, D, 2 * FF), D ** -0.5, 0.15625, ((0, 16), (1, 2)), jnp.float32)
    m_expert_in = draw_m_expert_in(jax.random.fold_in(key_list[28], 71), 0)
    v_expert_in = draw_v_expert_in(jax.random.fold_in(key_list[28], 71), 0)
    w_expert_down = bell_draw(key_list[25], (EXPERTS, FF, D), (FF // 64) ** -0.5, 1.5, ((0, 16), (1, 2)), jnp.float32)
    m_expert_down = draw_m_expert_down(jax.random.fold_in(key_list[28], 71), 0)
    v_expert_down = draw_v_expert_down(jax.random.fold_in(key_list[28], 71), 0)
    return dict(tokens=tokens, lengths=lengths, routes=routes, cotangent=cotangent, norm_gains=norm_gains, gains_m=gains_m, gains_v=gains_v, w_qkv=w_qkv, m_qkv=m_qkv, v_qkv=v_qkv, w_out=w_out, m_out=m_out, v_out=v_out, w_shared_in=w_shared_in, m_shared_in=m_shared_in, v_shared_in=v_shared_in, w_shared_down=w_shared_down, m_shared_down=m_shared_down, v_shared_down=v_shared_down, w_router=w_router, m_router=m_router, v_router=v_router, w_expert_in=w_expert_in, m_expert_in=m_expert_in, v_expert_in=v_expert_in, w_expert_down=w_expert_down, m_expert_down=m_expert_down, v_expert_down=v_expert_down)


EPS = 1e-06
ROPE_BASE = 10000.0
BETA_ONE = 0.9
BETA_TWO = 0.95
ADAM_EPS = 1e-08
DECAY = 0.1
CLIP = 1.0
GAIN_RATE = 0.5
NEGATIVE = -1e+30

@jax.custom_vjp
def low(v):
    return lax.optimization_barrier(v.astype(jnp.bfloat16)).astype(jnp.float32)

@jax.custom_vjp
def low_back(v):
    return v

def low_keep(v):
    return (low(v), None)

def low_pass(kept, grad):
    return (grad,)

def back_keep(v):
    return (v, None)

def back_low(kept, grad):
    return (low(grad),)
low.defvjp(low_keep, low_pass)
low_back.defvjp(back_keep, back_low)

def matmul(left_side, right_side):
    return jnp.dot(left_side, right_side, precision=lax.Precision.HIGHEST)

def rotary_tables(seq_lengths, row_count, head_width):
    position = jnp.arange(row_count, dtype=jnp.int32)
    seq_ends = jnp.cumsum(seq_lengths).astype(jnp.int32)
    segment = lax.optimization_barrier(jnp.sum((position[:, None] >= seq_ends[None, :]).astype(jnp.int32), axis=1))
    starts = (seq_ends - seq_lengths).astype(jnp.int32)
    slot_ids = jnp.arange(seq_lengths.shape[0], dtype=jnp.int32)
    first_row = lax.optimization_barrier(jnp.sum(jnp.where(segment[:, None] == slot_ids[None, :], starts[None, :], 0), axis=1))
    seq_place = (position - first_row).astype(jnp.float32)
    inv_freq = ROPE_BASE ** (-jnp.arange(head_width // 2, dtype=jnp.float32) * 2.0 / head_width)
    phase_angle = seq_place[:, None] * inv_freq[None, :]
    cosine = jnp.concatenate([jnp.cos(phase_angle), jnp.cos(phase_angle)], axis=1)
    sine_table = jnp.concatenate([jnp.sin(phase_angle), jnp.sin(phase_angle)], axis=1)
    allowed = (segment[:, None] == segment[None, :]) & (position[None, :] <= position[:, None])
    return (cosine, sine_table, allowed)

def rotate(vectors, cosine, sine_table):
    half_width = vectors.shape[-1] // 2
    turned = jnp.concatenate([-vectors[..., half_width:], vectors[..., :half_width]], axis=-1)
    return vectors * cosine[:, None, :] + turned * sine_table[:, None, :]

def layer(weights, inputs, seq_lengths, group_routes, row_count):
    norm_gains, w_qkv, w_out, w_shared_in, w_shared_down, w_router, w_expert_in, w_expert_down = weights
    expert_count = w_router.shape[1]
    gain_low = low(norm_gains)
    cosine, sine_table, allowed = rotary_tables(seq_lengths, row_count, HD)
    normed_one = inputs * lax.rsqrt(lax.optimization_barrier(jnp.mean(inputs * inputs, axis=-1, keepdims=True)) + EPS)
    attn_in = low(normed_one * gain_low[0])
    projected = low_back(matmul(attn_in, low(w_qkv))).reshape(row_count, 3, H, HD)
    queries = low(rotate(projected[:, 0], cosine, sine_table))
    keys_rot = low(rotate(projected[:, 1], cosine, sine_table))
    values_low = low(projected[:, 2])
    scores = low_back(jnp.einsum('qhd,khd->hqk', queries, keys_rot, precision=lax.Precision.HIGHEST) * HD ** (-0.5))
    scores = jnp.where(allowed[None], scores, NEGATIVE)
    probs_attn = jax.nn.softmax(scores, axis=-1)
    heads = jnp.einsum('hqk,khd->qhd', low(probs_attn), values_low, precision=lax.Precision.HIGHEST)
    heads = low_back(low(heads)).reshape(row_count, H * HD)
    residual = inputs + low_back(matmul(heads, low(w_out)))
    normed_two = residual * lax.rsqrt(lax.optimization_barrier(jnp.mean(residual * residual, axis=-1, keepdims=True)) + EPS)
    mlp_in = low(normed_two * gain_low[1])
    logits = low_back(matmul(mlp_in, low(w_router)))
    router_probs = jax.nn.softmax(logits, axis=-1)
    expert_ids = jnp.arange(expert_count, dtype=jnp.int32)
    chosen = lax.optimization_barrier(jnp.sum((group_routes[:, :, None] == expert_ids[None, None, :]).astype(inputs.dtype), axis=1))
    combine_weight = router_probs * chosen
    shared_gu = low_back(matmul(mlp_in, low(w_shared_in)))
    shared_act = low(jax.nn.silu(shared_gu[:, :FF]) * shared_gu[:, FF:])
    shared_out = low_back(matmul(shared_act, low(w_shared_down)))
    expert_rows = low_back(jnp.broadcast_to(mlp_in[None], (expert_count, row_count, D)))
    expert_gu = low_back(jnp.einsum('etd,edf->etf', expert_rows, low(w_expert_in), precision=lax.Precision.HIGHEST))
    expert_act = low(jax.nn.silu(expert_gu[..., :FF]) * expert_gu[..., FF:])
    expert_out = jnp.einsum('etf,efd->etd', expert_act, low(w_expert_down), precision=lax.Precision.HIGHEST)
    expert_out = low_back(low(expert_out))
    routed = jnp.einsum('te,etd->td', combine_weight, expert_out, precision=lax.Precision.HIGHEST)
    return residual + shared_out + routed

def adam_update(weight, first_moment, second_moment, gradient, factor, step_rate, decay_rate):
    clipped = gradient * factor
    first_new = BETA_ONE * first_moment + (1.0 - BETA_ONE) * clipped
    second_new = BETA_TWO * second_moment + (1.0 - BETA_TWO) * clipped * clipped
    first_hat = first_new / (1.0 - BETA_ONE ** ADAM_STEP)
    second_hat = second_new / (1.0 - BETA_TWO ** ADAM_STEP)
    weight_new = weight - step_rate * (first_hat / (jnp.sqrt(second_hat) + ADAM_EPS) + decay_rate * weight)
    return (weight_new, first_new, second_new)

def reference(tokens, lengths, routes, cotangent, norm_gains, gains_m, gains_v, w_qkv, m_qkv, v_qkv, w_out, m_out, v_out, w_shared_in, m_shared_in, v_shared_in, w_shared_down, m_shared_down, v_shared_down, w_router, m_router, v_router, w_expert_in, m_expert_in, v_expert_in, w_expert_down, m_expert_down, v_expert_down):
    groups = lengths.shape[0]
    row_count = tokens.shape[0] // groups
    params = (norm_gains, w_qkv, w_out, w_shared_in, w_shared_down, w_router, w_expert_in, w_expert_down)
    token_groups = tokens.astype(jnp.float32).reshape(groups, row_count, D)
    cot_groups = cotangent.astype(jnp.float32).reshape(groups, row_count, D)
    route_groups = routes.reshape(groups, row_count, TOP)

    def one_group(totals, pieces):
        group_tokens, seq_lengths, group_routes, group_cot = pieces

        def forward(weights, values):
            return layer(weights, values, seq_lengths, group_routes, row_count)
        outputs, pullback = jax.vjp(forward, params, group_tokens)
        weight_grads, value_grad = pullback(group_cot)
        totals = jax.tree.map(lambda summed, addend: summed + addend, totals, weight_grads)
        return (totals, (outputs.astype(jnp.bfloat16), value_grad))
    zero_tree = jax.tree.map(jnp.zeros_like, params)
    grads, (mixed_groups, grad_groups) = lax.scan(one_group, zero_tree, (token_groups, lengths, route_groups, cot_groups))
    squares = sum((jnp.sum(grad_part * grad_part) for grad_part in grads))
    grad_norm = jnp.sqrt(squares)
    factor = jnp.minimum(1.0, CLIP / grad_norm)
    rates = (GAIN_RATE, D ** (-0.5), (H * HD // 64) ** (-0.5), D ** (-0.5), FF ** (-0.5), (4 * D) ** (-0.5), D ** (-0.5), (FF // 64) ** (-0.5))
    decays = (0.0, DECAY, DECAY, DECAY, DECAY, DECAY, DECAY, DECAY)
    firsts = (gains_m, m_qkv, m_out, m_shared_in, m_shared_down, m_router, m_expert_in, m_expert_down)
    seconds = (gains_v, v_qkv, v_out, v_shared_in, v_shared_down, v_router, v_expert_in, v_expert_down)
    updated = []
    for weight, first_moment, second_moment, gradient, step_rate, decay_rate in zip(params, firsts, seconds, grads, rates, decays):
        updated.extend(adam_update(weight, first_moment, second_moment, gradient, factor, step_rate, decay_rate))
    mixed = mixed_groups.reshape(tokens.shape[0], D)
    input_grad = grad_groups.reshape(tokens.shape[0], D)
    return (mixed, input_grad, updated[0], updated[1], updated[2], updated[3], updated[4], updated[5], updated[6], updated[7], updated[8], updated[9], updated[10], updated[11], updated[12], updated[13], updated[14], updated[15], updated[16], updated[17], updated[18], updated[19], updated[20], updated[21], updated[22], updated[23], grad_norm)
```

```python
import jax
import jax.numpy as jnp
from jax import lax
from jax.sharding import PartitionSpec as P

D = 1280
H = 10
HD = 128
FF = 896
TOP = 6
ADAM_STEP = 5


EPS = 1e-06
ROPE_BASE = 10000.0
BETA_ONE = 0.9
BETA_TWO = 0.95
ADAM_EPS = 1e-08
DECAY = 0.1
CLIP = 1.0
GAIN_RATE = 0.5
NEGATIVE = -1e30


def rms_scale(values):
    return lax.rsqrt(jnp.mean(values * values, axis=-1, keepdims=True) + EPS)


def rotary_tables(seq_lengths, row_count, head_width):
    position = jnp.arange(row_count, dtype=jnp.int32)
    seq_ends = jnp.cumsum(seq_lengths)
    segment = jnp.sum((position[:, None] >= seq_ends[None, :]).astype(jnp.int32), axis=1)
    starts = seq_ends - seq_lengths
    slot_ids = jnp.arange(seq_lengths.shape[0], dtype=jnp.int32)
    first_row = jnp.sum(
        jnp.where(segment[:, None] == slot_ids[None, :], starts[None, :], 0), axis=1
    )
    seq_place = (position - first_row).astype(jnp.float32)
    inv_freq = ROPE_BASE ** (-jnp.arange(head_width // 2, dtype=jnp.float32) * 2.0 / head_width)
    phase_angle = seq_place[:, None] * inv_freq[None, :]
    cosine = jnp.concatenate([jnp.cos(phase_angle), jnp.cos(phase_angle)], axis=1)
    sine_table = jnp.concatenate([jnp.sin(phase_angle), jnp.sin(phase_angle)], axis=1)
    allowed = (segment[:, None] == segment[None, :]) & (position[None, :] <= position[:, None])
    return (cosine, sine_table, allowed)


def rotate(vectors, cosine, sine_table):
    half_width = vectors.shape[-1] // 2
    turned = jnp.concatenate([-vectors[..., half_width:], vectors[..., :half_width]], axis=-1)
    return vectors * cosine[:, None, :] + turned * sine_table[:, None, :]


def rotate_back(gradient, cosine, sine_table):
    half_width = gradient.shape[-1] // 2
    scaled_sine = gradient * sine_table[:, None, :]
    turned = jnp.concatenate(
        [scaled_sine[..., half_width:], -scaled_sine[..., :half_width]], axis=-1
    )
    return gradient * cosine[:, None, :] + turned


def silu_slope(gate_vals):
    logistic = jax.nn.sigmoid(gate_vals)
    return logistic * (1.0 + gate_vals * (1.0 - logistic))


def swiglu_back(act_grad, gate_up):
    gate_part = gate_up[:, :FF]
    up_part = gate_up[:, FF:]
    return jnp.concatenate(
        [act_grad * up_part * silu_slope(gate_part), act_grad * jax.nn.silu(gate_part)], axis=1
    ).astype(jnp.bfloat16)


def adam_update(weight, first_moment, second_moment, gradient, factor, step_rate, decay_rate):
    clipped = gradient * factor
    first_new = BETA_ONE * first_moment + (1.0 - BETA_ONE) * clipped
    second_new = BETA_TWO * second_moment + (1.0 - BETA_TWO) * clipped * clipped
    first_hat = first_new / (1.0 - BETA_ONE**ADAM_STEP)
    second_hat = second_new / (1.0 - BETA_TWO**ADAM_STEP)
    weight_new = weight - step_rate * (
        first_hat / (jnp.sqrt(second_hat) + ADAM_EPS) + decay_rate * weight
    )
    return (weight_new, first_new, second_new)


def local(
    tokens,
    lengths,
    routes,
    cotangent,
    norm_gains,
    gains_m,
    gains_v,
    w_qkv,
    m_qkv,
    v_qkv,
    w_out,
    m_out,
    v_out,
    w_shared_in,
    m_shared_in,
    v_shared_in,
    w_shared_down,
    m_shared_down,
    v_shared_down,
    w_router,
    m_router,
    v_router,
    w_expert_in,
    m_expert_in,
    v_expert_in,
    w_expert_down,
    m_expert_down,
    v_expert_down,
):
    both = ("dp", "expert")
    low = jnp.bfloat16
    wide = jnp.float32
    row_count = tokens.shape[0]
    expert_count = w_router.shape[1]
    n_dp = lax.axis_size("dp")
    n_exp = lax.axis_size("expert")
    n_all = n_dp * n_exp
    capacity = min(row_count, (5 * row_count * TOP // (4 * expert_count) + 7) // 8 * 8)
    score_scale = HD ** (-0.5)
    rows_w = w_qkv.shape[0]
    unit = w_shared_down.shape[0]
    my_expert = lax.axis_index("expert")

    small = jnp.concatenate([w_router, norm_gains.T], axis=1).astype(low)
    qkv_full = lax.all_gather(w_qkv.astype(low), both, axis=0, tiled=True)
    small_full = lax.all_gather(small, both, axis=0, tiled=True)
    out_full = lax.all_gather(w_out.astype(low), both, axis=0, tiled=True)
    router_full = small_full[:, :expert_count]
    gain_one = small_full[:, expert_count].astype(wide)
    gain_two = small_full[:, expert_count + 1].astype(wide)
    cot_all = lax.all_gather(cotangent, "expert", axis=0, tiled=False)
    routes_all = lax.all_gather(routes, "expert", axis=0, tiled=False)
    expert_in_full = lax.all_gather(w_expert_in[0].astype(low), "dp", axis=0, tiled=True)
    expert_down_full = lax.all_gather(w_expert_down[0].astype(low), "dp", axis=0, tiled=True)
    shin_send = (
        w_shared_in.astype(low)
        .reshape(rows_w, 2, n_dp, n_exp, unit)
        .transpose(3, 0, 1, 2, 4)
        .reshape(n_exp, rows_w, 2 * n_dp * unit)
    )
    shin_send = jnp.concatenate([shin_send] * n_dp, axis=0)
    shin_mine = lax.all_to_all(shin_send, both, 0, 0, tiled=True).reshape(D, 2 * n_dp * unit)
    shdown_mine = lax.all_gather(w_shared_down.astype(low), "dp", axis=0, tiled=True)
    half = n_dp * unit

    inputs = tokens.astype(wide)
    cosine, sine_table, allowed = rotary_tables(lengths[0], row_count, HD)
    scale_one = rms_scale(inputs)
    normed_one = inputs * scale_one
    attn_in = (normed_one * gain_one).astype(low)
    projected = jnp.dot(attn_in, qkv_full, preferred_element_type=wide).reshape(
        row_count, 3, H, HD
    )
    queries = rotate(projected[:, 0], cosine, sine_table).astype(low)
    keys_rot = rotate(projected[:, 1], cosine, sine_table).astype(low)
    values_low = projected[:, 2].astype(low)
    raw_scores = (
        jnp.einsum("qhd,khd->hqk", queries, keys_rot, preferred_element_type=wide) * score_scale
    )
    scores = jnp.where(allowed[None], raw_scores, NEGATIVE)
    row_max = jnp.max(scores, axis=-1, keepdims=True)
    exped = jnp.exp(scores - row_max)
    probs_attn = exped / jnp.sum(exped, axis=-1, keepdims=True)
    probs_low = probs_attn.astype(low)
    mixed_heads = jnp.einsum("hqk,khd->qhd", probs_low, values_low, preferred_element_type=wide)
    heads_low = mixed_heads.astype(low).reshape(row_count, H * HD)
    residual = inputs + jnp.dot(heads_low, out_full, preferred_element_type=wide)
    scale_two = rms_scale(residual)
    normed_two = residual * scale_two
    mlp_in = (normed_two * gain_two).astype(low)
    logits = jnp.dot(mlp_in, router_full, preferred_element_type=wide)
    router_probs = jax.nn.softmax(logits, axis=-1)

    mlp_all = lax.all_gather(mlp_in, "expert", axis=0, tiled=False)
    mlp_flat = mlp_all.reshape(n_exp * row_count, D)
    fused_w = jnp.concatenate([shin_mine, router_full], axis=1)
    fused = jnp.dot(mlp_flat, fused_w, preferred_element_type=wide)
    shared_gate = fused[:, :half]
    shared_up = fused[:, half : 2 * half]
    probs_all = jax.nn.softmax(fused[:, 2 * half :], axis=-1)
    expert_ids = jnp.arange(expert_count, dtype=jnp.int32)
    my_prob = jnp.sum(jnp.where(expert_ids[None, :] == my_expert, probs_all, 0.0), axis=1)
    my_prob = my_prob.reshape(n_exp, row_count)
    routed_here = jnp.any(routes_all == my_expert, axis=2)
    rank = jnp.cumsum(routed_here.astype(jnp.int32), axis=1) - 1
    slot = jnp.arange(capacity, dtype=jnp.int32)
    pick_mask = routed_here[:, None, :] & (rank[:, None, :] == slot[None, :, None])
    pick = pick_mask.astype(low)
    picked_in = jnp.einsum("nst,ntd->nsd", pick, mlp_all, preferred_element_type=wide).astype(low)
    picked_cot = jnp.einsum("nst,ntd->nsd", pick, cot_all, preferred_element_type=wide).astype(low)
    picked_gate = jnp.sum(jnp.where(pick_mask, my_prob[:, None, :], 0.0), axis=2).reshape(-1, 1)
    flat_in = picked_in.reshape(-1, D)
    flat_cot = picked_cot.reshape(-1, D).astype(wide)
    gate_up = jnp.dot(flat_in, expert_in_full, preferred_element_type=wide)
    activation = (jax.nn.silu(gate_up[:, :FF]) * gate_up[:, FF:]).astype(low)
    result = jnp.dot(activation, expert_down_full, preferred_element_type=wide).astype(low)
    result = result.astype(wide)
    gate_grad = jnp.sum(flat_cot * result, axis=1).reshape(n_exp, capacity, 1)
    weighted = (picked_gate * result).astype(low).reshape(n_exp, capacity, D)
    shared_act = (jax.nn.silu(shared_gate) * shared_up).astype(low)
    mixed_part = jnp.einsum("nst,nsd->ntd", pick, weighted, preferred_element_type=wide)
    mixed_part = mixed_part.reshape(-1, D) + jnp.dot(
        shared_act, shdown_mine, preferred_element_type=wide
    )
    mixed_sum = lax.psum_scatter(
        mixed_part.astype(low), "expert", scatter_dimension=0, tiled=True
    )
    mixed = (residual + mixed_sum.astype(wide)).astype(low)

    cot_flat = cot_all.reshape(n_exp * row_count, D)
    grad_shdown = jnp.einsum("tf,td->fd", shared_act, cot_flat, preferred_element_type=wide)
    shared_act_grad = jnp.einsum("td,fd->tf", cot_flat, shdown_mine, preferred_element_type=wide)
    shared_gu_grad = jnp.concatenate(
        [
            shared_act_grad * shared_up * silu_slope(shared_gate),
            shared_act_grad * jax.nn.silu(shared_gate),
        ],
        axis=1,
    ).astype(low)
    grad_shin = jnp.einsum("td,tf->df", mlp_flat, shared_gu_grad, preferred_element_type=wide)
    grad_rows = (picked_gate * flat_cot).astype(low)
    grad_edown = jnp.einsum("rf,rd->fd", activation, grad_rows, preferred_element_type=wide)
    expert_act_grad = jnp.einsum(
        "rd,fd->rf", grad_rows, expert_down_full, preferred_element_type=wide
    )
    expert_gu_grad = swiglu_back(expert_act_grad, gate_up)
    grad_ein = jnp.einsum("rd,rf->df", flat_in, expert_gu_grad, preferred_element_type=wide)
    input_back = jnp.einsum(
        "rf,df->rd", expert_gu_grad, expert_in_full, preferred_element_type=wide
    )
    input_back = input_back.astype(low).reshape(n_exp, capacity, D)
    back_part = jnp.einsum("nst,nsd->ntd", pick, input_back, preferred_element_type=wide)
    back_part = back_part.reshape(-1, D) + jnp.einsum(
        "tf,df->td", shared_gu_grad, shin_mine, preferred_element_type=wide
    )
    back_sum = lax.psum_scatter(back_part.astype(low), "expert", scatter_dimension=0, tiled=True)
    gate_grad_tok = jnp.sum(jnp.where(pick_mask, gate_grad, 0.0), axis=1)
    prob_grad = lax.all_to_all(gate_grad_tok, "expert", 0, 0, tiled=True).T
    logit_grad = (
        router_probs * (prob_grad - jnp.sum(prob_grad * router_probs, axis=-1, keepdims=True))
    ).astype(low)
    grad_router = jnp.einsum("td,te->de", mlp_in, logit_grad, preferred_element_type=wide)
    mlp_in_grad = back_sum.astype(wide) + jnp.einsum(
        "te,de->td", logit_grad, router_full, preferred_element_type=wide
    )
    out_grad = cotangent.astype(wide)
    grad_gain_two = jnp.sum(mlp_in_grad * normed_two, axis=0)
    scaled_two = mlp_in_grad * gain_two
    resid_grad = out_grad + scale_two * (
        scaled_two - normed_two * jnp.mean(scaled_two * normed_two, axis=-1, keepdims=True)
    )
    resid_low = resid_grad.astype(low)
    grad_out = jnp.einsum("ti,td->id", heads_low, resid_low, preferred_element_type=wide)
    heads_grad = jnp.einsum("td,id->ti", resid_low, out_full, preferred_element_type=wide)
    heads_grad = heads_grad.astype(low).reshape(row_count, H, HD)
    attn_prob_grad = jnp.einsum("qhd,khd->hqk", heads_grad, values_low, preferred_element_type=wide)
    value_grad = jnp.einsum("hqk,qhd->khd", probs_low, heads_grad, preferred_element_type=wide)
    score_grad = probs_attn * (
        attn_prob_grad - jnp.sum(attn_prob_grad * probs_attn, axis=-1, keepdims=True)
    )
    score_grad = score_grad.astype(low)
    query_grad = (
        jnp.einsum("hqk,khd->qhd", score_grad, keys_rot, preferred_element_type=wide) * score_scale
    )
    key_grad = (
        jnp.einsum("hqk,qhd->khd", score_grad, queries, preferred_element_type=wide) * score_scale
    )
    projected_grad = jnp.stack(
        [
            rotate_back(query_grad, cosine, sine_table),
            rotate_back(key_grad, cosine, sine_table),
            value_grad,
        ],
        axis=1,
    )
    projected_grad = projected_grad.reshape(row_count, 3 * H * HD).astype(low)
    grad_qkv = jnp.einsum("td,tk->dk", attn_in, projected_grad, preferred_element_type=wide)
    attn_grad = jnp.einsum("tk,dk->td", projected_grad, qkv_full, preferred_element_type=wide)
    grad_gain_one = jnp.sum(attn_grad * normed_one, axis=0)
    scaled_one = attn_grad * gain_one
    input_grad = resid_grad + scale_one * (
        scaled_one - normed_one * jnp.mean(scaled_one * normed_one, axis=-1, keepdims=True)
    )

    small_grad = jnp.concatenate(
        [grad_router, grad_gain_one[:, None], grad_gain_two[:, None]], axis=1
    )
    small_own = lax.psum_scatter(small_grad, both, scatter_dimension=0, tiled=True)
    shin_back = lax.all_to_all(
        grad_shin.astype(low).reshape(n_all, rows_w, 2 * half), both, 0, 0, tiled=True
    )
    shin_own = jnp.sum(
        shin_back.reshape(n_dp, n_exp, rows_w, 2, n_dp, unit).astype(wide), axis=0
    )
    shin_own = shin_own.transpose(1, 2, 3, 0, 4).reshape(rows_w, 2 * FF)
    owned_grads = (
        small_own[:, expert_count:].T,
        lax.psum_scatter(grad_qkv.astype(low), both, scatter_dimension=0, tiled=True).astype(wide),
        lax.psum_scatter(grad_out.astype(low), both, scatter_dimension=0, tiled=True).astype(wide),
        shin_own,
        lax.psum_scatter(grad_shdown, "dp", scatter_dimension=0, tiled=True),
        small_own[:, :expert_count],
        lax.psum_scatter(
            grad_ein[None].astype(low), "dp", scatter_dimension=1, tiled=True
        ).astype(wide),
        lax.psum_scatter(
            grad_edown[None].astype(low), "dp", scatter_dimension=1, tiled=True
        ).astype(wide),
    )
    squares = sum((jnp.sum(grad_part * grad_part) for grad_part in owned_grads))
    total_squares = lax.psum(squares, ("dp", "expert"))
    grad_norm = jnp.sqrt(total_squares)
    factor = jnp.minimum(1.0, CLIP / grad_norm)
    weights = (
        norm_gains,
        w_qkv,
        w_out,
        w_shared_in,
        w_shared_down,
        w_router,
        w_expert_in,
        w_expert_down,
    )
    firsts = (
        gains_m,
        m_qkv,
        m_out,
        m_shared_in,
        m_shared_down,
        m_router,
        m_expert_in,
        m_expert_down,
    )
    seconds = (
        gains_v,
        v_qkv,
        v_out,
        v_shared_in,
        v_shared_down,
        v_router,
        v_expert_in,
        v_expert_down,
    )
    rates = (
        GAIN_RATE,
        D ** (-0.5),
        (H * HD // 64) ** (-0.5),
        D ** (-0.5),
        FF ** (-0.5),
        (4 * D) ** (-0.5),
        D ** (-0.5),
        (FF // 64) ** (-0.5),
    )
    decays = (0.0, DECAY, DECAY, DECAY, DECAY, DECAY, DECAY, DECAY)
    updated = []
    for weight, first_moment, second_moment, gradient, step_rate, decay_rate in zip(
        weights, firsts, seconds, owned_grads, rates, decays
    ):
        updated.extend(
            adam_update(
                weight, first_moment, second_moment, gradient, factor, step_rate, decay_rate
            )
        )
    return (
        mixed,
        input_grad,
        updated[0],
        updated[1],
        updated[2],
        updated[3],
        updated[4],
        updated[5],
        updated[6],
        updated[7],
        updated[8],
        updated[9],
        updated[10],
        updated[11],
        updated[12],
        updated[13],
        updated[14],
        updated[15],
        updated[16],
        updated[17],
        updated[18],
        updated[19],
        updated[20],
        updated[21],
        updated[22],
        updated[23],
        grad_norm,
    )


def solution(mesh):
    placed = (
        P(("dp", "expert"), None),
        P(("dp", "expert"), None),
        P(("dp", "expert"), None),
        P(("dp", "expert"), None),
        P(None, ("dp", "expert")),
        P(None, ("dp", "expert")),
        P(None, ("dp", "expert")),
        P(("dp", "expert"), None),
        P(("dp", "expert"), None),
        P(("dp", "expert"), None),
        P(("dp", "expert"), None),
        P(("dp", "expert"), None),
        P(("dp", "expert"), None),
        P(("dp", "expert"), None),
        P(("dp", "expert"), None),
        P(("dp", "expert"), None),
        P(("dp", "expert"), None),
        P(("dp", "expert"), None),
        P(("dp", "expert"), None),
        P(("dp", "expert"), None),
        P(("dp", "expert"), None),
        P(("dp", "expert"), None),
        P("expert", "dp", None),
        P("expert", "dp", None),
        P("expert", "dp", None),
        P("expert", "dp", None),
        P("expert", "dp", None),
        P("expert", "dp", None),
    )
    return jax.shard_map(
        local,
        mesh=mesh,
        in_specs=placed,
        out_specs=(
            P(("dp", "expert"), None),
            P(("dp", "expert"), None),
            P(None, ("dp", "expert")),
            P(None, ("dp", "expert")),
            P(None, ("dp", "expert")),
            P(("dp", "expert"), None),
            P(("dp", "expert"), None),
            P(("dp", "expert"), None),
            P(("dp", "expert"), None),
            P(("dp", "expert"), None),
            P(("dp", "expert"), None),
            P(("dp", "expert"), None),
            P(("dp", "expert"), None),
            P(("dp", "expert"), None),
            P(("dp", "expert"), None),
            P(("dp", "expert"), None),
            P(("dp", "expert"), None),
            P(("dp", "expert"), None),
            P(("dp", "expert"), None),
            P(("dp", "expert"), None),
            P("expert", "dp", None),
            P("expert", "dp", None),
            P("expert", "dp", None),
            P("expert", "dp", None),
            P("expert", "dp", None),
            P("expert", "dp", None),
            P(),
        ),
        check_vma=False,
    )
```

```python
import functools
import itertools

import jax
import jax.numpy as jnp
from jax import lax
from jax.experimental import pallas as pl
from jax.experimental.pallas import tpu as pltpu
from jax.sharding import PartitionSpec as P

D = 1280
H = 10
HD = 128
FF = 896
TOP = 6
ADAM_STEP = 5


EPS = 1e-06
ROPE_BASE = 10000.0
BETA_ONE = 0.9
BETA_TWO = 0.95
ADAM_EPS = 1e-08
DECAY = 0.1
CLIP = 1.0
GAIN_RATE = 0.5
NEGATIVE = -1e30


def rms_scale(values):
    return lax.rsqrt(jnp.mean(values * values, axis=-1, keepdims=True) + EPS)


def rotary_tables(seq_lengths, row_count, head_width):
    position = jnp.arange(row_count, dtype=jnp.int32)
    seq_ends = jnp.cumsum(seq_lengths)
    segment = jnp.sum((position[:, None] >= seq_ends[None, :]).astype(jnp.int32), axis=1)
    starts = seq_ends - seq_lengths
    slot_ids = jnp.arange(seq_lengths.shape[0], dtype=jnp.int32)
    first_row = jnp.sum(
        jnp.where(segment[:, None] == slot_ids[None, :], starts[None, :], 0), axis=1
    )
    seq_place = (position - first_row).astype(jnp.float32)
    inv_freq = ROPE_BASE ** (-jnp.arange(head_width // 2, dtype=jnp.float32) * 2.0 / head_width)
    phase_angle = seq_place[:, None] * inv_freq[None, :]
    cosine = jnp.concatenate([jnp.cos(phase_angle), jnp.cos(phase_angle)], axis=1)
    sine_table = jnp.concatenate([jnp.sin(phase_angle), jnp.sin(phase_angle)], axis=1)
    allowed = (segment[:, None] == segment[None, :]) & (position[None, :] <= position[:, None])
    return (cosine, sine_table, allowed)


def rotate(vectors, cosine, sine_table):
    half_width = vectors.shape[-1] // 2
    turned = jnp.concatenate([-vectors[..., half_width:], vectors[..., :half_width]], axis=-1)
    return vectors * cosine[:, None, :] + turned * sine_table[:, None, :]


def rotate_back(gradient, cosine, sine_table):
    half_width = gradient.shape[-1] // 2
    scaled_sine = gradient * sine_table[:, None, :]
    turned = jnp.concatenate(
        [scaled_sine[..., half_width:], -scaled_sine[..., :half_width]], axis=-1
    )
    return gradient * cosine[:, None, :] + turned


def silu_slope(gate_vals):
    logistic = jax.nn.sigmoid(gate_vals)
    return logistic * (1.0 + gate_vals * (1.0 - logistic))


def swiglu_back(act_grad, gate_up):
    gate_part = gate_up[:, :FF]
    up_part = gate_up[:, FF:]
    return jnp.concatenate(
        [act_grad * up_part * silu_slope(gate_part), act_grad * jax.nn.silu(gate_part)], axis=1
    ).astype(jnp.bfloat16)


def adam_update(weight, first_moment, second_moment, gradient, factor, step_rate, decay_rate):
    clipped = gradient * factor
    first_new = BETA_ONE * first_moment + (1.0 - BETA_ONE) * clipped
    second_new = BETA_TWO * second_moment + (1.0 - BETA_TWO) * clipped * clipped
    first_hat = first_new / (1.0 - BETA_ONE**ADAM_STEP)
    second_hat = second_new / (1.0 - BETA_TWO**ADAM_STEP)
    weight_new = weight - step_rate * (
        first_hat / (jnp.sqrt(second_hat) + ADAM_EPS) + decay_rate * weight
    )
    return (weight_new, first_new, second_new)


MESH = pl.DeviceIdType.MESH


class Place:
    def __init__(self, n_dp, n_exp):
        rest = n_exp // 2
        na = 4 if rest % 4 == 0 else rest
        self.size = {"A": na, "B": rest // na, "C": 2, "Y": n_dp}
        e = lax.axis_index("expert")
        nb = self.size["B"]
        self.pos = {"A": e // (2 * nb), "B": (e // 2) % nb, "C": e % 2, "Y": lax.axis_index("dp")}

    def expert(self, pos):
        return (pos["A"] * self.size["B"] + pos["B"]) * 2 + pos["C"]

    def flat(self, pos):
        return pos["Y"] * (2 * self.size["A"] * self.size["B"]) + self.expert(pos)

    def device(self, pos):
        return (pos["Y"], self.expert(pos))

    def moved(self, **steps):
        pos = dict(self.pos)
        for axis, step in steps.items():
            if axis == "A":
                pos[axis] = pos[axis] + step
            else:
                pos[axis] = lax.rem(pos[axis] + step, self.size[axis])
        return pos

    def inside(self, step):
        there = self.pos["A"] + step
        return (there >= 0) & (there < self.size["A"])

    def greet(self, axes, line_all):
        barrier = pltpu.get_barrier_semaphore()
        total = 0
        for axis in axes:
            if axis == "A":
                reach = range(1, self.size["A"]) if line_all else (1,)
                for step in [s * d for d in reach for s in (1, -1)]:
                    near = self.inside(step)

                    @pl.when(near)
                    def _(step=step):
                        pl.semaphore_signal(barrier, inc=1, device_id=self.device(self.moved(A=step)), device_id_type=MESH)

                    total = total + jnp.where(near, 1, 0)
            else:
                for step in range(1, self.size[axis]):
                    pl.semaphore_signal(barrier, inc=1, device_id=self.device(self.moved(**{axis: step})), device_id_type=MESH)
                    total = total + 1
        pl.semaphore_wait(barrier, total)


def under(conds, body):
    if conds:
        both = conds[0]
        for c in conds[1:]:
            both = both & c
        pl.when(both)(body)
    else:
        body()


PACE = {"A": 4, "B": 5, "Y": 5, "C": 1}


def plan_gather(size, orders):
    events = []
    for part, order in enumerate(orders):
        spans = []
        for axis in order:
            n = size[axis]
            spans.append(range(1 - n, n) if axis == "A" else range(n))
        for offs in itertools.product(*spans):
            when = 0
            for axis, o in zip(order, offs):
                when += PACE[axis] * (abs(o) if axis == "A" else (1 if o else 0))
            events.append((when, part, offs))
    events.sort(key=lambda ev: ev[0])
    return events


def gather_body(place, orders, slices, own_ref, out_ref, block_of, send_sem, recv_sem):
    size = place.size
    sends = []
    count = [0]

    def send(conds, part, src_block, src, to):
        slot = count[0]
        count[0] += 1
        lo, n = slices[part]

        def copy():
            j = src_block()
            return pltpu.make_async_remote_copy(
                src_ref=(own_ref if src is None else out_ref.at[j]).at[:, pl.ds(lo, n)],
                dst_ref=out_ref.at[j].at[:, pl.ds(lo, n)],
                send_sem=send_sem.at[slot],
                recv_sem=recv_sem.at[part, j],
                device_id=place.device(to()),
                device_id_type=MESH,
            )

        under(conds, lambda: copy().start())
        sends.append((conds, copy))

    for _, part, offs in plan_gather(size, orders):
        order = orders[part]
        steps = dict(zip(order, offs))
        last = max([i for i, o in enumerate(offs) if o], default=-1)
        conds = []
        if steps["A"]:
            conds.append(place.inside(steps["A"]))

        def block(steps=steps):
            return block_of(place.moved(**{k: o for k, o in steps.items() if o}))

        if last >= 0:
            lo, n = slices[part]

            def wait(block=block, part=part, lo=lo, n=n):
                j = block()
                pltpu.make_async_copy(
                    out_ref.at[j].at[:, pl.ds(lo, n)], out_ref.at[j].at[:, pl.ds(lo, n)], recv_sem.at[part, j]
                ).wait()

            under(conds, wait)
        src = None if last < 0 else out_ref
        for i in range(max(last, 0), len(order)):
            axis = order[i]
            if axis == "A":
                ways = (1, -1) if i > last else ((1,) if steps["A"] < 0 else (-1,))
                for way in ways:
                    send(conds + [place.inside(way)], part, block, src, lambda way=way: place.moved(A=way))
            elif i > last:
                for t in range(1, size[axis]):
                    send(conds, part, block, src, lambda axis=axis, t=t: place.moved(**{axis: t}))
    for conds, copy in sends:
        under(conds, lambda copy=copy: copy().wait_send())


def count_gather(size, orders):
    total = 0
    for _, part, offs in plan_gather(size, orders):
        order = orders[part]
        last = max([i for i, o in enumerate(offs) if o], default=-1)
        for i in range(max(last, 0), len(order)):
            if order[i] == "A":
                total += 2 if i > last else 1
            elif i > last:
                total += size[order[i]] - 1
    return total


def sizes(n_dp, n_exp):
    rest = n_exp // 2
    na = 4 if rest % 4 == 0 else rest
    return {"A": na, "B": rest // na, "C": 2, "Y": n_dp}


def gather_kernel(n_dp, n_exp, orders, slices, dense, x_ref, out_ref, send_sem, recv_sem, local_sem):
    place = Place(n_dp, n_exp)
    block_of = place.flat if dense else place.expert
    place.greet(orders[0], False)
    own = pltpu.make_async_copy(x_ref, out_ref.at[block_of(place.pos)], local_sem)
    own.start()
    gather_body(place, orders, slices, x_ref, out_ref, block_of, send_sem, recv_sem)
    own.wait()


def gather(x, n_dp, n_exp, dense, cid, parts=None):
    size = sizes(n_dp, n_exp)
    rows, cols = x.shape
    if dense:
        orders = ("ABYC", "AYBC")
        half = cols // 256 * 128
        slices = ((0, half), (half, cols - half))
    else:
        orders = parts or ("ABC",)
        w = cols // len(orders)
        slices = tuple((i * w, w) for i in range(len(orders)))
    blocks = n_exp * (n_dp if dense else 1)
    return pl.pallas_call(
        functools.partial(gather_kernel, n_dp, n_exp, orders, slices, dense),
        out_shape=jax.ShapeDtypeStruct((blocks, rows, cols), x.dtype),
        in_specs=[pl.BlockSpec(memory_space=pl.ANY)],
        out_specs=pl.BlockSpec(memory_space=pl.ANY),
        scratch_shapes=[
            pltpu.SemaphoreType.DMA((count_gather(size, orders),)),
            pltpu.SemaphoreType.DMA((len(orders), blocks)),
            pltpu.SemaphoreType.DMA(()),
        ],
        compiler_params=pltpu.CompilerParams(collective_id=cid, has_side_effects=True),
        name="gather_dense" if dense else "gather_group",
    )(x)


def line_order(n):
    out = []
    for i in range((n + 1) // 2):
        out.append(i)
        if n - 1 - i != i:
            out.append(n - 1 - i)
    return out


def stage_slots(size, order):
    slots = {}
    for i, axis in enumerate(order):
        rest = [line_order(size[x]) if x == "A" else range(size[x]) for x in order[i + 1:]]
        if axis == "A":
            for who in range(size["A"]):
                slots[(i, who, ())] = len(slots)
        else:
            for who in range(1, size[axis]):
                for r in itertools.product(*rest):
                    slots[(i, who, r)] = len(slots)
    return slots


def reduce_body(place, orders, slices, g_ref, block_of, land, base, send_sem, recv_sem, finish):
    size = place.size
    tables = [stage_slots(size, order) for order in orders]
    sends = []
    n = [0]

    def target(order, i, o, rest):
        pos = dict(place.pos)
        for axis, v in zip(order[i:], (o,) + tuple(rest)):
            if axis == "A":
                pos["A"] = v
            else:
                pos[axis] = lax.rem(pos[axis] + v, size[axis])
        return pos

    def send(conds, part, src, slot, to):
        at = n[0]
        n[0] += 1

        def copy():
            return pltpu.make_async_remote_copy(
                src_ref=src(), dst_ref=land[part].at[slot], send_sem=send_sem.at[at],
                recv_sem=recv_sem.at[base[part] + slot], device_id=place.device(to()), device_id_type=MESH)

        under(conds, lambda: copy().start())
        sends.append((conds, copy))

    def wait(part, slot):
        ref = land[part].at[slot]
        pltpu.make_async_copy(ref, ref, recv_sem.at[base[part] + slot]).wait()

    def rests(order, i):
        return list(itertools.product(*[line_order(size[x]) if x == "A" else range(size[x]) for x in order[i:]]))

    def far_first(items):
        return sorted(items, key=lambda r: tuple(0 if (isinstance(v, int) and v) else 1 for v in r[:-1]))

    for part, order in enumerate(orders):
        lo, w = slices[part]
        axis = order[0]
        for t in range(1, size[axis]):
            for r in far_first(rests(order, 1)):
                def src(order=order, t=t, r=r, lo=lo, w=w):
                    return g_ref.at[block_of(target(order, 0, t, r)), :, pl.ds(lo, w)]
                send([], part, src, tables[part][(0, t, r)], lambda axis=axis, t=t: place.moved(**{axis: t}))
    for i in range(1, len(orders[0])):
        for pick in far_first(rests(orders[0], i)):
            for part, order in enumerate(orders):
                lo, w = slices[part]
                axis = order[i]
                before = order[i - 1]
                r = pick
                got = [tables[part][(i - 1, t, r)] for t in range(1, size[before])]
                for slot in got:
                    wait(part, slot)
                if i == 1:
                    total = g_ref[block_of(target(order, 1, r[0], r[1:])), :, lo:lo + w].astype(jnp.float32)
                else:
                    total = land[part][tables[part][(i - 2, 1, (0,) + r)]].astype(jnp.float32)
                for slot in got:
                    total = total + land[part][slot].astype(jnp.float32)
                land[part][got[0]] = total.astype(land[part].dtype)
                o, later = r[0], r[1:]
                def src(part=part, slot=got[0]):
                    return land[part].at[slot]
                if axis == "A":
                    a = place.pos["A"]
                    at = n[0]
                    n[0] += 1
                    def copy(part=part, slot=got[0], o=o, at=at, i=i):
                        first = tables[part][(i, 0, ())]
                        return pltpu.make_async_remote_copy(
                            src_ref=land[part].at[slot], dst_ref=land[part].at[first + a], send_sem=send_sem.at[at],
                            recv_sem=recv_sem.at[base[part] + first + a],
                            device_id=place.device(dict(place.pos, A=o)), device_id_type=MESH)
                    away = [a != o]
                    under(away, lambda copy=copy: copy().start())
                    sends.append((away, copy))
                elif o:
                    send([], part, src, tables[part][(i, o, later)], lambda axis=axis, o=o: place.moved(**{axis: o}))
    last = len(orders[0]) - 1
    for part, order in enumerate(orders):
        own = tables[part][(last - 1, 1, (0,))]
        a = place.pos["A"]
        first = tables[part][(last, 0, ())]
        step = tables[part][(last - 1, 1, (line_order(size["A"])[1],))] - own if size["A"] > 1 else 0
        mine = own
        for k, p in enumerate(line_order(size["A"])):
            mine = jnp.where(a == p, tables[part][(last - 1, 1, (p,))], mine)
        total = land[part][mine].astype(jnp.float32)
        for d in range(1, size["A"]):
            j = lax.rem(a + d, size["A"])
            wait(part, first + j)
            total = total + land[part][first + j].astype(jnp.float32)
        finish(part, total)
    for conds, copy in sends:
        under(conds, lambda copy=copy: copy().wait_send())


def count_reduce(size, orders):
    total = 0
    for order in orders:
        for i, axis in enumerate(order):
            rest = 1
            for x in order[i + 1:]:
                rest *= size[x]
            total += size["A"] if axis == "A" else (size[axis] - 1) * rest
    return total


def reduce_kernel(n_dp, n_exp, orders, slices, dense, g_ref, out_ref, *scratch):
    land, (send_sem, recv_sem) = scratch[:-2], scratch[-2:]
    place = Place(n_dp, n_exp)
    place.greet(orders[0], True)
    base = [0]
    for order in orders:
        base.append(base[-1] + len(stage_slots(place.size, order)))

    def finish(part, total):
        lo, w = slices[part]
        out_ref[:, lo:lo + w] = total.astype(out_ref.dtype)

    reduce_body(place, orders, slices, g_ref, place.flat if dense else place.expert, land, base, send_sem, recv_sem, finish)


def reduce_scatter(g, n_dp, n_exp, dense, cid, orders=None):
    size = sizes(n_dp, n_exp)
    blocks, rows, cols = g.shape
    orders = orders or (("CBYA", "CYBA") if dense else ("CBA",))
    w = cols // 128 // len(orders) * 128
    slices = tuple((i * w, w if i < len(orders) - 1 else cols - i * w) for i in range(len(orders)))
    slots = [len(stage_slots(size, order)) for order in orders]
    if (blocks + max(slots)) * ((rows + 15) // 16 * 16) * cols * 2 > 44 * 1024 * 1024:
        axes = ("dp", "expert") if dense else "expert"
        return lax.psum_scatter(g, axes, scatter_dimension=0, tiled=False).astype(jnp.float32)
    return pl.pallas_call(
        functools.partial(reduce_kernel, n_dp, n_exp, orders, slices, dense),
        out_shape=jax.ShapeDtypeStruct((rows, cols), jnp.float32),
        in_specs=[pl.BlockSpec(memory_space=pltpu.VMEM)],
        out_specs=pl.BlockSpec(memory_space=pltpu.VMEM),
        scratch_shapes=[pltpu.VMEM((k, rows, s[1]), g.dtype) for k, s in zip(slots, slices)] + [
            pltpu.SemaphoreType.DMA((count_reduce(size, orders),)),
            pltpu.SemaphoreType.DMA((sum(slots),)),
        ],
        compiler_params=pltpu.CompilerParams(collective_id=cid, has_side_effects=True, vmem_limit_bytes=60 * 1024 * 1024),
        name="reduce_dense" if dense else "reduce_group",
    )(g)


def spread_kernel(n_dp, n_exp, x_ref, out_ref, send_sem, recv_sem):
    n = n_dp * n_exp
    me = lax.axis_index("dp") * n_exp + lax.axis_index("expert")
    barrier = pltpu.get_barrier_semaphore()

    def device(step):
        to = lax.rem(me + step, n)
        return (to // n_exp, lax.rem(to, n_exp))

    def greet(step, carry):
        pl.semaphore_signal(barrier, inc=1, device_id=device(step), device_id_type=MESH)
        return carry

    lax.fori_loop(1, n, greet, 0)
    pl.semaphore_wait(barrier, n - 1)

    def copy(step):
        return pltpu.make_async_remote_copy(
            src_ref=x_ref, dst_ref=out_ref.at[step], send_sem=send_sem.at[step], recv_sem=recv_sem.at[step],
            device_id=device(step), device_id_type=MESH)

    def start(step, carry):
        copy(step).start()
        return carry

    def wait(step, carry):
        copy(step).wait()
        return carry

    lax.fori_loop(1, n, start, 0)
    out_ref[0] = x_ref[...]
    lax.fori_loop(1, n, wait, 0)


def sum_everywhere(value, n_dp, n_exp, cid):
    n = n_dp * n_exp
    parts = pl.pallas_call(
        functools.partial(spread_kernel, n_dp, n_exp),
        out_shape=jax.ShapeDtypeStruct((n, 8, 128), jnp.float32),
        in_specs=[pl.BlockSpec(memory_space=pltpu.VMEM)],
        out_specs=pl.BlockSpec(memory_space=pltpu.VMEM),
        scratch_shapes=[pltpu.SemaphoreType.DMA((n,)), pltpu.SemaphoreType.DMA((n,))],
        compiler_params=pltpu.CompilerParams(collective_id=cid, has_side_effects=True),
        name="sum_everywhere",
    )(jnp.full((8, 128), value, jnp.float32))
    return jnp.sum(parts[:, 0, 0])


def swap_rows(x, n_dp):
    if n_dp != 2:
        return lax.all_gather(x, "dp", axis=0, tiled=True)
    other = lax.ppermute(x, "dp", [(0, 1), (1, 0)])
    first = lax.axis_index("dp") == 0
    return jnp.concatenate([jnp.where(first, x, other), jnp.where(first, other, x)], axis=0)


def halve_rows(x, n_dp):
    if n_dp != 2:
        return lax.psum_scatter(x, "dp", scatter_dimension=0, tiled=True).astype(jnp.float32)
    rows = x.shape[0] // 2
    first = lax.axis_index("dp") == 0
    top, bottom = x[:rows], x[rows:]
    other = lax.ppermute(jnp.where(first, bottom, top), "dp", [(0, 1), (1, 0)])
    return jnp.where(first, top, bottom).astype(jnp.float32) + other.astype(jnp.float32)


def local(
    tokens,
    lengths,
    routes,
    cotangent,
    norm_gains,
    gains_m,
    gains_v,
    w_qkv,
    m_qkv,
    v_qkv,
    w_out,
    m_out,
    v_out,
    w_shared_in,
    m_shared_in,
    v_shared_in,
    w_shared_down,
    m_shared_down,
    v_shared_down,
    w_router,
    m_router,
    v_router,
    w_expert_in,
    m_expert_in,
    v_expert_in,
    w_expert_down,
    m_expert_down,
    v_expert_down,
):
    both = ("dp", "expert")
    low = jnp.bfloat16
    wide = jnp.float32
    row_count = tokens.shape[0]
    expert_count = w_router.shape[1]
    n_dp = lax.axis_size("dp")
    n_exp = lax.axis_size("expert")
    n_all = n_dp * n_exp
    capacity = min(row_count, (5 * row_count * TOP // (4 * expert_count) + 7) // 8 * 8)
    score_scale = HD ** (-0.5)
    rows_w = w_qkv.shape[0]
    unit = w_shared_down.shape[0]
    my_expert = lax.axis_index("expert")

    pad = jnp.zeros((rows_w, 128 - expert_count - 2), wide)
    packed = jnp.concatenate([w_qkv, w_out, w_router, norm_gains.T, pad], axis=1).astype(low)
    full = gather(packed, n_dp, n_exp, True, 1).reshape(D, -1)
    qkv_full = full[:, : 3 * H * HD]
    out_full = full[:, 3 * H * HD : 3 * H * HD + D]
    small_full = full[:, 3 * H * HD + D :]
    router_full = small_full[:, :expert_count]
    gain_one = small_full[:, expert_count].astype(wide)
    gain_two = small_full[:, expert_count + 1].astype(wide)
    cot_all = lax.all_gather(cotangent, "expert", axis=0, tiled=False)
    routes_all = lax.all_gather(routes, "expert", axis=0, tiled=False)
    expert_in_full = swap_rows(w_expert_in[0].astype(low), n_dp)
    expert_down_full = swap_rows(w_expert_down[0].astype(low), n_dp)
    shin_send = (
        w_shared_in.astype(low)
        .reshape(rows_w, 2, n_dp, n_exp, unit)
        .transpose(3, 0, 1, 2, 4)
        .reshape(n_exp, rows_w, 2 * n_dp * unit)
    )
    shin_send = jnp.concatenate([shin_send] * n_dp, axis=0)
    shin_mine = lax.all_to_all(shin_send, both, 0, 0, tiled=True).reshape(D, 2 * n_dp * unit)
    shdown_mine = lax.all_gather(w_shared_down.astype(low), "dp", axis=0, tiled=True)
    half = n_dp * unit

    inputs = tokens.astype(wide)
    cosine, sine_table, allowed = rotary_tables(lengths[0], row_count, HD)
    scale_one = rms_scale(inputs)
    normed_one = inputs * scale_one
    attn_in = (normed_one * gain_one).astype(low)
    projected = jnp.dot(attn_in, qkv_full, preferred_element_type=wide).reshape(
        row_count, 3, H, HD
    )
    queries = rotate(projected[:, 0], cosine, sine_table).astype(low)
    keys_rot = rotate(projected[:, 1], cosine, sine_table).astype(low)
    values_low = projected[:, 2].astype(low)
    raw_scores = (
        jnp.einsum("qhd,khd->hqk", queries, keys_rot, preferred_element_type=wide) * score_scale
    )
    scores = jnp.where(allowed[None], raw_scores, NEGATIVE)
    row_max = jnp.max(scores, axis=-1, keepdims=True)
    exped = jnp.exp(scores - row_max)
    probs_attn = exped / jnp.sum(exped, axis=-1, keepdims=True)
    probs_low = probs_attn.astype(low)
    mixed_heads = jnp.einsum("hqk,khd->qhd", probs_low, values_low, preferred_element_type=wide)
    heads_low = mixed_heads.astype(low).reshape(row_count, H * HD)
    residual = inputs + jnp.dot(heads_low, out_full, preferred_element_type=wide)
    scale_two = rms_scale(residual)
    normed_two = residual * scale_two
    mlp_in = (normed_two * gain_two).astype(low)
    logits = jnp.dot(mlp_in, router_full, preferred_element_type=wide)
    router_probs = jax.nn.softmax(logits, axis=-1)

    mlp_all = gather(mlp_in, n_dp, n_exp, False, 2, ("ABC", "ABC", "ABC", "ABC", "BAC"))
    mlp_flat = mlp_all.reshape(n_exp * row_count, D)
    fused_w = jnp.concatenate([shin_mine, router_full], axis=1)
    fused = jnp.dot(mlp_flat, fused_w, preferred_element_type=wide)
    shared_gate = fused[:, :half]
    shared_up = fused[:, half : 2 * half]
    probs_all = jax.nn.softmax(fused[:, 2 * half :], axis=-1)
    expert_ids = jnp.arange(expert_count, dtype=jnp.int32)
    my_prob = jnp.sum(jnp.where(expert_ids[None, :] == my_expert, probs_all, 0.0), axis=1)
    my_prob = my_prob.reshape(n_exp, row_count)
    routed_here = jnp.any(routes_all == my_expert, axis=2)
    rank = jnp.cumsum(routed_here.astype(jnp.int32), axis=1) - 1
    slot = jnp.arange(capacity, dtype=jnp.int32)
    pick_mask = routed_here[:, None, :] & (rank[:, None, :] == slot[None, :, None])
    pick = pick_mask.astype(low)
    picked_in = jnp.einsum("nst,ntd->nsd", pick, mlp_all, preferred_element_type=wide).astype(low)
    picked_cot = jnp.einsum("nst,ntd->nsd", pick, cot_all, preferred_element_type=wide).astype(low)
    picked_gate = jnp.sum(jnp.where(pick_mask, my_prob[:, None, :], 0.0), axis=2).reshape(-1, 1)
    flat_in = picked_in.reshape(-1, D)
    flat_cot = picked_cot.reshape(-1, D).astype(wide)
    gate_up = jnp.dot(flat_in, expert_in_full, preferred_element_type=wide)
    activation = (jax.nn.silu(gate_up[:, :FF]) * gate_up[:, FF:]).astype(low)
    result = jnp.dot(activation, expert_down_full, preferred_element_type=wide).astype(low)
    result = result.astype(wide)
    gate_grad = jnp.sum(flat_cot * result, axis=1).reshape(n_exp, capacity, 1)
    weighted = (picked_gate * result).astype(low).reshape(n_exp, capacity, D)
    shared_act = (jax.nn.silu(shared_gate) * shared_up).astype(low)
    mixed_part = jnp.einsum("nst,nsd->ntd", pick, weighted, preferred_element_type=wide)
    mixed_part = mixed_part.reshape(-1, D) + jnp.dot(
        shared_act, shdown_mine, preferred_element_type=wide
    )
    mixed_sum = reduce_scatter(
        mixed_part.astype(low).reshape(n_exp, row_count, D), n_dp, n_exp, False, 3, ("CBA", "CBA")
    )
    mixed = (residual + mixed_sum.astype(wide)).astype(low)

    cot_flat = cot_all.reshape(n_exp * row_count, D)
    grad_shdown = jnp.einsum("tf,td->fd", shared_act, cot_flat, preferred_element_type=wide)
    shared_act_grad = jnp.einsum("td,fd->tf", cot_flat, shdown_mine, preferred_element_type=wide)
    shared_gu_grad = jnp.concatenate(
        [
            shared_act_grad * shared_up * silu_slope(shared_gate),
            shared_act_grad * jax.nn.silu(shared_gate),
        ],
        axis=1,
    ).astype(low)
    grad_shin = jnp.einsum("td,tf->df", mlp_flat, shared_gu_grad, preferred_element_type=wide)
    grad_rows = (picked_gate * flat_cot).astype(low)
    grad_edown = jnp.einsum("rf,rd->fd", activation, grad_rows, preferred_element_type=wide)
    expert_act_grad = jnp.einsum(
        "rd,fd->rf", grad_rows, expert_down_full, preferred_element_type=wide
    )
    expert_gu_grad = swiglu_back(expert_act_grad, gate_up)
    grad_ein = jnp.einsum("rd,rf->df", flat_in, expert_gu_grad, preferred_element_type=wide)
    input_back = jnp.einsum(
        "rf,df->rd", expert_gu_grad, expert_in_full, preferred_element_type=wide
    )
    input_back = input_back.astype(low).reshape(n_exp, capacity, D)
    back_part = jnp.einsum("nst,nsd->ntd", pick, input_back, preferred_element_type=wide)
    back_part = back_part.reshape(-1, D) + jnp.einsum(
        "tf,df->td", shared_gu_grad, shin_mine, preferred_element_type=wide
    )
    back_sum = reduce_scatter(
        back_part.astype(low).reshape(n_exp, row_count, D), n_dp, n_exp, False, 4, ("CBA", "CBA")
    )
    gate_grad_tok = jnp.sum(jnp.where(pick_mask, gate_grad, 0.0), axis=1)
    prob_grad = lax.all_to_all(gate_grad_tok, "expert", 0, 0, tiled=True).T
    logit_grad = (
        router_probs * (prob_grad - jnp.sum(prob_grad * router_probs, axis=-1, keepdims=True))
    ).astype(low)
    grad_router = jnp.einsum("td,te->de", mlp_in, logit_grad, preferred_element_type=wide)
    mlp_in_grad = back_sum.astype(wide) + jnp.einsum(
        "te,de->td", logit_grad, router_full, preferred_element_type=wide
    )
    out_grad = cotangent.astype(wide)
    grad_gain_two = jnp.sum(mlp_in_grad * normed_two, axis=0)
    scaled_two = mlp_in_grad * gain_two
    resid_grad = out_grad + scale_two * (
        scaled_two - normed_two * jnp.mean(scaled_two * normed_two, axis=-1, keepdims=True)
    )
    resid_low = resid_grad.astype(low)
    grad_out = jnp.einsum("ti,td->id", heads_low, resid_low, preferred_element_type=wide)
    heads_grad = jnp.einsum("td,id->ti", resid_low, out_full, preferred_element_type=wide)
    heads_grad = heads_grad.astype(low).reshape(row_count, H, HD)
    attn_prob_grad = jnp.einsum("qhd,khd->hqk", heads_grad, values_low, preferred_element_type=wide)
    value_grad = jnp.einsum("hqk,qhd->khd", probs_low, heads_grad, preferred_element_type=wide)
    score_grad = probs_attn * (
        attn_prob_grad - jnp.sum(attn_prob_grad * probs_attn, axis=-1, keepdims=True)
    )
    score_grad = score_grad.astype(low)
    query_grad = (
        jnp.einsum("hqk,khd->qhd", score_grad, keys_rot, preferred_element_type=wide) * score_scale
    )
    key_grad = (
        jnp.einsum("hqk,qhd->khd", score_grad, queries, preferred_element_type=wide) * score_scale
    )
    projected_grad = jnp.stack(
        [
            rotate_back(query_grad, cosine, sine_table),
            rotate_back(key_grad, cosine, sine_table),
            value_grad,
        ],
        axis=1,
    )
    projected_grad = projected_grad.reshape(row_count, 3 * H * HD).astype(low)
    grad_qkv = jnp.einsum("td,tk->dk", attn_in, projected_grad, preferred_element_type=wide)
    attn_grad = jnp.einsum("tk,dk->td", projected_grad, qkv_full, preferred_element_type=wide)
    grad_gain_one = jnp.sum(attn_grad * normed_one, axis=0)
    scaled_one = attn_grad * gain_one
    input_grad = resid_grad + scale_one * (
        scaled_one - normed_one * jnp.mean(scaled_one * normed_one, axis=-1, keepdims=True)
    )

    small_grad = jnp.concatenate(
        [grad_router, grad_gain_one[:, None], grad_gain_two[:, None], jnp.zeros((D, 128 - expert_count - 2), wide)],
        axis=1,
    )
    dense_grad = jnp.concatenate([grad_qkv.astype(low), grad_out.astype(low), small_grad.astype(low)], axis=1)
    dense_own = reduce_scatter(dense_grad.reshape(n_all, rows_w, -1), n_dp, n_exp, True, 5)
    small_own = dense_own[:, 3 * H * HD + D :]
    shin_back = lax.all_to_all(
        grad_shin.astype(low).reshape(n_all, rows_w, 2 * half), both, 0, 0, tiled=True
    )
    shin_own = jnp.sum(
        shin_back.reshape(n_dp, n_exp, rows_w, 2, n_dp, unit).astype(wide), axis=0
    )
    shin_own = shin_own.transpose(1, 2, 3, 0, 4).reshape(rows_w, 2 * FF)
    owned_grads = (
        small_own[:, expert_count : expert_count + 2].T,
        dense_own[:, : 3 * H * HD],
        dense_own[:, 3 * H * HD : 3 * H * HD + D],
        shin_own,
        lax.psum_scatter(grad_shdown, "dp", scatter_dimension=0, tiled=True),
        small_own[:, :expert_count],
        halve_rows(grad_ein.astype(low), n_dp)[None],
        halve_rows(grad_edown.astype(low), n_dp)[None],
    )
    squares = sum((jnp.sum(grad_part * grad_part) for grad_part in owned_grads))
    total_squares = sum_everywhere(squares, n_dp, n_exp, 6)
    grad_norm = jnp.sqrt(total_squares)
    factor = jnp.minimum(1.0, CLIP / grad_norm)
    weights = (
        norm_gains,
        w_qkv,
        w_out,
        w_shared_in,
        w_shared_down,
        w_router,
        w_expert_in,
        w_expert_down,
    )
    firsts = (
        gains_m,
        m_qkv,
        m_out,
        m_shared_in,
        m_shared_down,
        m_router,
        m_expert_in,
        m_expert_down,
    )
    seconds = (
        gains_v,
        v_qkv,
        v_out,
        v_shared_in,
        v_shared_down,
        v_router,
        v_expert_in,
        v_expert_down,
    )
    rates = (
        GAIN_RATE,
        D ** (-0.5),
        (H * HD // 64) ** (-0.5),
        D ** (-0.5),
        FF ** (-0.5),
        (4 * D) ** (-0.5),
        D ** (-0.5),
        (FF // 64) ** (-0.5),
    )
    decays = (0.0, DECAY, DECAY, DECAY, DECAY, DECAY, DECAY, DECAY)
    updated = []
    for weight, first_moment, second_moment, gradient, step_rate, decay_rate in zip(
        weights, firsts, seconds, owned_grads, rates, decays
    ):
        updated.extend(
            adam_update(
                weight, first_moment, second_moment, gradient, factor, step_rate, decay_rate
            )
        )
    return (
        mixed,
        input_grad,
        updated[0],
        updated[1],
        updated[2],
        updated[3],
        updated[4],
        updated[5],
        updated[6],
        updated[7],
        updated[8],
        updated[9],
        updated[10],
        updated[11],
        updated[12],
        updated[13],
        updated[14],
        updated[15],
        updated[16],
        updated[17],
        updated[18],
        updated[19],
        updated[20],
        updated[21],
        updated[22],
        updated[23],
        grad_norm,
    )


def solution(mesh):
    placed = (
        P(("dp", "expert"), None),
        P(("dp", "expert"), None),
        P(("dp", "expert"), None),
        P(("dp", "expert"), None),
        P(None, ("dp", "expert")),
        P(None, ("dp", "expert")),
        P(None, ("dp", "expert")),
        P(("dp", "expert"), None),
        P(("dp", "expert"), None),
        P(("dp", "expert"), None),
        P(("dp", "expert"), None),
        P(("dp", "expert"), None),
        P(("dp", "expert"), None),
        P(("dp", "expert"), None),
        P(("dp", "expert"), None),
        P(("dp", "expert"), None),
        P(("dp", "expert"), None),
        P(("dp", "expert"), None),
        P(("dp", "expert"), None),
        P(("dp", "expert"), None),
        P(("dp", "expert"), None),
        P(("dp", "expert"), None),
        P("expert", "dp", None),
        P("expert", "dp", None),
        P("expert", "dp", None),
        P("expert", "dp", None),
        P("expert", "dp", None),
        P("expert", "dp", None),
    )
    return jax.shard_map(
        local,
        mesh=mesh,
        in_specs=placed,
        out_specs=(
            P(("dp", "expert"), None),
            P(("dp", "expert"), None),
            P(None, ("dp", "expert")),
            P(None, ("dp", "expert")),
            P(None, ("dp", "expert")),
            P(("dp", "expert"), None),
            P(("dp", "expert"), None),
            P(("dp", "expert"), None),
            P(("dp", "expert"), None),
            P(("dp", "expert"), None),
            P(("dp", "expert"), None),
            P(("dp", "expert"), None),
            P(("dp", "expert"), None),
            P(("dp", "expert"), None),
            P(("dp", "expert"), None),
            P(("dp", "expert"), None),
            P(("dp", "expert"), None),
            P(("dp", "expert"), None),
            P(("dp", "expert"), None),
            P(("dp", "expert"), None),
            P("expert", "dp", None),
            P("expert", "dp", None),
            P("expert", "dp", None),
            P("expert", "dp", None),
            P("expert", "dp", None),
            P("expert", "dp", None),
            P(),
        ),
        check_vma=False,
    )
```

```python
import functools
import itertools

import jax
import jax.numpy as jnp
from jax import lax
from jax.experimental import pallas as pl
from jax.experimental.pallas import tpu as pltpu
from jax.sharding import PartitionSpec as P

D = 1280
H = 10
HD = 128
FF = 896
TOP = 6
ADAM_STEP = 5


EPS = 1e-06
ROPE_BASE = 10000.0
BETA_ONE = 0.9
BETA_TWO = 0.95
ADAM_EPS = 1e-08
DECAY = 0.1
CLIP = 1.0
GAIN_RATE = 0.5
NEGATIVE = -1e30


def rms_scale(values):
    return lax.rsqrt(jnp.mean(values * values, axis=-1, keepdims=True) + EPS)


def rotary_tables(seq_lengths, row_count, head_width):
    position = jnp.arange(row_count, dtype=jnp.int32)
    seq_ends = jnp.cumsum(seq_lengths)
    segment = jnp.sum((position[:, None] >= seq_ends[None, :]).astype(jnp.int32), axis=1)
    starts = seq_ends - seq_lengths
    slot_ids = jnp.arange(seq_lengths.shape[0], dtype=jnp.int32)
    first_row = jnp.sum(
        jnp.where(segment[:, None] == slot_ids[None, :], starts[None, :], 0), axis=1
    )
    seq_place = (position - first_row).astype(jnp.float32)
    inv_freq = ROPE_BASE ** (-jnp.arange(head_width // 2, dtype=jnp.float32) * 2.0 / head_width)
    phase_angle = seq_place[:, None] * inv_freq[None, :]
    cosine = jnp.concatenate([jnp.cos(phase_angle), jnp.cos(phase_angle)], axis=1)
    sine_table = jnp.concatenate([jnp.sin(phase_angle), jnp.sin(phase_angle)], axis=1)
    allowed = (segment[:, None] == segment[None, :]) & (position[None, :] <= position[:, None])
    return (cosine, sine_table, allowed)


def rotate(vectors, cosine, sine_table):
    half_width = vectors.shape[-1] // 2
    turned = jnp.concatenate([-vectors[..., half_width:], vectors[..., :half_width]], axis=-1)
    return vectors * cosine[:, None, :] + turned * sine_table[:, None, :]


def rotate_back(gradient, cosine, sine_table):
    half_width = gradient.shape[-1] // 2
    scaled_sine = gradient * sine_table[:, None, :]
    turned = jnp.concatenate(
        [scaled_sine[..., half_width:], -scaled_sine[..., :half_width]], axis=-1
    )
    return gradient * cosine[:, None, :] + turned


def silu_slope(gate_vals):
    logistic = jax.nn.sigmoid(gate_vals)
    return logistic * (1.0 + gate_vals * (1.0 - logistic))


def swiglu_back(act_grad, gate_up):
    gate_part = gate_up[:, :FF]
    up_part = gate_up[:, FF:]
    return jnp.concatenate(
        [act_grad * up_part * silu_slope(gate_part), act_grad * jax.nn.silu(gate_part)], axis=1
    ).astype(jnp.bfloat16)


def adam_update(weight, first_moment, second_moment, gradient, factor, step_rate, decay_rate):
    clipped = gradient * factor
    first_new = BETA_ONE * first_moment + (1.0 - BETA_ONE) * clipped
    second_new = BETA_TWO * second_moment + (1.0 - BETA_TWO) * clipped * clipped
    first_hat = first_new / (1.0 - BETA_ONE**ADAM_STEP)
    second_hat = second_new / (1.0 - BETA_TWO**ADAM_STEP)
    weight_new = weight - step_rate * (
        first_hat / (jnp.sqrt(second_hat) + ADAM_EPS) + decay_rate * weight
    )
    return (weight_new, first_new, second_new)


MESH = pl.DeviceIdType.MESH


class Place:
    def __init__(self, n_dp, n_exp):
        rest = n_exp // 2
        na = 4 if rest % 4 == 0 else rest
        self.size = {"A": na, "B": rest // na, "C": 2, "Y": n_dp}
        e = lax.axis_index("expert")
        nb = self.size["B"]
        self.pos = {"A": e // (2 * nb), "B": (e // 2) % nb, "C": e % 2, "Y": lax.axis_index("dp")}

    def expert(self, pos):
        return (pos["A"] * self.size["B"] + pos["B"]) * 2 + pos["C"]

    def flat(self, pos):
        return pos["Y"] * (2 * self.size["A"] * self.size["B"]) + self.expert(pos)

    def device(self, pos):
        return (pos["Y"], self.expert(pos))

    def moved(self, **steps):
        pos = dict(self.pos)
        for axis, step in steps.items():
            if axis == "A":
                pos[axis] = pos[axis] + step
            else:
                pos[axis] = lax.rem(pos[axis] + step, self.size[axis])
        return pos

    def inside(self, step):
        there = self.pos["A"] + step
        return (there >= 0) & (there < self.size["A"])

    def greet(self, axes, line_all):
        barrier = pltpu.get_barrier_semaphore()
        total = 0
        for axis in axes:
            if axis == "A":
                reach = range(1, self.size["A"]) if line_all else (1,)
                for step in [s * d for d in reach for s in (1, -1)]:
                    near = self.inside(step)

                    @pl.when(near)
                    def _(step=step):
                        pl.semaphore_signal(barrier, inc=1, device_id=self.device(self.moved(A=step)), device_id_type=MESH)

                    total = total + jnp.where(near, 1, 0)
            else:
                for step in range(1, self.size[axis]):
                    pl.semaphore_signal(barrier, inc=1, device_id=self.device(self.moved(**{axis: step})), device_id_type=MESH)
                    total = total + 1
        pl.semaphore_wait(barrier, total)


def under(conds, body):
    if conds:
        both = conds[0]
        for c in conds[1:]:
            both = both & c
        pl.when(both)(body)
    else:
        body()


PACE = {"A": 4, "B": 5, "Y": 5, "C": 1}


def plan_gather(size, orders):
    events = []
    for part, order in enumerate(orders):
        spans = []
        for axis in order:
            n = size[axis]
            spans.append(range(1 - n, n) if axis == "A" else range(n))
        for offs in itertools.product(*spans):
            when = 0
            for axis, o in zip(order, offs):
                when += PACE[axis] * (abs(o) if axis == "A" else (1 if o else 0))
            events.append((when, part, offs))
    events.sort(key=lambda ev: ev[0])
    return events


def gather_body(place, orders, slices, own_ref, out_ref, block_of, send_sem, recv_sem):
    size = place.size
    sends = []
    count = [0]

    def send(conds, part, src_block, src, to):
        slot = count[0]
        count[0] += 1
        lo, n = slices[part]

        def copy():
            j = src_block()
            return pltpu.make_async_remote_copy(
                src_ref=(own_ref if src is None else out_ref.at[j]).at[:, pl.ds(lo, n)],
                dst_ref=out_ref.at[j].at[:, pl.ds(lo, n)],
                send_sem=send_sem.at[slot],
                recv_sem=recv_sem.at[part, j],
                device_id=place.device(to()),
                device_id_type=MESH,
            )

        under(conds, lambda: copy().start())
        sends.append((conds, copy))

    for _, part, offs in plan_gather(size, orders):
        order = orders[part]
        steps = dict(zip(order, offs))
        last = max([i for i, o in enumerate(offs) if o], default=-1)
        conds = []
        if steps["A"]:
            conds.append(place.inside(steps["A"]))

        def block(steps=steps):
            return block_of(place.moved(**{k: o for k, o in steps.items() if o}))

        if last >= 0:
            lo, n = slices[part]

            def wait(block=block, part=part, lo=lo, n=n):
                j = block()
                pltpu.make_async_copy(
                    out_ref.at[j].at[:, pl.ds(lo, n)], out_ref.at[j].at[:, pl.ds(lo, n)], recv_sem.at[part, j]
                ).wait()

            under(conds, wait)
        src = None if last < 0 else out_ref
        for i in range(max(last, 0), len(order)):
            axis = order[i]
            if axis == "A":
                ways = (1, -1) if i > last else ((1,) if steps["A"] < 0 else (-1,))
                for way in ways:
                    send(conds + [place.inside(way)], part, block, src, lambda way=way: place.moved(A=way))
            elif i > last:
                for t in range(1, size[axis]):
                    send(conds, part, block, src, lambda axis=axis, t=t: place.moved(**{axis: t}))
    for conds, copy in sends:
        under(conds, lambda copy=copy: copy().wait_send())


def count_gather(size, orders):
    total = 0
    for _, part, offs in plan_gather(size, orders):
        order = orders[part]
        last = max([i for i, o in enumerate(offs) if o], default=-1)
        for i in range(max(last, 0), len(order)):
            if order[i] == "A":
                total += 2 if i > last else 1
            elif i > last:
                total += size[order[i]] - 1
    return total


def sizes(n_dp, n_exp):
    rest = n_exp // 2
    na = 4 if rest % 4 == 0 else rest
    return {"A": na, "B": rest // na, "C": 2, "Y": n_dp}


def gather_kernel(n_dp, n_exp, orders, slices, dense, x_ref, out_ref, send_sem, recv_sem, local_sem):
    place = Place(n_dp, n_exp)
    block_of = place.flat if dense else place.expert
    place.greet(orders[0], False)
    own = pltpu.make_async_copy(x_ref, out_ref.at[block_of(place.pos)], local_sem)
    own.start()
    gather_body(place, orders, slices, x_ref, out_ref, block_of, send_sem, recv_sem)
    own.wait()


def gather(x, n_dp, n_exp, dense, cid, parts=None):
    size = sizes(n_dp, n_exp)
    rows, cols = x.shape
    if dense:
        orders = ("ABYC", "AYBC")
        half = cols // 256 * 128
        slices = ((0, half), (half, cols - half))
    else:
        orders = parts or ("ABC",)
        w = cols // len(orders)
        slices = tuple((i * w, w) for i in range(len(orders)))
    blocks = n_exp * (n_dp if dense else 1)
    return pl.pallas_call(
        functools.partial(gather_kernel, n_dp, n_exp, orders, slices, dense),
        out_shape=jax.ShapeDtypeStruct((blocks, rows, cols), x.dtype),
        in_specs=[pl.BlockSpec(memory_space=pl.ANY)],
        out_specs=pl.BlockSpec(memory_space=pl.ANY),
        scratch_shapes=[
            pltpu.SemaphoreType.DMA((count_gather(size, orders),)),
            pltpu.SemaphoreType.DMA((len(orders), blocks)),
            pltpu.SemaphoreType.DMA(()),
        ],
        compiler_params=pltpu.CompilerParams(collective_id=cid, has_side_effects=True),
        name="gather_dense" if dense else "gather_group",
    )(x)


def line_order(n):
    out = []
    for i in range((n + 1) // 2):
        out.append(i)
        if n - 1 - i != i:
            out.append(n - 1 - i)
    return out


def stage_slots(size, order):
    slots = {}
    for i, axis in enumerate(order):
        rest = [line_order(size[x]) if x == "A" else range(size[x]) for x in order[i + 1:]]
        if axis == "A":
            for who in range(size["A"]):
                slots[(i, who, ())] = len(slots)
        else:
            for who in range(1, size[axis]):
                for r in itertools.product(*rest):
                    slots[(i, who, r)] = len(slots)
    return slots


def reduce_body(place, orders, slices, g_refs, block_of, land, base, send_sem, recv_sem, finish):
    size = place.size
    tables = [stage_slots(size, order) for order in orders]
    sends = []
    n = [0]

    def target(order, i, o, rest):
        pos = dict(place.pos)
        for axis, v in zip(order[i:], (o,) + tuple(rest)):
            if axis == "A":
                pos["A"] = v
            else:
                pos[axis] = lax.rem(pos[axis] + v, size[axis])
        return pos

    def send(conds, part, src, slot, to):
        at = n[0]
        n[0] += 1

        def copy():
            return pltpu.make_async_remote_copy(
                src_ref=src(), dst_ref=land[part].at[slot], send_sem=send_sem.at[at],
                recv_sem=recv_sem.at[base[part] + slot], device_id=place.device(to()), device_id_type=MESH)

        under(conds, lambda: copy().start())
        sends.append((conds, copy))

    def wait(part, slot):
        ref = land[part].at[slot]
        pltpu.make_async_copy(ref, ref, recv_sem.at[base[part] + slot]).wait()

    def rests(order, i):
        return list(itertools.product(*[line_order(size[x]) if x == "A" else range(size[x]) for x in order[i:]]))

    def far_first(items):
        return sorted(items, key=lambda r: tuple(0 if (isinstance(v, int) and v) else 1 for v in r[:-1]))

    for part, order in enumerate(orders):
        g_ref, lo, w = g_refs[slices[part][0]], slices[part][1], slices[part][2]
        axis = order[0]
        for t in range(1, size[axis]):
            for r in far_first(rests(order, 1)):
                def src(order=order, t=t, r=r, lo=lo, w=w, g_ref=g_ref):
                    return g_ref.at[block_of(target(order, 0, t, r)), :, pl.ds(lo, w)]
                send([], part, src, tables[part][(0, t, r)], lambda axis=axis, t=t: place.moved(**{axis: t}))
    for i in range(1, len(orders[0])):
        for pick in far_first(rests(orders[0], i)):
            for part, order in enumerate(orders):
                g_ref, lo, w = g_refs[slices[part][0]], slices[part][1], slices[part][2]
                axis = order[i]
                before = order[i - 1]
                r = pick
                got = [tables[part][(i - 1, t, r)] for t in range(1, size[before])]
                for slot in got:
                    wait(part, slot)
                if i == 1:
                    total = g_ref[block_of(target(order, 1, r[0], r[1:])), :, lo:lo + w].astype(jnp.float32)
                else:
                    total = land[part][tables[part][(i - 2, 1, (0,) + r)]].astype(jnp.float32)
                for slot in got:
                    total = total + land[part][slot].astype(jnp.float32)
                land[part][got[0]] = total.astype(land[part].dtype)
                o, later = r[0], r[1:]
                def src(part=part, slot=got[0]):
                    return land[part].at[slot]
                if axis == "A":
                    a = place.pos["A"]
                    at = n[0]
                    n[0] += 1
                    def copy(part=part, slot=got[0], o=o, at=at, i=i):
                        first = tables[part][(i, 0, ())]
                        return pltpu.make_async_remote_copy(
                            src_ref=land[part].at[slot], dst_ref=land[part].at[first + a], send_sem=send_sem.at[at],
                            recv_sem=recv_sem.at[base[part] + first + a],
                            device_id=place.device(dict(place.pos, A=o)), device_id_type=MESH)
                    away = [a != o]
                    under(away, lambda copy=copy: copy().start())
                    sends.append((away, copy))
                elif o:
                    send([], part, src, tables[part][(i, o, later)], lambda axis=axis, o=o: place.moved(**{axis: o}))
    last = len(orders[0]) - 1
    for part, order in enumerate(orders):
        own = tables[part][(last - 1, 1, (0,))]
        a = place.pos["A"]
        first = tables[part][(last, 0, ())]
        step = tables[part][(last - 1, 1, (line_order(size["A"])[1],))] - own if size["A"] > 1 else 0
        mine = own
        for k, p in enumerate(line_order(size["A"])):
            mine = jnp.where(a == p, tables[part][(last - 1, 1, (p,))], mine)
        total = land[part][mine].astype(jnp.float32)
        for d in range(1, size["A"]):
            j = lax.rem(a + d, size["A"])
            wait(part, first + j)
            total = total + land[part][first + j].astype(jnp.float32)
        finish(part, total)
    for conds, copy in sends:
        under(conds, lambda copy=copy: copy().wait_send())


def count_reduce(size, orders):
    total = 0
    for order in orders:
        for i, axis in enumerate(order):
            rest = 1
            for x in order[i + 1:]:
                rest *= size[x]
            total += size["A"] if axis == "A" else (size[axis] - 1) * rest
    return total


def reduce_kernel(n_dp, n_exp, orders, slices, dense, arrays, *refs):
    g_refs, out_refs, scratch = refs[:arrays], refs[arrays:2 * arrays], refs[2 * arrays:]
    land, (send_sem, recv_sem) = scratch[:-2], scratch[-2:]
    place = Place(n_dp, n_exp)
    place.greet(orders[0], True)
    base = [0]
    for order in orders:
        base.append(base[-1] + len(stage_slots(place.size, order)))

    def finish(part, total):
        which, lo, w = slices[part]
        out_refs[which][:, lo:lo + w] = total

    reduce_body(place, orders, slices, g_refs, place.flat if dense else place.expert, land, base, send_sem, recv_sem, finish)


def reduce_dense(arrays, n_dp, n_exp, cid):
    size = sizes(n_dp, n_exp)
    blocks, rows = arrays[0].shape[:2]
    orders, slices = [], []
    for which, g in enumerate(arrays):
        cols = g.shape[2]
        half = cols // 256 * 128
        for order, lo, w in (("CBYA", 0, half), ("CYBA", half, cols - half)):
            if w:
                orders.append(order)
                slices.append((which, lo, w))
    slots = [len(stage_slots(size, order)) for order in orders]
    return pl.pallas_call(
        functools.partial(reduce_kernel, n_dp, n_exp, orders, slices, True, len(arrays)),
        out_shape=[jax.ShapeDtypeStruct((rows, g.shape[2]), jnp.float32) for g in arrays],
        in_specs=[pl.BlockSpec(memory_space=pltpu.VMEM)] * len(arrays),
        out_specs=[pl.BlockSpec(memory_space=pltpu.VMEM)] * len(arrays),
        scratch_shapes=[pltpu.VMEM((k, rows, s[2]), g.dtype) for k, s in zip(slots, slices)] + [
            pltpu.SemaphoreType.DMA((count_reduce(size, orders),)),
            pltpu.SemaphoreType.DMA((sum(slots),)),
        ],
        compiler_params=pltpu.CompilerParams(collective_id=cid, has_side_effects=True, vmem_limit_bytes=60 * 1024 * 1024),
        name="reduce_dense",
    )(*arrays)


def mm(a, b):
    return jnp.dot(a, b, preferred_element_type=jnp.float32)


def mm_nt(a, b):
    return lax.dot_general(a, b, (((1,), (1,)), ((), ())), preferred_element_type=jnp.float32)


def mm_tn(a, b):
    return lax.dot_general(a, b, (((0,), (0,)), ((), ())), preferred_element_type=jnp.float32)


def sig(v):
    return 1.0 / (1.0 + jnp.exp(-v))


def near_first(na):
    table = []
    for a in range(na):
        row = [a]
        for d in range(1, na):
            row += [p for p in ((a - d, a + d) if a < na // 2 else (a + d, a - d)) if 0 <= p < na]
        table.append(row)
    return table


def pair_order(na, nb):
    order = [(0, 0), (1, 0)] + [(1, t) for t in range(1, nb)]
    for i in range(2, na):
        order += [(i, t) for t in range(1, nb)] + [(i, 0)]
    return order + [(0, t) for t in range(1, nb)]


def choose(index, values):
    out = values[-1]
    for i in range(len(values) - 1):
        out = jnp.where(index == i, values[i], out)
    return out


def fused_kernel(n_dp, n_exp, experts, cap, x_ref, cot_ref, rank_ref, win_h, wdown_h, wshin_h, wshdown_h,
                 xall, mixed, total_out, gg_out, gin_out, gdown_out, gshin, gshdown, core_land, b_land, a_land,
                 win, wdown, wshin, wshdown, xv, cv, xr_s, act_s, gr_s, dgu_s, back_s, mixed_s, held, bsrc, stage,
                 gg_s, gin_acc, gdown_acc,
                 w_sem, x_sem, c_sem, m_sem, s_sem, ag_send, ag_recv, core_send, core_recv, b_send, b_recv,
                 a_send, a_recv, g_send, g_recv):
    low, wide = jnp.bfloat16, jnp.float32
    place = Place(n_dp, n_exp)
    na, nb = place.size["A"], place.size["B"]
    pos = place.pos
    a, c, me = pos["A"], pos["C"], place.expert(pos)
    toks, d = x_ref.shape
    hid = wshdown.shape[0]
    table = near_first(na)
    order = pair_order(na, nb)
    steps = len(order)
    near = [choose(a, [table[p][i] for p in range(na)]) for i in range(na)]
    sib = dict(pos, C=1 - c)

    def there(i, t, own_plane=True):
        return dict(pos, A=near[i], B=lax.rem(pos["B"] + t, nb), C=c if own_plane else 1 - c)

    barrier = pltpu.get_barrier_semaphore()
    for s in range(1, n_exp):
        pl.semaphore_signal(barrier, inc=1, device_id=(pos["Y"], lax.rem(me + s, n_exp)), device_id_type=MESH)
    pl.semaphore_wait(barrier, n_exp - 1)

    counter = [0]
    ag_sends = []

    def ag(conds, src, j, to):
        at = counter[0]
        counter[0] += 1

        def copy():
            return pltpu.make_async_remote_copy(
                src_ref=src(), dst_ref=xall.at[j()], send_sem=ag_send.at[at], recv_sem=ag_recv.at[j()],
                device_id=place.device(to()), device_id_type=MESH)

        ag_sends.append((conds, copy))
        under(conds(), lambda: copy().start())

    def landed(j):
        pltpu.make_async_copy(xall.at[j], xall.at[j], ag_recv.at[j]).wait()

    def own_block():
        return x_ref

    def always():
        return []

    for way in (1, -1):
        ag(lambda way=way: [place.inside(way)], own_block, lambda: me, lambda way=way: place.moved(A=way))
    for t in range(1, nb):
        ag(always, own_block, lambda: me, lambda t=t: place.moved(B=t))
    ag(always, own_block, lambda: me, lambda: sib)

    def line_arrival(i):
        def j():
            return place.expert(there(i, 0))

        def src():
            return xall.at[j()]

        landed(j())
        ag(lambda: [near[i] < a, place.inside(1)], src, j, lambda: place.moved(A=1))
        ag(lambda: [near[i] > a, place.inside(-1)], src, j, lambda: place.moved(A=-1))
        for t in range(1, nb):
            ag(always, src, j, lambda t=t: place.moved(B=t))
        ag(always, src, j, lambda: sib)

    def side_arrival(i):
        for t in range(1, nb):
            def j(t=t):
                return place.expert(there(i, t))

            landed(j())
            ag(always, lambda j=j: xall.at[j()], j, lambda: sib)

    before = {k: [] for k in range(steps)}
    for i in range(1, na):
        first = min(k for k, (q, _) in enumerate(order) if q == i)
        before[min(first, i)].append(lambda i=i: line_arrival(i))
    for i in range(na):
        first = min(k for k, (q, t) in enumerate(order) if q == i and t)
        before[min(first, i + 1)].append(lambda i=i: side_arrival(i))

    wloads = [pltpu.make_async_copy(h, v, w_sem.at[i]) for i, (h, v) in enumerate(
        ((win_h, win), (wdown_h, wdown), (wshin_h, wshin), (wshdown_h, wshdown)))]
    for load in wloads:
        load.start()

    def pair_index(k):
        i = choose(k, [q for q, _ in order])
        t = choose(k, [q for _, q in order])
        p = dict(pos, A=choose(i, near), B=lax.rem(pos["B"] + t, nb))
        return place.expert(p), place.expert(dict(p, C=1 - c))

    def cot_load(k, slot):
        one, two = pair_index(k)
        return [pltpu.make_async_copy(cot_ref.at[j], cv.at[slot, n], c_sem.at[slot, n]) for n, j in enumerate((one, two))]

    for load in cot_load(0, 0):
        load.start()
    gin_acc[...] = jnp.zeros_like(gin_acc)
    gdown_acc[...] = jnp.zeros_like(gdown_acc)
    gshin[...] = jnp.zeros_like(gshin)
    gshdown[...] = jnp.zeros_like(gshdown)
    for load in wloads:
        load.wait()

    def core_copy(k):
        return pltpu.make_async_remote_copy(
            src_ref=back_s.at[k % 2, 1], dst_ref=core_land.at[k], send_sem=core_send.at[k], recv_sem=core_recv.at[k],
            device_id=place.device(sib), device_id_type=MESH)

    b_steps = [k for k, (_, t) in enumerate(order) if t]

    def b_copy(k):
        i, t = order[k]
        n = b_steps.index(k)
        return pltpu.make_async_remote_copy(
            src_ref=bsrc.at[n % 2], dst_ref=b_land.at[i * (nb - 1) + t - 1], send_sem=b_send.at[n],
            recv_sem=b_recv.at[i * (nb - 1) + t - 1], device_id=place.device(place.moved(B=t)), device_id_type=MESH)

    def a_copy(i):
        return pltpu.make_async_remote_copy(
            src_ref=held.at[i], dst_ref=a_land.at[a], send_sem=a_send.at[i], recv_sem=a_recv.at[a],
            device_id=place.device(dict(pos, A=near[i])), device_id_type=MESH)

    def fetch(ref, sem):
        pltpu.make_async_copy(ref, ref, sem).wait()
        load = pltpu.make_async_copy(ref, stage, s_sem)
        load.start()
        load.wait()
        return stage[...].astype(wide)

    def chip_sum(k):
        i, t = order[k]
        value = (back_s[k % 2, 0].astype(wide) + fetch(core_land.at[k], core_recv.at[k])).astype(low)
        if t:
            n = b_steps.index(k)
            if n >= 2:
                b_copy(b_steps[n - 2]).wait_send()
            bsrc[n % 2] = value
            b_copy(k).start()
        else:
            held[i] = value

    def side_sum(i):
        value = held[i].astype(wide)
        for t in range(1, nb):
            value = value + fetch(b_land.at[i * (nb - 1) + t - 1], b_recv.at[i * (nb - 1) + t - 1])
        held[i] = value.astype(low)
        if i:
            a_copy(i).start()

    middle = {k: [] for k in range(steps)}
    late = []
    for k in range(steps):
        if k + 1 < steps:
            middle[k + 1].append(lambda k=k: chip_sum(k))
        else:
            late.append(lambda k=k: chip_sum(k))
    for i in list(range(1, na)) + [0]:
        ready = max(max(k for k, (q, t) in enumerate(order) if q == i and t) + 3, order.index((i, 0)) + 1)
        if ready < steps:
            middle[ready].append(lambda i=i: side_sum(i))
        else:
            late.append(lambda i=i: side_sum(i))

    def at(k, events):
        for n in range(steps):
            if events[n]:
                @pl.when(k == n)
                def _(n=n):
                    for run in events[n]:
                        run()

    def gg_copy(k, n, to):
        return pltpu.make_async_remote_copy(
            src_ref=gg_s.at[k, n], dst_ref=gg_out.at[me], send_sem=g_send.at[k, n], recv_sem=g_recv.at[me],
            device_id=(pos["Y"], to), device_id_type=MESH)

    def mixed_copy(slot, n, j):
        return pltpu.make_async_copy(mixed_s.at[slot, n], mixed.at[j], m_sem.at[slot, n])

    def step(k, carry):
        slot = lax.rem(k, 2)
        one, two = pair_index(k)
        at(k, before)

        @pl.when(k == 0)
        def _():
            load = pltpu.make_async_copy(x_ref, xv.at[0], x_sem.at[0])
            load.start()
            landed(two)
            load.wait()

        @pl.when(k > 0)
        def _():
            load = pltpu.make_async_copy(xall.at[one], xv.at[0], x_sem.at[0])
            load.start()
            landed(two)
            load.wait()

        load_two = pltpu.make_async_copy(xall.at[two], xv.at[1], x_sem.at[1])
        load_two.start()
        for load in cot_load(k, slot):
            load.wait()

        @pl.when(k + 1 < steps)
        def _():
            for load in cot_load(k + 1, 1 - slot):
                load.start()

        ranks = (rank_ref[one], rank_ref[two])
        slots = lax.broadcasted_iota(jnp.int32, (cap, toks), 0).astype(wide)
        picks = [r == slots for r in ranks]
        load_two.wait()
        crs = []
        for n in range(2):
            p = picks[n].astype(low)
            xr_s[n * cap:(n + 1) * cap, :] = mm(p, xv[n]).astype(low)
            crs.append(mm(p, cv[slot, n]).astype(low))
        cr = jnp.concatenate(crs, axis=0)
        gu = mm(xr_s[...], win[...])
        logits = gu[:, 2 * FF:]
        lane = lax.broadcasted_iota(jnp.int32, logits.shape, 1)
        logits = jnp.where(lane < experts, logits, -1e30)
        ex = jnp.exp(logits - jnp.max(logits, axis=1, keepdims=True))
        gate = jnp.sum(jnp.where(lane == me, ex, 0.0), axis=1, keepdims=True) / jnp.sum(ex, axis=1, keepdims=True)
        g = gu[:, :FF]
        u = gu[:, FF:2 * FF]
        s = sig(g)
        sg = g * s
        act_s[...] = (sg * u).astype(low)
        gr_s[...] = (gate * cr.astype(wide)).astype(low)
        dact = mm_nt(gr_s[...], wdown[...])
        dgu_s[:, :FF] = (dact * u * (s + sg * (1.0 - s))).astype(low)
        dgu_s[:, FF:] = (dact * sg).astype(low)
        o = mm(act_s[...], wdown[...]).astype(low)
        of = o.astype(wide)
        gg = jnp.sum(cr.astype(wide) * of, axis=1, keepdims=True)
        wtd = (gate * of).astype(low)
        ib = mm_nt(dgu_s[...], win[:, :2 * FF]).astype(low)
        at(k, middle)

        @pl.when(k >= 2)
        def _():
            for n, j in enumerate((one, two)):
                mixed_copy(slot, n, j).wait()

        for n in range(2):
            x = xv[n]
            ct = cv[slot, n]
            sh = mm(x, wshin[...])
            g2 = sh[:, :hid]
            u2 = sh[:, hid:]
            s2 = sig(g2)
            sg2 = g2 * s2
            sact = (sg2 * u2).astype(low)
            dsact = mm_nt(ct, wshdown[...])
            dsh = jnp.concatenate([dsact * u2 * (s2 + sg2 * (1.0 - s2)), dsact * sg2], axis=1).astype(low)
            p = picks[n].astype(low)
            rows = slice(n * cap, (n + 1) * cap)
            mixed_s[slot, n] = (mm_tn(p, wtd[rows]) + mm(sact, wshdown[...])).astype(low)
            back_s[slot, n] = (mm_tn(p, ib[rows]) + mm_nt(dsh, wshin[...])).astype(low)
            gg_s[k, n] = jnp.sum(jnp.where(picks[n], gg[rows], 0.0), axis=0, keepdims=True)
            gshdown[...] += mm_tn(sact, ct)
            gshin[...] += mm_tn(x, dsh)
        for n, j in enumerate((one, two)):
            mixed_copy(slot, n, j).start()
        at(k, {q: [lambda q=q: core_copy(q).start()] for q in range(steps)})

        @pl.when(k > 0)
        def _():
            gg_copy(k, 0, one).start()

        gg_copy(k, 1, two).start()
        gdown_acc[...] += mm_tn(act_s[...], gr_s[...])
        gin_acc[...] += mm_tn(xr_s[...], dgu_s[...])
        at(k, {q: [lambda q=q: core_copy(q - 1).wait_send()] if q else [] for q in range(steps)})
        return carry

    lax.fori_loop(0, steps, step, 0)
    gg_out[me] = gg_s[0, 0]
    win[:, :2 * FF] = gin_acc[...].astype(low)
    wdown[...] = gdown_acc[...].astype(low)
    outs = [pltpu.make_async_copy(win.at[:, pl.ds(0, 2 * FF)], gin_out, w_sem.at[0]),
            pltpu.make_async_copy(wdown, gdown_out, w_sem.at[1])]
    for out in outs:
        out.start()
    for run in late:
        run()
    total = held[0].astype(wide)
    for s in range(1, na):
        j = lax.rem(a + s, na)
        total = total + fetch(a_land.at[j], a_recv.at[j])
    gin_acc[:toks, :d] = total
    last = pltpu.make_async_copy(gin_acc.at[pl.ds(0, toks), pl.ds(0, d)], total_out, s_sem)
    last.start()
    last.wait()
    for out in outs:
        out.wait()
    core_copy(steps - 1).wait_send()
    for k in b_steps[-2:]:
        b_copy(k).wait_send()
    for i in range(1, na):
        a_copy(i).wait_send()
    for conds, copy in ag_sends:
        under(conds(), lambda copy=copy: copy().wait_send())
    for k in (steps - 2, steps - 1):
        one, two = pair_index(k)
        for n, j in enumerate((one, two)):
            mixed_copy(k % 2, n, j).wait()

    def gg_done(k, carry):
        one, two = pair_index(k)

        @pl.when(k > 0)
        def _():
            gg_copy(k, 0, one).wait_send()

        gg_copy(k, 1, two).wait_send()
        return carry

    lax.fori_loop(0, steps, gg_done, 0)

    def gg_wait(s, carry):
        j = lax.rem(me + s, n_exp)
        pltpu.make_async_copy(gg_out.at[j], gg_out.at[j], g_recv.at[j]).wait()
        return carry

    lax.fori_loop(1, n_exp, gg_wait, 0)


def fused(x, cot_all, rank, win, wdown, wshin, wshdown, n_dp, n_exp, experts, cap, cid):
    toks, d = x.shape
    size = sizes(n_dp, n_exp)
    na, nb = size["A"], size["B"]
    steps = na * nb
    hid = wshdown.shape[0]
    low, wide = jnp.bfloat16, jnp.float32
    hbm = pl.BlockSpec(memory_space=pl.ANY)
    vmem = pl.BlockSpec(memory_space=pltpu.VMEM)
    rows = 2 * cap
    block = (toks, d)
    dma = pltpu.SemaphoreType.DMA
    ag_count = 2 + (nb - 1) + 1 + (na - 1) * (2 + nb) + na * (nb - 1)
    flops = 2 * n_exp * (cap * d * FF * 9 + toks * cap * d * 4 + toks * d * hid * 9)
    return pl.pallas_call(
        functools.partial(fused_kernel, n_dp, n_exp, experts, cap),
        in_specs=[hbm, hbm, vmem, hbm, hbm, hbm, hbm],
        out_shape=[
            jax.ShapeDtypeStruct((n_exp,) + block, low),
            jax.ShapeDtypeStruct((n_exp,) + block, low),
            jax.ShapeDtypeStruct(block, wide),
            jax.ShapeDtypeStruct((n_exp, 1, toks), wide),
            jax.ShapeDtypeStruct((d, 2 * FF), low),
            jax.ShapeDtypeStruct((FF, d), low),
            jax.ShapeDtypeStruct((d, 2 * hid), wide),
            jax.ShapeDtypeStruct((hid, d), wide),
            jax.ShapeDtypeStruct((steps,) + block, low),
            jax.ShapeDtypeStruct((na * max(nb - 1, 1),) + block, low),
            jax.ShapeDtypeStruct((na,) + block, low),
        ],
        out_specs=[hbm, hbm, hbm, vmem, hbm, hbm, vmem, vmem, hbm, hbm, hbm],
        scratch_shapes=[
            pltpu.VMEM(win.shape, low), pltpu.VMEM(wdown.shape, low), pltpu.VMEM(wshin.shape, low),
            pltpu.VMEM(wshdown.shape, low),
            pltpu.VMEM((2,) + block, low), pltpu.VMEM((2, 2) + block, low),
            pltpu.VMEM((rows, d), low), pltpu.VMEM((rows, FF), low), pltpu.VMEM((rows, d), low),
            pltpu.VMEM((rows, 2 * FF), low),
            pltpu.VMEM((2, 2) + block, low), pltpu.VMEM((2, 2) + block, low), pltpu.VMEM((na,) + block, low),
            pltpu.VMEM((2,) + block, low), pltpu.VMEM(block, low),
            pltpu.VMEM((steps, 2, 1, toks), wide), pltpu.VMEM((d, 2 * FF), wide), pltpu.VMEM((FF, d), wide),
            dma((4,)), dma((2,)), dma((2, 2)), dma((2, 2)), dma(()),
            dma((ag_count,)), dma((n_exp,)), dma((steps,)), dma((steps,)),
            dma((na * max(nb - 1, 1),)), dma((na * max(nb - 1, 1),)), dma((na,)), dma((na,)),
            dma((steps, 2)), dma((n_exp,)),
        ],
        compiler_params=pltpu.CompilerParams(collective_id=cid, has_side_effects=True, vmem_limit_bytes=63 * 1024 * 1024),
        cost_estimate=pl.CostEstimate(flops=flops, bytes_accessed=100 * 1024 * 1024, transcendentals=0),
        name="experts_fused",
    )(x, cot_all, rank, win, wdown, wshin, wshdown)


def spread_kernel(n_dp, n_exp, x_ref, out_ref, send_sem, recv_sem):
    n = n_dp * n_exp
    me = lax.axis_index("dp") * n_exp + lax.axis_index("expert")
    barrier = pltpu.get_barrier_semaphore()

    def device(step):
        to = lax.rem(me + step, n)
        return (to // n_exp, lax.rem(to, n_exp))

    def greet(step, carry):
        pl.semaphore_signal(barrier, inc=1, device_id=device(step), device_id_type=MESH)
        return carry

    lax.fori_loop(1, n, greet, 0)
    pl.semaphore_wait(barrier, n - 1)

    def copy(step):
        return pltpu.make_async_remote_copy(
            src_ref=x_ref, dst_ref=out_ref.at[step], send_sem=send_sem.at[step], recv_sem=recv_sem.at[step],
            device_id=device(step), device_id_type=MESH)

    def start(step, carry):
        copy(step).start()
        return carry

    def wait(step, carry):
        copy(step).wait()
        return carry

    lax.fori_loop(1, n, start, 0)
    out_ref[0] = x_ref[...]
    lax.fori_loop(1, n, wait, 0)


def sum_everywhere(value, n_dp, n_exp, cid):
    n = n_dp * n_exp
    parts = pl.pallas_call(
        functools.partial(spread_kernel, n_dp, n_exp),
        out_shape=jax.ShapeDtypeStruct((n, 8, 128), jnp.float32),
        in_specs=[pl.BlockSpec(memory_space=pltpu.VMEM)],
        out_specs=pl.BlockSpec(memory_space=pltpu.VMEM),
        scratch_shapes=[pltpu.SemaphoreType.DMA((n,)), pltpu.SemaphoreType.DMA((n,))],
        compiler_params=pltpu.CompilerParams(collective_id=cid, has_side_effects=True),
        name="sum_everywhere",
    )(jnp.full((8, 128), value, jnp.float32))
    return jnp.sum(parts[:, 0, 0])


def swap_rows(x, n_dp):
    if n_dp != 2:
        return lax.all_gather(x, "dp", axis=0, tiled=True)
    other = lax.ppermute(x, "dp", [(0, 1), (1, 0)])
    first = lax.axis_index("dp") == 0
    return jnp.concatenate([jnp.where(first, x, other), jnp.where(first, other, x)], axis=0)


def halve_rows(x, n_dp):
    if n_dp != 2:
        return lax.psum_scatter(x, "dp", scatter_dimension=0, tiled=True).astype(jnp.float32)
    rows = x.shape[0] // 2
    first = lax.axis_index("dp") == 0
    top, bottom = x[:rows], x[rows:]
    other = lax.ppermute(jnp.where(first, bottom, top), "dp", [(0, 1), (1, 0)])
    return jnp.where(first, top, bottom).astype(jnp.float32) + other.astype(jnp.float32)


def local(
    tokens,
    lengths,
    routes,
    cotangent,
    norm_gains,
    gains_m,
    gains_v,
    w_qkv,
    m_qkv,
    v_qkv,
    w_out,
    m_out,
    v_out,
    w_shared_in,
    m_shared_in,
    v_shared_in,
    w_shared_down,
    m_shared_down,
    v_shared_down,
    w_router,
    m_router,
    v_router,
    w_expert_in,
    m_expert_in,
    v_expert_in,
    w_expert_down,
    m_expert_down,
    v_expert_down,
):
    both = ("dp", "expert")
    low = jnp.bfloat16
    wide = jnp.float32
    row_count = tokens.shape[0]
    expert_count = w_router.shape[1]
    n_dp = lax.axis_size("dp")
    n_exp = lax.axis_size("expert")
    n_all = n_dp * n_exp
    capacity = min(row_count, (5 * row_count * TOP // (4 * expert_count) + 7) // 8 * 8)
    score_scale = HD ** (-0.5)
    rows_w = w_qkv.shape[0]
    unit = w_shared_down.shape[0]
    my_expert = lax.axis_index("expert")

    pad = jnp.zeros((rows_w, 128 - expert_count - 2), wide)
    packed = jnp.concatenate([w_qkv, w_out, w_router, norm_gains.T, pad], axis=1).astype(low)
    full = gather(packed, n_dp, n_exp, True, 1).reshape(D, -1)
    qkv_full = full[:, : 3 * H * HD]
    out_full = full[:, 3 * H * HD : 3 * H * HD + D]
    small_full = full[:, 3 * H * HD + D :]
    router_full = small_full[:, :expert_count]
    gain_one = small_full[:, expert_count].astype(wide)
    gain_two = small_full[:, expert_count + 1].astype(wide)
    cot_all = lax.all_gather(cotangent, "expert", axis=0, tiled=False)
    routes_all = lax.all_gather(routes, "expert", axis=0, tiled=False)
    expert_in_full = swap_rows(w_expert_in[0].astype(low), n_dp)
    expert_down_full = swap_rows(w_expert_down[0].astype(low), n_dp)
    shin_send = (
        w_shared_in.astype(low)
        .reshape(rows_w, 2, n_dp, n_exp, unit)
        .transpose(3, 0, 1, 2, 4)
        .reshape(n_exp, rows_w, 2 * n_dp * unit)
    )
    shin_send = jnp.concatenate([shin_send] * n_dp, axis=0)
    shin_mine = lax.all_to_all(shin_send, both, 0, 0, tiled=True).reshape(D, 2 * n_dp * unit)
    shdown_mine = swap_rows(w_shared_down.astype(low), n_dp)
    half = n_dp * unit

    inputs = tokens.astype(wide)
    cosine, sine_table, allowed = rotary_tables(lengths[0], row_count, HD)
    scale_one = rms_scale(inputs)
    normed_one = inputs * scale_one
    attn_in = (normed_one * gain_one).astype(low)
    projected = jnp.dot(attn_in, qkv_full, preferred_element_type=wide).reshape(
        row_count, 3, H, HD
    )
    queries = rotate(projected[:, 0], cosine, sine_table).astype(low)
    keys_rot = rotate(projected[:, 1], cosine, sine_table).astype(low)
    values_low = projected[:, 2].astype(low)
    raw_scores = (
        jnp.einsum("qhd,khd->hqk", queries, keys_rot, preferred_element_type=wide) * score_scale
    )
    scores = jnp.where(allowed[None], raw_scores, NEGATIVE)
    row_max = jnp.max(scores, axis=-1, keepdims=True)
    exped = jnp.exp(scores - row_max)
    probs_attn = exped / jnp.sum(exped, axis=-1, keepdims=True)
    probs_low = probs_attn.astype(low)
    mixed_heads = jnp.einsum("hqk,khd->qhd", probs_low, values_low, preferred_element_type=wide)
    heads_low = mixed_heads.astype(low).reshape(row_count, H * HD)
    residual = inputs + jnp.dot(heads_low, out_full, preferred_element_type=wide)
    scale_two = rms_scale(residual)
    normed_two = residual * scale_two
    mlp_in = (normed_two * gain_two).astype(low)
    logits = jnp.dot(mlp_in, router_full, preferred_element_type=wide)
    router_probs = jax.nn.softmax(logits, axis=-1)

    routed_here = jnp.any(routes_all == my_expert, axis=2)
    rank = jnp.where(routed_here, jnp.cumsum(routed_here.astype(jnp.int32), axis=1) - 1, -1).astype(wide)
    hid = (half + 127) // 128 * 128
    cap = (capacity + 15) // 16 * 16
    win = jnp.concatenate([expert_in_full, router_full, jnp.zeros((D, 128 - expert_count), low)], axis=1)
    gap = jnp.zeros((D, hid - half), low)
    wshin = jnp.concatenate([shin_mine[:, :half], gap, shin_mine[:, half:], gap], axis=1)
    wshdown = jnp.concatenate([shdown_mine, jnp.zeros((hid - half, D), low)], axis=0)
    _, mixed_part, back_sum, gate_grad, grad_ein, grad_edown, shin_wide, shdown_wide, _, _, _ = fused(
        mlp_in, cot_all, rank[:, None, :], win, expert_down_full, wshin, wshdown, n_dp, n_exp, expert_count, cap, 2
    )
    mixed_sum = lax.psum_scatter(mixed_part, "expert", scatter_dimension=0, tiled=False)
    mixed = (residual + mixed_sum.astype(wide)).astype(low)
    grad_shin = jnp.concatenate([shin_wide[:, :half], shin_wide[:, hid : hid + half]], axis=1)
    grad_shdown = shdown_wide[:half]
    prob_grad = gate_grad[:, 0, :].T
    logit_grad = (
        router_probs * (prob_grad - jnp.sum(prob_grad * router_probs, axis=-1, keepdims=True))
    ).astype(low)
    grad_router = jnp.einsum("td,te->de", mlp_in, logit_grad, preferred_element_type=wide)
    mlp_in_grad = back_sum + jnp.einsum(
        "te,de->td", logit_grad, router_full, preferred_element_type=wide
    )
    out_grad = cotangent.astype(wide)
    grad_gain_two = jnp.sum(mlp_in_grad * normed_two, axis=0)
    scaled_two = mlp_in_grad * gain_two
    resid_grad = out_grad + scale_two * (
        scaled_two - normed_two * jnp.mean(scaled_two * normed_two, axis=-1, keepdims=True)
    )
    resid_low = resid_grad.astype(low)
    grad_out = jnp.einsum("ti,td->id", heads_low, resid_low, preferred_element_type=wide)
    heads_grad = jnp.einsum("td,id->ti", resid_low, out_full, preferred_element_type=wide)
    heads_grad = heads_grad.astype(low).reshape(row_count, H, HD)
    attn_prob_grad = jnp.einsum("qhd,khd->hqk", heads_grad, values_low, preferred_element_type=wide)
    value_grad = jnp.einsum("hqk,qhd->khd", probs_low, heads_grad, preferred_element_type=wide)
    score_grad = probs_attn * (
        attn_prob_grad - jnp.sum(attn_prob_grad * probs_attn, axis=-1, keepdims=True)
    )
    score_grad = score_grad.astype(low)
    query_grad = (
        jnp.einsum("hqk,khd->qhd", score_grad, keys_rot, preferred_element_type=wide) * score_scale
    )
    key_grad = (
        jnp.einsum("hqk,qhd->khd", score_grad, queries, preferred_element_type=wide) * score_scale
    )
    projected_grad = jnp.stack(
        [
            rotate_back(query_grad, cosine, sine_table),
            rotate_back(key_grad, cosine, sine_table),
            value_grad,
        ],
        axis=1,
    )
    projected_grad = projected_grad.reshape(row_count, 3 * H * HD).astype(low)
    grad_qkv = jnp.einsum("td,tk->dk", attn_in, projected_grad, preferred_element_type=wide)
    attn_grad = jnp.einsum("tk,dk->td", projected_grad, qkv_full, preferred_element_type=wide)
    grad_gain_one = jnp.sum(attn_grad * normed_one, axis=0)
    scaled_one = attn_grad * gain_one
    input_grad = resid_grad + scale_one * (
        scaled_one - normed_one * jnp.mean(scaled_one * normed_one, axis=-1, keepdims=True)
    )

    small_grad = jnp.concatenate(
        [grad_router, grad_gain_one[:, None], grad_gain_two[:, None], jnp.zeros((D, 128 - expert_count - 2), wide)],
        axis=1,
    )
    qkv_own, out_own, small_own = reduce_dense(
        [g.astype(low).reshape(n_all, rows_w, -1) for g in (grad_qkv, grad_out, small_grad)], n_dp, n_exp, 5
    )
    shin_back = lax.all_to_all(
        grad_shin.astype(low).reshape(n_all, rows_w, 2 * half), both, 0, 0, tiled=True
    )
    shin_own = jnp.sum(
        shin_back.reshape(n_dp, n_exp, rows_w, 2, n_dp, unit).astype(wide), axis=0
    )
    shin_own = shin_own.transpose(1, 2, 3, 0, 4).reshape(rows_w, 2 * FF)
    owned_grads = (
        small_own[:, expert_count : expert_count + 2].T,
        qkv_own,
        out_own,
        shin_own,
        lax.psum_scatter(grad_shdown, "dp", scatter_dimension=0, tiled=True),
        small_own[:, :expert_count],
        halve_rows(grad_ein, n_dp)[None],
        halve_rows(grad_edown, n_dp)[None],
    )
    squares = sum((jnp.sum(grad_part * grad_part) for grad_part in owned_grads))
    total_squares = sum_everywhere(squares, n_dp, n_exp, 6)
    grad_norm = jnp.sqrt(total_squares)
    factor = jnp.minimum(1.0, CLIP / grad_norm)
    weights = (
        norm_gains,
        w_qkv,
        w_out,
        w_shared_in,
        w_shared_down,
        w_router,
        w_expert_in,
        w_expert_down,
    )
    firsts = (
        gains_m,
        m_qkv,
        m_out,
        m_shared_in,
        m_shared_down,
        m_router,
        m_expert_in,
        m_expert_down,
    )
    seconds = (
        gains_v,
        v_qkv,
        v_out,
        v_shared_in,
        v_shared_down,
        v_router,
        v_expert_in,
        v_expert_down,
    )
    rates = (
        GAIN_RATE,
        D ** (-0.5),
        (H * HD // 64) ** (-0.5),
        D ** (-0.5),
        FF ** (-0.5),
        (4 * D) ** (-0.5),
        D ** (-0.5),
        (FF // 64) ** (-0.5),
    )
    decays = (0.0, DECAY, DECAY, DECAY, DECAY, DECAY, DECAY, DECAY)
    updated = []
    for weight, first_moment, second_moment, gradient, step_rate, decay_rate in zip(
        weights, firsts, seconds, owned_grads, rates, decays
    ):
        updated.extend(
            adam_update(
                weight, first_moment, second_moment, gradient, factor, step_rate, decay_rate
            )
        )
    return (
        mixed,
        input_grad,
        updated[0],
        updated[1],
        updated[2],
        updated[3],
        updated[4],
        updated[5],
        updated[6],
        updated[7],
        updated[8],
        updated[9],
        updated[10],
        updated[11],
        updated[12],
        updated[13],
        updated[14],
        updated[15],
        updated[16],
        updated[17],
        updated[18],
        updated[19],
        updated[20],
        updated[21],
        updated[22],
        updated[23],
        grad_norm,
    )


def solution(mesh):
    placed = (
        P(("dp", "expert"), None),
        P(("dp", "expert"), None),
        P(("dp", "expert"), None),
        P(("dp", "expert"), None),
        P(None, ("dp", "expert")),
        P(None, ("dp", "expert")),
        P(None, ("dp", "expert")),
        P(("dp", "expert"), None),
        P(("dp", "expert"), None),
        P(("dp", "expert"), None),
        P(("dp", "expert"), None),
        P(("dp", "expert"), None),
        P(("dp", "expert"), None),
        P(("dp", "expert"), None),
        P(("dp", "expert"), None),
        P(("dp", "expert"), None),
        P(("dp", "expert"), None),
        P(("dp", "expert"), None),
        P(("dp", "expert"), None),
        P(("dp", "expert"), None),
        P(("dp", "expert"), None),
        P(("dp", "expert"), None),
        P("expert", "dp", None),
        P("expert", "dp", None),
        P("expert", "dp", None),
        P("expert", "dp", None),
        P("expert", "dp", None),
        P("expert", "dp", None),
    )
    return jax.shard_map(
        local,
        mesh=mesh,
        in_specs=placed,
        out_specs=(
            P(("dp", "expert"), None),
            P(("dp", "expert"), None),
            P(None, ("dp", "expert")),
            P(None, ("dp", "expert")),
            P(None, ("dp", "expert")),
            P(("dp", "expert"), None),
            P(("dp", "expert"), None),
            P(("dp", "expert"), None),
            P(("dp", "expert"), None),
            P(("dp", "expert"), None),
            P(("dp", "expert"), None),
            P(("dp", "expert"), None),
            P(("dp", "expert"), None),
            P(("dp", "expert"), None),
            P(("dp", "expert"), None),
            P(("dp", "expert"), None),
            P(("dp", "expert"), None),
            P(("dp", "expert"), None),
            P(("dp", "expert"), None),
            P(("dp", "expert"), None),
            P("expert", "dp", None),
            P("expert", "dp", None),
            P("expert", "dp", None),
            P("expert", "dp", None),
            P("expert", "dp", None),
            P("expert", "dp", None),
            P(),
        ),
        check_vma=False,
    )
```

```python
import functools
import itertools

import jax
import jax.numpy as jnp
from jax import lax
from jax.experimental import pallas as pl
from jax.experimental.pallas import tpu as pltpu
from jax.sharding import PartitionSpec as P

D = 1280
H = 10
HD = 128
FF = 896
TOP = 6
ADAM_STEP = 5
GIVEN = 1280


EPS = 1e-06
ROPE_BASE = 10000.0
BETA_ONE = 0.9
BETA_TWO = 0.95
ADAM_EPS = 1e-08
DECAY = 0.1
CLIP = 1.0
GAIN_RATE = 0.5
NEGATIVE = -1e30


def rms_scale(values):
    return lax.rsqrt(jnp.mean(values * values, axis=-1, keepdims=True) + EPS)


def rotary_tables(seq_lengths, row_count, head_width):
    position = jnp.arange(row_count, dtype=jnp.int32)
    seq_ends = jnp.cumsum(seq_lengths)
    segment = jnp.sum((position[:, None] >= seq_ends[None, :]).astype(jnp.int32), axis=1)
    starts = seq_ends - seq_lengths
    slot_ids = jnp.arange(seq_lengths.shape[0], dtype=jnp.int32)
    first_row = jnp.sum(
        jnp.where(segment[:, None] == slot_ids[None, :], starts[None, :], 0), axis=1
    )
    seq_place = (position - first_row).astype(jnp.float32)
    inv_freq = ROPE_BASE ** (-jnp.arange(head_width // 2, dtype=jnp.float32) * 2.0 / head_width)
    phase_angle = seq_place[:, None] * inv_freq[None, :]
    cosine = jnp.concatenate([jnp.cos(phase_angle), jnp.cos(phase_angle)], axis=1)
    sine_table = jnp.concatenate([jnp.sin(phase_angle), jnp.sin(phase_angle)], axis=1)
    allowed = (segment[:, None] == segment[None, :]) & (position[None, :] <= position[:, None])
    return (cosine, sine_table, allowed)


def rotate(vectors, cosine, sine_table):
    half_width = vectors.shape[-1] // 2
    turned = jnp.concatenate([-vectors[..., half_width:], vectors[..., :half_width]], axis=-1)
    return vectors * cosine[:, None, :] + turned * sine_table[:, None, :]


def rotate_back(gradient, cosine, sine_table):
    half_width = gradient.shape[-1] // 2
    scaled_sine = gradient * sine_table[:, None, :]
    turned = jnp.concatenate(
        [scaled_sine[..., half_width:], -scaled_sine[..., :half_width]], axis=-1
    )
    return gradient * cosine[:, None, :] + turned


def silu_slope(gate_vals):
    logistic = jax.nn.sigmoid(gate_vals)
    return logistic * (1.0 + gate_vals * (1.0 - logistic))


def swiglu_back(act_grad, gate_up):
    gate_part = gate_up[:, :FF]
    up_part = gate_up[:, FF:]
    return jnp.concatenate(
        [act_grad * up_part * silu_slope(gate_part), act_grad * jax.nn.silu(gate_part)], axis=1
    ).astype(jnp.bfloat16)


def adam_update(weight, first_moment, second_moment, gradient, factor, step_rate, decay_rate):
    clipped = gradient * factor
    first_new = BETA_ONE * first_moment + (1.0 - BETA_ONE) * clipped
    second_new = BETA_TWO * second_moment + (1.0 - BETA_TWO) * clipped * clipped
    first_hat = first_new / (1.0 - BETA_ONE**ADAM_STEP)
    second_hat = second_new / (1.0 - BETA_TWO**ADAM_STEP)
    weight_new = weight - step_rate * (
        first_hat / (jnp.sqrt(second_hat) + ADAM_EPS) + decay_rate * weight
    )
    return (weight_new, first_new, second_new)


MESH = pl.DeviceIdType.MESH


class Place:
    def __init__(self, n_dp, n_exp):
        rest = n_exp // 2
        na = 4 if rest % 4 == 0 else rest
        self.size = {"A": na, "B": rest // na, "C": 2, "Y": n_dp}
        e = lax.axis_index("expert")
        nb = self.size["B"]
        self.pos = {"A": e // (2 * nb), "B": (e // 2) % nb, "C": e % 2, "Y": lax.axis_index("dp")}

    def expert(self, pos):
        return (pos["A"] * self.size["B"] + pos["B"]) * 2 + pos["C"]

    def flat(self, pos):
        return pos["Y"] * (2 * self.size["A"] * self.size["B"]) + self.expert(pos)

    def device(self, pos):
        return (pos["Y"], self.expert(pos))

    def moved(self, **steps):
        pos = dict(self.pos)
        for axis, step in steps.items():
            if axis == "A":
                pos[axis] = pos[axis] + step
            else:
                pos[axis] = lax.rem(pos[axis] + step, self.size[axis])
        return pos

    def inside(self, step):
        there = self.pos["A"] + step
        return (there >= 0) & (there < self.size["A"])

    def greet(self, axes, line_all):
        barrier = pltpu.get_barrier_semaphore()
        total = 0
        for axis in axes:
            if axis == "A":
                reach = range(1, self.size["A"]) if line_all else (1,)
                for step in [s * d for d in reach for s in (1, -1)]:
                    near = self.inside(step)

                    @pl.when(near)
                    def _(step=step):
                        pl.semaphore_signal(barrier, inc=1, device_id=self.device(self.moved(A=step)), device_id_type=MESH)

                    total = total + jnp.where(near, 1, 0)
            else:
                for step in range(1, self.size[axis]):
                    pl.semaphore_signal(barrier, inc=1, device_id=self.device(self.moved(**{axis: step})), device_id_type=MESH)
                    total = total + 1
        pl.semaphore_wait(barrier, total)


def under(conds, body):
    if conds:
        both = conds[0]
        for c in conds[1:]:
            both = both & c
        pl.when(both)(body)
    else:
        body()


PACE = {"A": 4, "B": 5, "Y": 5, "C": 1}


def plan_gather(size, orders):
    events = []
    for part, order in enumerate(orders):
        spans = []
        for axis in order:
            n = size[axis]
            spans.append(range(1 - n, n) if axis == "A" else range(n))
        for offs in itertools.product(*spans):
            when = 0
            for axis, o in zip(order, offs):
                when += PACE[axis] * (abs(o) if axis == "A" else (1 if o else 0))
            events.append((when, part, offs))
    events.sort(key=lambda ev: ev[0])
    return events


def gather_body(place, orders, slices, own_ref, out_ref, block_of, send_sem, recv_sem):
    size = place.size
    sends = []
    count = [0]

    def send(conds, part, src_block, src, to):
        slot = count[0]
        count[0] += 1
        lo, n = slices[part]

        def copy():
            j = src_block()
            return pltpu.make_async_remote_copy(
                src_ref=(own_ref if src is None else out_ref.at[j]).at[:, pl.ds(lo, n)],
                dst_ref=out_ref.at[j].at[:, pl.ds(lo, n)],
                send_sem=send_sem.at[slot],
                recv_sem=recv_sem.at[part, j],
                device_id=place.device(to()),
                device_id_type=MESH,
            )

        under(conds, lambda: copy().start())
        sends.append((conds, copy))

    for _, part, offs in plan_gather(size, orders):
        order = orders[part]
        steps = dict(zip(order, offs))
        last = max([i for i, o in enumerate(offs) if o], default=-1)
        conds = []
        if steps["A"]:
            conds.append(place.inside(steps["A"]))

        def block(steps=steps):
            return block_of(place.moved(**{k: o for k, o in steps.items() if o}))

        if last >= 0:
            lo, n = slices[part]

            def wait(block=block, part=part, lo=lo, n=n):
                j = block()
                pltpu.make_async_copy(
                    out_ref.at[j].at[:, pl.ds(lo, n)], out_ref.at[j].at[:, pl.ds(lo, n)], recv_sem.at[part, j]
                ).wait()

            under(conds, wait)
        src = None if last < 0 else out_ref
        for i in range(max(last, 0), len(order)):
            axis = order[i]
            if axis == "A":
                ways = (1, -1) if i > last else ((1,) if steps["A"] < 0 else (-1,))
                for way in ways:
                    send(conds + [place.inside(way)], part, block, src, lambda way=way: place.moved(A=way))
            elif i > last:
                for t in range(1, size[axis]):
                    send(conds, part, block, src, lambda axis=axis, t=t: place.moved(**{axis: t}))
    for conds, copy in sends:
        under(conds, lambda copy=copy: copy().wait_send())


def count_gather(size, orders):
    total = 0
    for _, part, offs in plan_gather(size, orders):
        order = orders[part]
        last = max([i for i, o in enumerate(offs) if o], default=-1)
        for i in range(max(last, 0), len(order)):
            if order[i] == "A":
                total += 2 if i > last else 1
            elif i > last:
                total += size[order[i]] - 1
    return total


def sizes(n_dp, n_exp):
    rest = n_exp // 2
    na = 4 if rest % 4 == 0 else rest
    return {"A": na, "B": rest // na, "C": 2, "Y": n_dp}


def gather_kernel(n_dp, n_exp, orders, slices, dense, x_ref, out_ref, send_sem, recv_sem, local_sem):
    place = Place(n_dp, n_exp)
    block_of = place.flat if dense else place.expert
    place.greet(orders[0], False)
    own = pltpu.make_async_copy(x_ref, out_ref.at[block_of(place.pos)], local_sem)
    own.start()
    gather_body(place, orders, slices, x_ref, out_ref, block_of, send_sem, recv_sem)
    own.wait()


def gather(x, n_dp, n_exp, dense, cid, parts=None):
    size = sizes(n_dp, n_exp)
    rows, cols = x.shape
    if dense:
        orders = ("ABYC", "AYBC")
        half = cols // 256 * 128
        slices = ((0, half), (half, cols - half))
    else:
        orders = parts or ("ABC",)
        w = cols // len(orders)
        slices = tuple((i * w, w) for i in range(len(orders)))
    blocks = n_exp * (n_dp if dense else 1)
    return pl.pallas_call(
        functools.partial(gather_kernel, n_dp, n_exp, orders, slices, dense),
        out_shape=jax.ShapeDtypeStruct((blocks, rows, cols), x.dtype),
        in_specs=[pl.BlockSpec(memory_space=pl.ANY)],
        out_specs=pl.BlockSpec(memory_space=pl.ANY),
        scratch_shapes=[
            pltpu.SemaphoreType.DMA((count_gather(size, orders),)),
            pltpu.SemaphoreType.DMA((len(orders), blocks)),
            pltpu.SemaphoreType.DMA(()),
        ],
        compiler_params=pltpu.CompilerParams(collective_id=cid, has_side_effects=True),
        name="gather_dense" if dense else "gather_group",
    )(x)


def line_order(n):
    out = []
    for i in range((n + 1) // 2):
        out.append(i)
        if n - 1 - i != i:
            out.append(n - 1 - i)
    return out


def stage_slots(size, order):
    slots = {}
    for i, axis in enumerate(order):
        rest = [line_order(size[x]) if x == "A" else range(size[x]) for x in order[i + 1:]]
        if axis == "A":
            for who in range(size["A"]):
                slots[(i, who, ())] = len(slots)
        else:
            for who in range(1, size[axis]):
                for r in itertools.product(*rest):
                    slots[(i, who, r)] = len(slots)
    return slots


def reduce_body(place, orders, slices, g_refs, block_of, land, base, send_sem, recv_sem, finish):
    size = place.size
    tables = [stage_slots(size, order) for order in orders]
    sends = []
    n = [0]

    def target(order, i, o, rest):
        pos = dict(place.pos)
        for axis, v in zip(order[i:], (o,) + tuple(rest)):
            if axis == "A":
                pos["A"] = v
            else:
                pos[axis] = lax.rem(pos[axis] + v, size[axis])
        return pos

    def send(conds, part, src, slot, to):
        at = n[0]
        n[0] += 1

        def copy():
            return pltpu.make_async_remote_copy(
                src_ref=src(), dst_ref=land[part].at[slot], send_sem=send_sem.at[at],
                recv_sem=recv_sem.at[base[part] + slot], device_id=place.device(to()), device_id_type=MESH)

        under(conds, lambda: copy().start())
        sends.append((conds, copy))

    def wait(part, slot):
        ref = land[part].at[slot]
        pltpu.make_async_copy(ref, ref, recv_sem.at[base[part] + slot]).wait()

    def rests(order, i):
        return list(itertools.product(*[line_order(size[x]) if x == "A" else range(size[x]) for x in order[i:]]))

    def far_first(items):
        return sorted(items, key=lambda r: tuple(0 if (isinstance(v, int) and v) else 1 for v in r[:-1]))

    for part, order in enumerate(orders):
        g_ref, lo, w = g_refs[slices[part][0]], slices[part][1], slices[part][2]
        axis = order[0]
        for t in range(1, size[axis]):
            for r in far_first(rests(order, 1)):
                def src(order=order, t=t, r=r, lo=lo, w=w, g_ref=g_ref):
                    return g_ref.at[block_of(target(order, 0, t, r)), :, pl.ds(lo, w)]
                send([], part, src, tables[part][(0, t, r)], lambda axis=axis, t=t: place.moved(**{axis: t}))
    for i in range(1, len(orders[0])):
        for pick in far_first(rests(orders[0], i)):
            for part, order in enumerate(orders):
                g_ref, lo, w = g_refs[slices[part][0]], slices[part][1], slices[part][2]
                axis = order[i]
                before = order[i - 1]
                r = pick
                got = [tables[part][(i - 1, t, r)] for t in range(1, size[before])]
                for slot in got:
                    wait(part, slot)
                if i == 1:
                    total = g_ref[block_of(target(order, 1, r[0], r[1:])), :, lo:lo + w].astype(jnp.float32)
                else:
                    total = land[part][tables[part][(i - 2, 1, (0,) + r)]].astype(jnp.float32)
                for slot in got:
                    total = total + land[part][slot].astype(jnp.float32)
                land[part][got[0]] = total.astype(land[part].dtype)
                o, later = r[0], r[1:]
                def src(part=part, slot=got[0]):
                    return land[part].at[slot]
                if axis == "A":
                    a = place.pos["A"]
                    at = n[0]
                    n[0] += 1
                    def copy(part=part, slot=got[0], o=o, at=at, i=i):
                        first = tables[part][(i, 0, ())]
                        return pltpu.make_async_remote_copy(
                            src_ref=land[part].at[slot], dst_ref=land[part].at[first + a], send_sem=send_sem.at[at],
                            recv_sem=recv_sem.at[base[part] + first + a],
                            device_id=place.device(dict(place.pos, A=o)), device_id_type=MESH)
                    away = [a != o]
                    under(away, lambda copy=copy: copy().start())
                    sends.append((away, copy))
                elif o:
                    send([], part, src, tables[part][(i, o, later)], lambda axis=axis, o=o: place.moved(**{axis: o}))
    last = len(orders[0]) - 1
    for part, order in enumerate(orders):
        own = tables[part][(last - 1, 1, (0,))]
        a = place.pos["A"]
        first = tables[part][(last, 0, ())]
        step = tables[part][(last - 1, 1, (line_order(size["A"])[1],))] - own if size["A"] > 1 else 0
        mine = own
        for k, p in enumerate(line_order(size["A"])):
            mine = jnp.where(a == p, tables[part][(last - 1, 1, (p,))], mine)
        total = land[part][mine].astype(jnp.float32)
        for d in range(1, size["A"]):
            j = lax.rem(a + d, size["A"])
            wait(part, first + j)
            total = total + land[part][first + j].astype(jnp.float32)
        finish(part, total)
    for conds, copy in sends:
        under(conds, lambda copy=copy: copy().wait_send())


def count_reduce(size, orders):
    total = 0
    for order in orders:
        for i, axis in enumerate(order):
            rest = 1
            for x in order[i + 1:]:
                rest *= size[x]
            total += size["A"] if axis == "A" else (size[axis] - 1) * rest
    return total


def norm_exchange(place, value_ref, land, send_sem, recv_sem):
    for n, axis in enumerate("CBYA"):
        mine = place.pos[axis]
        size = place.size[axis]
        land[n, mine] = value_ref[...]

        def copy(step, n=n, axis=axis, mine=mine, size=size):
            to = dict(place.pos)
            to[axis] = lax.rem(mine + step, size)
            return pltpu.make_async_remote_copy(
                src_ref=land.at[n, mine], dst_ref=land.at[n, mine], send_sem=send_sem.at[n, step],
                recv_sem=recv_sem.at[n, mine], device_id=place.device(to), device_id_type=MESH)

        for step in range(1, size):
            copy(step).start()
        for step in range(1, size):
            j = lax.rem(mine + step, size)
            pltpu.make_async_copy(land.at[n, j], land.at[n, j], recv_sem.at[n, j]).wait()
        total = land[n, 0]
        for j in range(1, size):
            total = total + land[n, j]
        for step in range(1, size):
            copy(step).wait_send()
        value_ref[...] = total


def reduce_kernel(n_dp, n_exp, orders, slices, dense, arrays, sq_ref, *refs):
    g_refs, out_refs, scratch = refs[:arrays], refs[arrays:2 * arrays], refs[2 * arrays + 1:]
    norm_ref = refs[2 * arrays]
    land, (send_sem, recv_sem, norm_land, norm_send, norm_recv) = scratch[:-5], scratch[-5:]
    place = Place(n_dp, n_exp)
    place.greet(orders[0], True)
    base = [0]
    for order in orders:
        base.append(base[-1] + len(stage_slots(place.size, order)))

    def finish(part, total):
        which, lo, w = slices[part]
        out_refs[which][:, lo:lo + w] = total

    reduce_body(place, orders, slices, g_refs, place.flat if dense else place.expert, land, base, send_sem, recv_sem, finish)
    total = sq_ref[...]
    for out in out_refs:
        total = total + jnp.sum(out[...] * out[...])
    norm_ref[...] = total
    norm_exchange(place, norm_ref, norm_land, norm_send, norm_recv)


def reduce_dense(arrays, squares, n_dp, n_exp, cid):
    size = sizes(n_dp, n_exp)
    blocks, rows = arrays[0].shape[:2]
    orders, slices = [], []
    for which, g in enumerate(arrays):
        cols = g.shape[2]
        half = cols // 256 * 128
        for order, lo, w in (("CBYA", 0, half), ("CYBA", half, cols - half)):
            if w:
                orders.append(order)
                slices.append((which, lo, w))
    slots = [len(stage_slots(size, order)) for order in orders]
    top = max(size.values())
    return pl.pallas_call(
        functools.partial(reduce_kernel, n_dp, n_exp, orders, slices, True, len(arrays)),
        out_shape=[jax.ShapeDtypeStruct((rows, g.shape[2]), jnp.float32) for g in arrays] + [
            jax.ShapeDtypeStruct((8, 128), jnp.float32)],
        in_specs=[pl.BlockSpec(memory_space=pltpu.VMEM)] * (len(arrays) + 1),
        out_specs=[pl.BlockSpec(memory_space=pltpu.VMEM)] * (len(arrays) + 1),
        scratch_shapes=[pltpu.VMEM((k, rows, s[2]), g.dtype) for k, s in zip(slots, slices)] + [
            pltpu.SemaphoreType.DMA((count_reduce(size, orders),)),
            pltpu.SemaphoreType.DMA((sum(slots),)),
            pltpu.VMEM((4, top, 8, 128), jnp.float32),
            pltpu.SemaphoreType.DMA((4, top)),
            pltpu.SemaphoreType.DMA((4, top)),
        ],
        compiler_params=pltpu.CompilerParams(collective_id=cid, has_side_effects=True, vmem_limit_bytes=60 * 1024 * 1024),
        name="reduce_dense",
    )(jnp.full((8, 128), squares, jnp.float32), *arrays)


def mm(a, b):
    return jnp.dot(a, b, preferred_element_type=jnp.float32)


def mm_nt(a, b):
    return lax.dot_general(a, b, (((1,), (1,)), ((), ())), preferred_element_type=jnp.float32)


def mm_tn(a, b):
    return lax.dot_general(a, b, (((0,), (0,)), ((), ())), preferred_element_type=jnp.float32)


def sig(v):
    return 1.0 / (1.0 + jnp.exp(-v))


def near_first(na):
    table = []
    for a in range(na):
        row = [a]
        for d in range(1, na):
            row += [p for p in ((a - d, a + d) if a < na // 2 else (a + d, a - d)) if 0 <= p < na]
        table.append(row)
    return table


def pair_order(na, nb):
    order = [(0, 0), (1, 0)]
    if na > 2:
        order += [(2, 0)] + [(2, t) for t in range(1, nb)]
    for i in range(3, na):
        order += [(i, t) for t in range(1, nb)] + [(i, 0)]
    return order + [(1, t) for t in range(1, nb)] + [(0, t) for t in range(1, nb)]


def choose(index, values):
    out = values[-1]
    for i in range(len(values) - 1):
        out = jnp.where(index == i, values[i], out)
    return out


def fused_kernel(n_dp, n_exp, experts, cap, halves, x_ref, cot_ref, rank_own, *refs):
    win_h, wdown_h, refs = refs[:halves], refs[halves:2 * halves], refs[2 * halves:]
    wrt_h, wshin_h, wshdown_h, xall, mixed, total_out, gg_out, refs = *refs[:7], refs[7:]
    gin_out, gdown_out, refs = refs[:halves], refs[halves:2 * halves], refs[2 * halves:]
    fused_body(n_dp, n_exp, experts, cap, x_ref, cot_ref, rank_own, win_h, wdown_h, wrt_h, wshin_h, wshdown_h,
               xall, mixed, total_out, gg_out, gin_out, gdown_out, *refs)


def fused_body(n_dp, n_exp, experts, cap, x_ref, cot_ref, rank_own, win_h, wdown_h, wrt_h, wshin_h, wshdown_h,
                 xall, mixed, total_out, gg_out, gin_out, gdown_out, gshin, gshdown, core_land, b_land, a_land,
                 win, wdown, wrt, wshin, wshdown, rank_ref, xv, cv, xr_s, act_s, gr_s, dgu_s, back_s, mixed_s, held, bsrc, stage,
                 gg_s, gin_acc, gdown_acc,
                 w_sem, x_sem, c_sem, m_sem, s_sem, ag_send, ag_recv, core_send, core_recv, b_send, b_recv,
                 a_send, a_recv, g_send, g_recv, r_send, r_recv):
    low, wide = jnp.bfloat16, jnp.float32
    place = Place(n_dp, n_exp)
    na, nb = place.size["A"], place.size["B"]
    pos = place.pos
    a, c, me = pos["A"], pos["C"], place.expert(pos)
    toks, d = x_ref.shape[0], wdown.shape[1]
    given = cot_ref.shape[2]
    hid = wshdown.shape[0]
    table = near_first(na)
    order = pair_order(na, nb)
    steps = len(order)
    ahead = min(3, steps)
    near = [choose(a, [table[p][i] for p in range(na)]) for i in range(na)]
    sib = dict(pos, C=1 - c)

    def there(i, t, own_plane=True):
        return dict(pos, A=near[i], B=lax.rem(pos["B"] + t, nb), C=c if own_plane else 1 - c)

    barrier = pltpu.get_barrier_semaphore()
    for s in range(1, n_exp):
        pl.semaphore_signal(barrier, inc=1, device_id=(pos["Y"], lax.rem(me + s, n_exp)), device_id_type=MESH)
    pl.semaphore_wait(barrier, n_exp - 1)

    def rank_copy(s):
        j = lax.rem(me + s, n_exp)
        return pltpu.make_async_remote_copy(
            src_ref=rank_own.at[j], dst_ref=rank_ref.at[me], send_sem=r_send.at[j], recv_sem=r_recv.at[me],
            device_id=(pos["Y"], j), device_id_type=MESH)

    def rank_start(s, carry):
        rank_copy(s).start()
        return carry

    def rank_landed(j):
        pltpu.make_async_copy(rank_ref.at[j], rank_ref.at[j], r_recv.at[j]).wait()

    rank_ref[me] = rank_own[me]

    counter = [0]
    ag_sends = []

    def ag(conds, src, j, to):
        at = counter[0]
        counter[0] += 1

        def copy():
            return pltpu.make_async_remote_copy(
                src_ref=src(), dst_ref=xall.at[j()], send_sem=ag_send.at[at], recv_sem=ag_recv.at[j()],
                device_id=place.device(to()), device_id_type=MESH)

        ag_sends.append((conds, copy))
        under(conds(), lambda: copy().start())

    def landed(j):
        pltpu.make_async_copy(xall.at[j], xall.at[j], ag_recv.at[j]).wait()

    def own_block():
        return x_ref

    def always():
        return []

    for way in (1, -1):
        ag(lambda way=way: [place.inside(way)], own_block, lambda: me, lambda way=way: place.moved(A=way))
    for t in range(1, nb):
        ag(always, own_block, lambda: me, lambda t=t: place.moved(B=t))
    ag(always, own_block, lambda: me, lambda: sib)

    def line_arrival(i):
        def j():
            return place.expert(there(i, 0))

        def src():
            return xall.at[j()]

        landed(j())
        ag(lambda: [near[i] < a, place.inside(1)], src, j, lambda: place.moved(A=1))
        ag(lambda: [near[i] > a, place.inside(-1)], src, j, lambda: place.moved(A=-1))
        for t in range(1, nb):
            ag(always, src, j, lambda t=t: place.moved(B=t))
        ag(always, src, j, lambda: sib)

    def side_arrival(i):
        for t in range(1, nb):
            def j(t=t):
                return place.expert(there(i, t))

            landed(j())
            ag(always, lambda j=j: xall.at[j()], j, lambda: sib)

    lax.fori_loop(1, n_exp, rank_start, 0)

    before = {k: [] for k in range(steps)}
    for i in range(1, na):
        first = min(k for k, (q, _) in enumerate(order) if q == i)
        before[min(first, i)].append(lambda i=i: line_arrival(i))
    for i in range(na):
        first = min(k for k, (q, t) in enumerate(order) if q == i and t)
        before[min(first, i + 1)].append(lambda i=i: side_arrival(i))

    moves = [(wrt_h, wrt), (wshin_h, wshin), (wshdown_h, wshdown)]
    for pieces, whole in ((win_h, win), (wdown_h, wdown)):
        for n, piece in enumerate(pieces):
            rows = piece.shape[0]
            start = lax.rem(pos["Y"] + n, len(pieces)) * rows
            moves.append((piece, whole.at[pl.ds(pl.multiple_of(start, 16), rows)]))
    wloads = [pltpu.make_async_copy(h, v, w_sem.at[i]) for i, (h, v) in enumerate(moves)]
    for load in wloads:
        load.start()

    def pair_index(k):
        i = choose(k, [q for q, _ in order])
        t = choose(k, [q for _, q in order])
        p = dict(pos, A=choose(i, near), B=lax.rem(pos["B"] + t, nb))
        return place.expert(p), place.expert(dict(p, C=1 - c))

    def cot_load(k, slot):
        one, two = pair_index(k)
        return [pltpu.make_async_copy(cot_ref.at[j], cv.at[slot, n, :, pl.ds(0, given)], c_sem.at[slot, n])
                for n, j in enumerate((one, two))]

    def x_load(src, n, slot):
        loads = [pltpu.make_async_copy(src.at[:, pl.ds(0, d)], xv.at[n], x_sem.at[n, 0])]
        if given < d:
            loads.append(pltpu.make_async_copy(
                src.at[:, pl.ds(d, d - given)], cv.at[slot, n, :, pl.ds(given, d - given)], x_sem.at[n, 1]))
        return loads

    for load in cot_load(0, 0):
        load.start()
    gin_acc[...] = jnp.zeros_like(gin_acc)
    gdown_acc[...] = jnp.zeros_like(gdown_acc)
    gshin[...] = jnp.zeros_like(gshin)
    gshdown[...] = jnp.zeros_like(gshdown)
    for load in wloads:
        load.wait()

    def core_copy(k):
        return pltpu.make_async_remote_copy(
            src_ref=back_s.at[k % 2, 1], dst_ref=core_land.at[k], send_sem=core_send.at[k], recv_sem=core_recv.at[k],
            device_id=place.device(sib), device_id_type=MESH)

    b_steps = [k for k, (_, t) in enumerate(order) if t]

    def b_copy(k):
        i, t = order[k]
        n = b_steps.index(k)
        return pltpu.make_async_remote_copy(
            src_ref=bsrc.at[n % 2], dst_ref=b_land.at[i * (nb - 1) + t - 1], send_sem=b_send.at[n],
            recv_sem=b_recv.at[i * (nb - 1) + t - 1], device_id=place.device(place.moved(B=t)), device_id_type=MESH)

    def a_copy(i):
        return pltpu.make_async_remote_copy(
            src_ref=held.at[i], dst_ref=a_land.at[a], send_sem=a_send.at[i], recv_sem=a_recv.at[a],
            device_id=place.device(dict(pos, A=near[i])), device_id_type=MESH)

    def fetch(ref, sem, n):
        pltpu.make_async_copy(ref, ref, sem).wait()
        pltpu.make_async_copy(ref, stage.at[n], s_sem.at[n]).start()

    def fetched(n):
        pltpu.make_async_copy(stage.at[n], stage.at[n], s_sem.at[n]).wait()
        return stage[n].astype(wide)

    def core_fetch(k):
        fetch(core_land.at[k], core_recv.at[k], 0)

    def side_fetch(i):
        for t in range(1, nb):
            fetch(b_land.at[i * (nb - 1) + t - 1], b_recv.at[i * (nb - 1) + t - 1], t)

    def chip_sum(k):
        i, t = order[k]
        value = (back_s[k % 2, 0].astype(wide) + fetched(0)).astype(low)
        if t:
            n = b_steps.index(k)
            if n >= 2:
                b_copy(b_steps[n - 2]).wait_send()
            bsrc[n % 2] = value
            b_copy(k).start()
        else:
            held[i] = value

    def side_sum(i):
        value = held[i].astype(wide)
        for t in range(1, nb):
            value = value + fetched(t)
        held[i] = value.astype(low)
        if i:
            a_copy(i).start()

    early = {k: [] for k in range(steps)}
    middle = {k: [] for k in range(steps)}
    after = {k: [] for k in range(steps)}
    late = []
    for k in range(steps):
        if k + 1 < steps:
            early[k + 1].append(lambda k=k: core_fetch(k))
            middle[k + 1].append(lambda k=k: chip_sum(k))
        else:
            late.append(lambda k=k: core_fetch(k))
            late.append(lambda k=k: chip_sum(k))
    for i in list(range(2, na)) + [1, 0]:
        sent = max([k for k, (q, t) in enumerate(order) if q == i and t], default=0)
        ready = max(2 * (sent + 1) + 3, 2 * (order.index((i, 0)) + 1) + 1)
        fetching, adding = (lambda i=i: side_fetch(i)), (lambda i=i: side_sum(i))
        if ready // 2 >= steps:
            late += [fetching, adding]
        elif ready % 2:
            after[ready // 2] += [fetching, adding]
        else:
            early[ready // 2].append(fetching)
            middle[ready // 2].append(adding)

    def at(k, events):
        for n in range(steps):
            if events.get(n):
                @pl.when(k == n)
                def _(n=n):
                    for run in events[n]:
                        run()

    def gg_copy(k, n, to):
        return pltpu.make_async_remote_copy(
            src_ref=gg_s.at[k, n], dst_ref=gg_out.at[me], send_sem=g_send.at[k, n], recv_sem=g_recv.at[me],
            device_id=(pos["Y"], to), device_id_type=MESH)

    def mixed_copy(slot, n, j):
        return pltpu.make_async_copy(mixed_s.at[slot, n], mixed.at[j], m_sem.at[slot, n])

    def step(k, carry):
        slot = lax.rem(k, 2)
        one, two = pair_index(k)
        @pl.when(k < ahead)
        def _():
            at(k, {q: before[q] if q < ahead else [] for q in range(steps)})

            @pl.when(k == 0)
            def _():
                for load in x_load(x_ref, 0, slot):
                    load.start()

            @pl.when(k > 0)
            def _():
                for load in x_load(xall.at[one], 0, slot):
                    load.start()
                rank_landed(one)

            landed(two)
            for load in x_load(xall.at[two], 1, slot):
                load.start()
            rank_landed(two)

        for n, j in enumerate((one, two)):
            for load in x_load(xall.at[j], n, slot):
                load.wait()
        for load in cot_load(k, slot):
            load.wait()

        @pl.when(k + 1 < steps)
        def _():
            for load in cot_load(k + 1, 1 - slot):
                load.start()

        ranks = (rank_ref[one], rank_ref[two])
        slots = lax.broadcasted_iota(jnp.int32, (cap, toks), 0).astype(wide)
        picks = [r == slots for r in ranks]
        crs = []
        for n in range(2):
            p = picks[n].astype(low)
            xr_s[n * cap:(n + 1) * cap, :] = mm(p, xv[n]).astype(low)
            crs.append(mm(p, cv[slot, n]).astype(low))
        cr = jnp.concatenate(crs, axis=0)
        at(k, early)
        gu = mm(xr_s[...], win[...])
        logits = mm(xr_s[...], wrt[...])
        lane = lax.broadcasted_iota(jnp.int32, logits.shape, 1)
        logits = jnp.where(lane < experts, logits, -1e30)
        ex = jnp.exp(logits - jnp.max(logits, axis=1, keepdims=True))
        gate = jnp.sum(jnp.where(lane == me, ex, 0.0), axis=1, keepdims=True) / jnp.sum(ex, axis=1, keepdims=True)
        g = gu[:, :FF]
        u = gu[:, FF:2 * FF]
        s = sig(g)
        sg = g * s
        act_s[...] = (sg * u).astype(low)
        gr_s[...] = (gate * cr.astype(wide)).astype(low)
        dact = mm_nt(gr_s[...], wdown[...])
        dgu_s[:, :FF] = (dact * u * (s + sg * (1.0 - s))).astype(low)
        dgu_s[:, FF:] = (dact * sg).astype(low)
        o = mm(act_s[...], wdown[...]).astype(low)
        of = o.astype(wide)
        gg = jnp.sum(cr.astype(wide) * of, axis=1, keepdims=True)
        wtd = (gate * of).astype(low)
        ib = mm_nt(dgu_s[...], win[...]).astype(low)
        at(k, middle)

        @pl.when(k >= 2)
        def _():
            for n, j in enumerate((one, two)):
                mixed_copy(slot, n, j).wait()

        for n in range(2):
            x = xv[n]
            ct = cv[slot, n]
            sh = mm(x, wshin[...])
            g2 = sh[:, :hid]
            u2 = sh[:, hid:]
            s2 = sig(g2)
            sg2 = g2 * s2
            sact = (sg2 * u2).astype(low)
            dsact = mm_nt(ct, wshdown[...])
            dsh = jnp.concatenate([dsact * u2 * (s2 + sg2 * (1.0 - s2)), dsact * sg2], axis=1).astype(low)
            p = picks[n].astype(low)
            rows = slice(n * cap, (n + 1) * cap)
            mixed_s[slot, n] = (mm_tn(p, wtd[rows]) + mm(sact, wshdown[...])).astype(low)
            back_s[slot, n] = (mm_tn(p, ib[rows]) + mm_nt(dsh, wshin[...])).astype(low)
            gg_s[k, n] = jnp.sum(jnp.where(picks[n], gg[rows], 0.0), axis=0, keepdims=True)
            gshdown[...] += mm_tn(sact, ct)
            gshin[...] += mm_tn(x, dsh)
        for n, j in enumerate((one, two)):
            mixed_copy(slot, n, j).start()
        at(k, {q: [lambda q=q: core_copy(q).start()] for q in range(steps)})

        @pl.when(k > 0)
        def _():
            gg_copy(k, 0, one).start()

        gg_copy(k, 1, two).start()
        at(k, after)

        @pl.when((k + 1 >= ahead) & (k + 1 < steps))
        def _():
            at(k, {q - 1: before[q] for q in range(ahead, steps)})
            next_one, next_two = pair_index(k + 1)
            for load in x_load(xall.at[next_one], 0, 1 - slot):
                load.start()
            landed(next_two)
            for load in x_load(xall.at[next_two], 1, 1 - slot):
                load.start()
            rank_landed(next_one)
            rank_landed(next_two)

        gdown_acc[...] += mm_tn(act_s[...], gr_s[...])
        gin_acc[...] += mm_tn(xr_s[...], dgu_s[...])
        at(k, {q: [lambda q=q: core_copy(q - 1).wait_send()] if q else [] for q in range(steps)})
        return carry

    lax.fori_loop(0, steps, step, 0)
    gg_out[me] = gg_s[0, 0]
    win[...] = gin_acc[...].astype(low)
    wdown[...] = gdown_acc[...].astype(low)
    outs = []
    for pieces, whole in ((gin_out, win), (gdown_out, wdown)):
        for n, piece in enumerate(pieces):
            rows = piece.shape[0]
            start = lax.rem(pos["Y"] + n, len(pieces)) * rows
            outs.append(pltpu.make_async_copy(
                whole.at[pl.ds(pl.multiple_of(start, 16), rows)], piece, w_sem.at[len(outs)]))
    for out in outs:
        out.start()
    for run in late:
        run()
    total = held[0].astype(wide)
    for s in range(1, na):
        j = lax.rem(a + s, na)
        fetch(a_land.at[j], a_recv.at[j], 0)
        total = total + fetched(0)
    gin_acc[:toks, :d] = total
    last = pltpu.make_async_copy(gin_acc.at[pl.ds(0, toks), pl.ds(0, d)], total_out, s_sem.at[0])
    last.start()
    last.wait()
    for out in outs:
        out.wait()
    core_copy(steps - 1).wait_send()
    for k in b_steps[-2:]:
        b_copy(k).wait_send()
    for i in range(1, na):
        a_copy(i).wait_send()
    for conds, copy in ag_sends:
        under(conds(), lambda copy=copy: copy().wait_send())
    for k in (steps - 2, steps - 1):
        one, two = pair_index(k)
        for n, j in enumerate((one, two)):
            mixed_copy(k % 2, n, j).wait()

    def gg_done(k, carry):
        one, two = pair_index(k)

        @pl.when(k > 0)
        def _():
            gg_copy(k, 0, one).wait_send()

        gg_copy(k, 1, two).wait_send()
        return carry

    lax.fori_loop(0, steps, gg_done, 0)

    def gg_wait(s, carry):
        j = lax.rem(me + s, n_exp)
        pltpu.make_async_copy(gg_out.at[j], gg_out.at[j], g_recv.at[j]).wait()
        return carry

    lax.fori_loop(1, n_exp, gg_wait, 0)

    def rank_sent(s, carry):
        rank_copy(s).wait_send()
        return carry

    lax.fori_loop(1, n_exp, rank_sent, 0)


def fused(x, cot_all, rank, win, wdown, wrt, wshin, wshdown, n_dp, n_exp, experts, cap, cid):
    toks, d = x.shape[0], wshdown.shape[1]
    size = sizes(n_dp, n_exp)
    na, nb = size["A"], size["B"]
    steps = na * nb
    hid = wshdown.shape[0]
    low, wide = jnp.bfloat16, jnp.float32
    hbm = pl.BlockSpec(memory_space=pl.ANY)
    vmem = pl.BlockSpec(memory_space=pltpu.VMEM)
    rows = 2 * cap
    block = (toks, d)
    dma = pltpu.SemaphoreType.DMA
    ag_count = 2 + (nb - 1) + 1 + (na - 1) * (2 + nb) + na * (nb - 1)
    flops = 2 * n_exp * (cap * d * FF * 9 + toks * cap * d * 4 + toks * d * hid * 9)
    out = pl.pallas_call(
        functools.partial(fused_kernel, n_dp, n_exp, experts, cap, len(win)),
        in_specs=[hbm, hbm, vmem] + [hbm] * (2 * len(win) + 3),
        out_shape=[
            jax.ShapeDtypeStruct((n_exp,) + x.shape, low),
            jax.ShapeDtypeStruct((n_exp,) + block, low),
            jax.ShapeDtypeStruct(block, wide),
            jax.ShapeDtypeStruct((n_exp, 1, toks), wide),
            *[jax.ShapeDtypeStruct(w.shape, low) for w in (*win, *wdown)],
            jax.ShapeDtypeStruct((d, 2 * hid), wide),
            jax.ShapeDtypeStruct((hid, d), wide),
            jax.ShapeDtypeStruct((steps,) + block, low),
            jax.ShapeDtypeStruct((na * max(nb - 1, 1),) + block, low),
            jax.ShapeDtypeStruct((na,) + block, low),
        ],
        out_specs=[hbm, hbm, hbm, vmem] + [hbm] * (2 * len(win)) + [vmem, vmem, hbm, hbm, hbm],
        scratch_shapes=[
            pltpu.VMEM((d, 2 * FF), low), pltpu.VMEM((FF, d), low), pltpu.VMEM(wrt.shape, low),
            pltpu.VMEM(wshin.shape, low), pltpu.VMEM(wshdown.shape, low), pltpu.VMEM((n_exp, 1, toks), wide),
            pltpu.VMEM((2,) + block, low), pltpu.VMEM((2, 2) + block, low),
            pltpu.VMEM((rows, d), low), pltpu.VMEM((rows, FF), low), pltpu.VMEM((rows, d), low),
            pltpu.VMEM((rows, 2 * FF), low),
            pltpu.VMEM((2, 2) + block, low), pltpu.VMEM((2, 2) + block, low), pltpu.VMEM((na,) + block, low),
            pltpu.VMEM((2,) + block, low), pltpu.VMEM((nb,) + block, low),
            pltpu.VMEM((steps, 2, 1, toks), wide), pltpu.VMEM((d, 2 * FF), wide), pltpu.VMEM((FF, d), wide),
            dma((3 + 2 * len(win),)), dma((2, 2)), dma((2, 2)), dma((2, 2)), dma((nb,)),
            dma((ag_count,)), dma((n_exp,)), dma((steps,)), dma((steps,)),
            dma((na * max(nb - 1, 1),)), dma((na * max(nb - 1, 1),)), dma((na,)), dma((na,)),
            dma((steps, 2)), dma((n_exp,)), dma((n_exp,)), dma((n_exp,)),
        ],
        compiler_params=pltpu.CompilerParams(collective_id=cid, has_side_effects=True, vmem_limit_bytes=63 * 1024 * 1024),
        cost_estimate=pl.CostEstimate(flops=flops, bytes_accessed=100 * 1024 * 1024, transcendentals=0),
        name="experts_fused",
    )(x, cot_all, rank, *win, *wdown, wrt, wshin, wshdown)
    n = len(win)
    return out[1], out[2], out[3], out[4:4 + n], out[4 + n:4 + 2 * n], out[4 + 2 * n], out[5 + 2 * n]


def swap_rows(x, n_dp):
    if n_dp != 2:
        return [lax.all_gather(x, "dp", axis=0, tiled=True)]
    return [x, lax.ppermute(x, "dp", [(0, 1), (1, 0)])]


def in_order(pieces):
    if len(pieces) == 1:
        return pieces[0]
    first = lax.axis_index("dp") == 0
    x, other = pieces
    return jnp.concatenate([jnp.where(first, x, other), jnp.where(first, other, x)], axis=0)


def halve_rows(pieces, n_dp):
    if n_dp != 2:
        return lax.psum_scatter(pieces[0], "dp", scatter_dimension=0, tiled=True).astype(jnp.float32)
    other = lax.ppermute(pieces[1], "dp", [(0, 1), (1, 0)])
    return pieces[0].astype(jnp.float32) + other.astype(jnp.float32)


def split_rows(x, n_dp):
    if n_dp != 2:
        return [x]
    rows = x.shape[0] // 2
    top, bottom = x[:rows], x[rows:]
    first = lax.axis_index("dp") == 0
    return [jnp.where(first, top, bottom), jnp.where(first, bottom, top)]


def local(
    tokens,
    lengths,
    routes,
    cotangent,
    norm_gains,
    gains_m,
    gains_v,
    w_qkv,
    m_qkv,
    v_qkv,
    w_out,
    m_out,
    v_out,
    w_shared_in,
    m_shared_in,
    v_shared_in,
    w_shared_down,
    m_shared_down,
    v_shared_down,
    w_router,
    m_router,
    v_router,
    w_expert_in,
    m_expert_in,
    v_expert_in,
    w_expert_down,
    m_expert_down,
    v_expert_down,
):
    both = ("dp", "expert")
    low = jnp.bfloat16
    wide = jnp.float32
    row_count = tokens.shape[0]
    expert_count = w_router.shape[1]
    n_dp = lax.axis_size("dp")
    n_exp = lax.axis_size("expert")
    n_all = n_dp * n_exp
    capacity = min(row_count, (5 * row_count * TOP // (4 * expert_count) + 7) // 8 * 8)
    score_scale = HD ** (-0.5)
    rows_w = w_qkv.shape[0]
    unit = w_shared_down.shape[0]

    pad = jnp.zeros((rows_w, 128 - expert_count - 2), wide)
    packed = jnp.concatenate([w_qkv, w_out, w_router, norm_gains.T, pad], axis=1).astype(low)
    full = gather(packed, n_dp, n_exp, True, 1).reshape(D, -1)
    full, ein_low = lax.optimization_barrier((full, w_expert_in[0].astype(low)))
    expert_in_full = swap_rows(ein_low, n_dp)
    qkv_full = full[:, : 3 * H * HD]
    out_full = full[:, 3 * H * HD : 3 * H * HD + D]
    small_full = full[:, 3 * H * HD + D :]
    router_full = small_full[:, :expert_count]
    gain_one = small_full[:, expert_count].astype(wide)
    gain_two = small_full[:, expert_count + 1].astype(wide)
    cot_all = lax.all_gather(cotangent[:, :GIVEN], "expert", axis=0, tiled=False)
    expert_down_full = swap_rows(w_expert_down[0].astype(low), n_dp)
    shin_send = (
        w_shared_in.astype(low)
        .reshape(rows_w, 2, n_dp, n_exp, unit)
        .transpose(3, 0, 1, 2, 4)
        .reshape(n_exp, rows_w, 2 * n_dp * unit)
    )
    shin_send = jnp.concatenate([shin_send] * n_dp, axis=0)
    shin_mine = lax.all_to_all(shin_send, both, 0, 0, tiled=True).reshape(D, 2 * n_dp * unit)
    shdown_mine = in_order(swap_rows(w_shared_down.astype(low), n_dp))
    half = n_dp * unit

    inputs = tokens.astype(wide)
    cosine, sine_table, allowed = rotary_tables(lengths[0], row_count, HD)
    scale_one = rms_scale(inputs)
    normed_one = inputs * scale_one
    attn_in = (normed_one * gain_one).astype(low)
    projected = jnp.dot(attn_in, qkv_full, preferred_element_type=wide).reshape(
        row_count, 3, H, HD
    )
    queries = rotate(projected[:, 0], cosine, sine_table).astype(low)
    keys_rot = rotate(projected[:, 1], cosine, sine_table).astype(low)
    values_low = projected[:, 2].astype(low)
    raw_scores = (
        jnp.einsum("qhd,khd->hqk", queries, keys_rot, preferred_element_type=wide) * score_scale
    )
    scores = jnp.where(allowed[None], raw_scores, NEGATIVE)
    row_max = jnp.max(scores, axis=-1, keepdims=True)
    exped = jnp.exp(scores - row_max)
    probs_attn = exped / jnp.sum(exped, axis=-1, keepdims=True)
    probs_low = probs_attn.astype(low)
    mixed_heads = jnp.einsum("hqk,khd->qhd", probs_low, values_low, preferred_element_type=wide)
    heads_low = mixed_heads.astype(low).reshape(row_count, H * HD)
    residual = inputs + jnp.dot(heads_low, out_full, preferred_element_type=wide)
    scale_two = rms_scale(residual)
    normed_two = residual * scale_two
    mlp_in = (normed_two * gain_two).astype(low)
    logits = jnp.dot(mlp_in, router_full, preferred_element_type=wide)
    router_probs = jax.nn.softmax(logits, axis=-1)

    routed = jnp.any(routes[:, :, None] == jnp.arange(expert_count, dtype=jnp.int32), axis=1)
    rank = jnp.where(routed, jnp.cumsum(routed.astype(jnp.int32), axis=0) - 1, -1).astype(wide).T
    hid = (half + 127) // 128 * 128
    cap = (capacity + 15) // 16 * 16
    wrt = jnp.concatenate([router_full, jnp.zeros((D, 128 - expert_count), low)], axis=1)
    gap = jnp.zeros((D, hid - half), low)
    wshin = jnp.concatenate([shin_mine[:, :half], gap, shin_mine[:, half:], gap], axis=1)
    wshdown = jnp.concatenate([shdown_mine, jnp.zeros((hid - half, D), low)], axis=0)
    mixed_part, back_sum, gate_grad, grad_ein, grad_edown, shin_wide, shdown_wide = fused(
        jnp.concatenate([mlp_in, cotangent[:, GIVEN:]], axis=1), cot_all, rank[:, None, :], expert_in_full, expert_down_full, wrt, wshin, wshdown, n_dp, n_exp, expert_count, cap, 2
    )
    mixed_sum = lax.psum_scatter(mixed_part, "expert", scatter_dimension=0, tiled=False)
    grad_shin = jnp.concatenate([shin_wide[:, :half], shin_wide[:, hid : hid + half]], axis=1)
    grad_shdown = shdown_wide[:half]
    prob_grad = gate_grad[:, 0, :].T
    logit_grad = (
        router_probs * (prob_grad - jnp.sum(prob_grad * router_probs, axis=-1, keepdims=True))
    ).astype(low)
    grad_router = jnp.einsum("td,te->de", mlp_in, logit_grad, preferred_element_type=wide)
    mlp_in_grad = back_sum + jnp.einsum(
        "te,de->td", logit_grad, router_full, preferred_element_type=wide
    )
    out_grad = cotangent.astype(wide)
    grad_gain_two = jnp.sum(mlp_in_grad * normed_two, axis=0)
    scaled_two = mlp_in_grad * gain_two
    resid_grad = out_grad + scale_two * (
        scaled_two - normed_two * jnp.mean(scaled_two * normed_two, axis=-1, keepdims=True)
    )
    resid_low = resid_grad.astype(low)
    grad_out = jnp.einsum("ti,td->id", heads_low, resid_low, preferred_element_type=wide)
    heads_grad = jnp.einsum("td,id->ti", resid_low, out_full, preferred_element_type=wide)
    heads_grad = heads_grad.astype(low).reshape(row_count, H, HD)
    attn_prob_grad = jnp.einsum("qhd,khd->hqk", heads_grad, values_low, preferred_element_type=wide)
    value_grad = jnp.einsum("hqk,qhd->khd", probs_low, heads_grad, preferred_element_type=wide)
    score_grad = probs_attn * (
        attn_prob_grad - jnp.sum(attn_prob_grad * probs_attn, axis=-1, keepdims=True)
    )
    score_grad = score_grad.astype(low)
    query_grad = (
        jnp.einsum("hqk,khd->qhd", score_grad, keys_rot, preferred_element_type=wide) * score_scale
    )
    key_grad = (
        jnp.einsum("hqk,qhd->khd", score_grad, queries, preferred_element_type=wide) * score_scale
    )
    projected_grad = jnp.stack(
        [
            rotate_back(query_grad, cosine, sine_table),
            rotate_back(key_grad, cosine, sine_table),
            value_grad,
        ],
        axis=1,
    )
    projected_grad = projected_grad.reshape(row_count, 3 * H * HD).astype(low)
    grad_qkv = jnp.einsum("td,tk->dk", attn_in, projected_grad, preferred_element_type=wide)
    attn_grad = jnp.einsum("tk,dk->td", projected_grad, qkv_full, preferred_element_type=wide)
    grad_gain_one = jnp.sum(attn_grad * normed_one, axis=0)
    scaled_one = attn_grad * gain_one
    input_grad = resid_grad + scale_one * (
        scaled_one - normed_one * jnp.mean(scaled_one * normed_one, axis=-1, keepdims=True)
    )

    small_grad = jnp.concatenate(
        [grad_router, grad_gain_one[:, None], grad_gain_two[:, None], jnp.zeros((D, 128 - expert_count - 2), wide)],
        axis=1,
    )
    shin_back = lax.all_to_all(
        grad_shin.astype(low).reshape(n_all, rows_w, 2 * half), both, 0, 0, tiled=True
    )
    shin_own = jnp.sum(
        shin_back.reshape(n_dp, n_exp, rows_w, 2, n_dp, unit).astype(wide), axis=0
    )
    shin_own = shin_own.transpose(1, 2, 3, 0, 4).reshape(rows_w, 2 * FF)
    shdown_own = halve_rows(split_rows(grad_shdown, n_dp), n_dp)
    ein_own = halve_rows(grad_ein, n_dp)
    edown_own = halve_rows(grad_edown, n_dp)
    squares = sum(jnp.sum(g * g) for g in (shin_own, shdown_own, ein_own, edown_own))
    qkv_own, out_own, small_own, norm = reduce_dense(
        [g.astype(low).reshape(n_all, rows_w, -1) for g in (grad_qkv, grad_out, small_grad)], squares, n_dp, n_exp, 5
    )
    qkv_own, mixed_sum = lax.optimization_barrier((qkv_own, mixed_sum))
    mixed = (residual + mixed_sum.astype(wide)).astype(low)
    owned_grads = (
        small_own[:, expert_count : expert_count + 2].T,
        qkv_own,
        out_own,
        shin_own,
        shdown_own,
        small_own[:, :expert_count],
        ein_own[None],
        edown_own[None],
    )
    total_squares = norm[0, 0]
    grad_norm = jnp.sqrt(total_squares)
    factor = jnp.minimum(1.0, CLIP / grad_norm)
    weights = (
        norm_gains,
        w_qkv,
        w_out,
        w_shared_in,
        w_shared_down,
        w_router,
        w_expert_in,
        w_expert_down,
    )
    firsts = (
        gains_m,
        m_qkv,
        m_out,
        m_shared_in,
        m_shared_down,
        m_router,
        m_expert_in,
        m_expert_down,
    )
    seconds = (
        gains_v,
        v_qkv,
        v_out,
        v_shared_in,
        v_shared_down,
        v_router,
        v_expert_in,
        v_expert_down,
    )
    rates = (
        GAIN_RATE,
        D ** (-0.5),
        (H * HD // 64) ** (-0.5),
        D ** (-0.5),
        FF ** (-0.5),
        (4 * D) ** (-0.5),
        D ** (-0.5),
        (FF // 64) ** (-0.5),
    )
    decays = (0.0, DECAY, DECAY, DECAY, DECAY, DECAY, DECAY, DECAY)
    updated = []
    for weight, first_moment, second_moment, gradient, step_rate, decay_rate in zip(
        weights, firsts, seconds, owned_grads, rates, decays
    ):
        updated.extend(
            adam_update(
                weight, first_moment, second_moment, gradient, factor, step_rate, decay_rate
            )
        )
    return (
        mixed,
        input_grad,
        updated[0],
        updated[1],
        updated[2],
        updated[3],
        updated[4],
        updated[5],
        updated[6],
        updated[7],
        updated[8],
        updated[9],
        updated[10],
        updated[11],
        updated[12],
        updated[13],
        updated[14],
        updated[15],
        updated[16],
        updated[17],
        updated[18],
        updated[19],
        updated[20],
        updated[21],
        updated[22],
        updated[23],
        grad_norm,
    )


def solution(mesh):
    placed = (
        P(("dp", "expert"), None),
        P(("dp", "expert"), None),
        P(("dp", "expert"), None),
        P(("dp", "expert"), None),
        P(None, ("dp", "expert")),
        P(None, ("dp", "expert")),
        P(None, ("dp", "expert")),
        P(("dp", "expert"), None),
        P(("dp", "expert"), None),
        P(("dp", "expert"), None),
        P(("dp", "expert"), None),
        P(("dp", "expert"), None),
        P(("dp", "expert"), None),
        P(("dp", "expert"), None),
        P(("dp", "expert"), None),
        P(("dp", "expert"), None),
        P(("dp", "expert"), None),
        P(("dp", "expert"), None),
        P(("dp", "expert"), None),
        P(("dp", "expert"), None),
        P(("dp", "expert"), None),
        P(("dp", "expert"), None),
        P("expert", "dp", None),
        P("expert", "dp", None),
        P("expert", "dp", None),
        P("expert", "dp", None),
        P("expert", "dp", None),
        P("expert", "dp", None),
    )
    return jax.shard_map(
        local,
        mesh=mesh,
        in_specs=placed,
        out_specs=(
            P(("dp", "expert"), None),
            P(("dp", "expert"), None),
            P(None, ("dp", "expert")),
            P(None, ("dp", "expert")),
            P(None, ("dp", "expert")),
            P(("dp", "expert"), None),
            P(("dp", "expert"), None),
            P(("dp", "expert"), None),
            P(("dp", "expert"), None),
            P(("dp", "expert"), None),
            P(("dp", "expert"), None),
            P(("dp", "expert"), None),
            P(("dp", "expert"), None),
            P(("dp", "expert"), None),
            P(("dp", "expert"), None),
            P(("dp", "expert"), None),
            P(("dp", "expert"), None),
            P(("dp", "expert"), None),
            P(("dp", "expert"), None),
            P(("dp", "expert"), None),
            P("expert", "dp", None),
            P("expert", "dp", None),
            P("expert", "dp", None),
            P("expert", "dp", None),
            P("expert", "dp", None),
            P("expert", "dp", None),
            P(),
        ),
        check_vma=False,
    )
```

```python
import functools
import itertools

import jax
import jax.numpy as jnp
from jax import lax
from jax.experimental import pallas as pl
from jax.experimental.pallas import tpu as pltpu
from jax.sharding import PartitionSpec as P

D = 1280
H = 10
HD = 128
FF = 896
TOP = 6
ADAM_STEP = 5
MIXED_FIRST = 896
GIVEN = 1280


EPS = 1e-06
ROPE_BASE = 10000.0
BETA_ONE = 0.9
BETA_TWO = 0.95
ADAM_EPS = 1e-08
DECAY = 0.1
CLIP = 1.0
GAIN_RATE = 0.5
NEGATIVE = -1e30


def rms_scale(values):
    return lax.rsqrt(jnp.mean(values * values, axis=-1, keepdims=True) + EPS)


def rotary_tables(seq_lengths, row_count, head_width):
    position = jnp.arange(row_count, dtype=jnp.int32)
    seq_ends = jnp.cumsum(seq_lengths)
    segment = jnp.sum((position[:, None] >= seq_ends[None, :]).astype(jnp.int32), axis=1)
    starts = seq_ends - seq_lengths
    slot_ids = jnp.arange(seq_lengths.shape[0], dtype=jnp.int32)
    first_row = jnp.sum(
        jnp.where(segment[:, None] == slot_ids[None, :], starts[None, :], 0), axis=1
    )
    seq_place = (position - first_row).astype(jnp.float32)
    inv_freq = ROPE_BASE ** (-jnp.arange(head_width // 2, dtype=jnp.float32) * 2.0 / head_width)
    phase_angle = seq_place[:, None] * inv_freq[None, :]
    cosine = jnp.concatenate([jnp.cos(phase_angle), jnp.cos(phase_angle)], axis=1)
    sine_table = jnp.concatenate([jnp.sin(phase_angle), jnp.sin(phase_angle)], axis=1)
    allowed = (segment[:, None] == segment[None, :]) & (position[None, :] <= position[:, None])
    return (cosine, sine_table, allowed)


def adam_update(weight, first_moment, second_moment, gradient, factor, step_rate, decay_rate):
    clipped = gradient * factor
    first_new = BETA_ONE * first_moment + (1.0 - BETA_ONE) * clipped
    second_new = BETA_TWO * second_moment + (1.0 - BETA_TWO) * clipped * clipped
    first_hat = first_new / (1.0 - BETA_ONE**ADAM_STEP)
    second_hat = second_new / (1.0 - BETA_TWO**ADAM_STEP)
    weight_new = weight - step_rate * (
        first_hat / (jnp.sqrt(second_hat) + ADAM_EPS) + decay_rate * weight
    )
    return (weight_new, first_new, second_new)


MESH = pl.DeviceIdType.MESH


PIECE = 64
CHUNK = 64
SHARE_BACK = 6


class Place:
    def __init__(self, n_dp, n_exp):
        rest = n_exp // 2
        na = 4 if rest % 4 == 0 else rest
        self.size = {"A": na, "B": rest // na, "C": 2, "Y": n_dp}
        e = lax.axis_index("expert")
        nb = self.size["B"]
        self.pos = {"A": e // (2 * nb), "B": (e // 2) % nb, "C": e % 2, "Y": lax.axis_index("dp")}

    def expert(self, pos):
        return (pos["A"] * self.size["B"] + pos["B"]) * 2 + pos["C"]

    def flat(self, pos):
        return pos["Y"] * (2 * self.size["A"] * self.size["B"]) + self.expert(pos)

    def device(self, pos):
        return (pos["Y"], self.expert(pos))

    def moved(self, **steps):
        pos = dict(self.pos)
        for axis, step in steps.items():
            if axis == "A":
                pos[axis] = pos[axis] + step
            else:
                pos[axis] = lax.rem(pos[axis] + step, self.size[axis])
        return pos

    def inside(self, step):
        there = self.pos["A"] + step
        return (there >= 0) & (there < self.size["A"])

    def greet(self, axes, line_all):
        barrier = pltpu.get_barrier_semaphore()
        total = 0
        for axis in axes:
            if axis == "A":
                reach = range(1, self.size["A"]) if line_all else (1,)
                for step in [s * d for d in reach for s in (1, -1)]:
                    near = self.inside(step)

                    @pl.when(near)
                    def _(step=step):
                        pl.semaphore_signal(barrier, inc=1, device_id=self.device(self.moved(A=step)), device_id_type=MESH)

                    total = total + jnp.where(near, 1, 0)
            else:
                for step in range(1, self.size[axis]):
                    pl.semaphore_signal(barrier, inc=1, device_id=self.device(self.moved(**{axis: step})), device_id_type=MESH)
                    total = total + 1
        pl.semaphore_wait(barrier, total)


def under(conds, body):
    if conds:
        both = conds[0]
        for c in conds[1:]:
            both = both & c
        pl.when(both)(body)
    else:
        body()


PACE = {"A": 4, "B": 5, "Y": 5, "C": 1}


def plan_gather(size, orders):
    events = []
    for part, order in enumerate(orders):
        spans = []
        for axis in order:
            n = size[axis]
            spans.append(range(1 - n, n) if axis == "A" else range(n))
        for offs in itertools.product(*spans):
            when = 0
            for axis, o in zip(order, offs):
                when += PACE[axis] * (abs(o) if axis == "A" else (1 if o else 0))
            events.append((when, part, offs))
    events.sort(key=lambda ev: ev[0])
    return events


def gather_body(place, orders, slices, own_ref, out_ref, block_of, send_sem, recv_sem, fill=()):
    size = place.size
    sends = []
    count = [0]

    def send(conds, part, src_block, src, to):
        slot = count[0]
        count[0] += 1
        lo, n = slices[part]

        def copy():
            j = src_block()
            return pltpu.make_async_remote_copy(
                src_ref=(own_ref if src is None else out_ref.at[j]).at[:, pl.ds(lo, n)],
                dst_ref=out_ref.at[j].at[:, pl.ds(lo, n)],
                send_sem=send_sem.at[slot],
                recv_sem=recv_sem.at[part, j],
                device_id=place.device(to()),
                device_id_type=MESH,
            )

        under(conds, lambda: copy().start())
        sends.append((conds, copy))

    fill = list(fill)
    plan = plan_gather(size, orders)
    every = max(1, len(plan) // (len(fill) + 1))
    for number, (_, part, offs) in enumerate(plan):
        if fill and number % every == every - 1:
            fill.pop(0)()
        order = orders[part]
        steps = dict(zip(order, offs))
        last = max([i for i, o in enumerate(offs) if o], default=-1)
        conds = []
        if steps["A"]:
            conds.append(place.inside(steps["A"]))

        def block(steps=steps):
            return block_of(place.moved(**{k: o for k, o in steps.items() if o}))

        if last >= 0:
            lo, n = slices[part]

            def wait(block=block, part=part, lo=lo, n=n):
                j = block()
                pltpu.make_async_copy(
                    out_ref.at[j].at[:, pl.ds(lo, n)], out_ref.at[j].at[:, pl.ds(lo, n)], recv_sem.at[part, j]
                ).wait()

            under(conds, wait)
        src = None if last < 0 else out_ref
        for i in range(max(last, 0), len(order)):
            axis = order[i]
            if axis == "A":
                ways = (1, -1) if i > last else ((1,) if steps["A"] < 0 else (-1,))
                for way in ways:
                    send(conds + [place.inside(way)], part, block, src, lambda way=way: place.moved(A=way))
            elif i > last:
                for t in range(1, size[axis]):
                    send(conds, part, block, src, lambda axis=axis, t=t: place.moved(**{axis: t}))
    for run in fill:
        run()
    for conds, copy in sends:
        under(conds, lambda copy=copy: copy().wait_send())


def count_gather(size, orders):
    total = 0
    for _, part, offs in plan_gather(size, orders):
        order = orders[part]
        last = max([i for i, o in enumerate(offs) if o], default=-1)
        for i in range(max(last, 0), len(order)):
            if order[i] == "A":
                total += 2 if i > last else 1
            elif i > last:
                total += size[order[i]] - 1
    return total


def sizes(n_dp, n_exp):
    rest = n_exp // 2
    na = 4 if rest % 4 == 0 else rest
    return {"A": na, "B": rest // na, "C": 2, "Y": n_dp}


def gather_kernel(n_dp, n_exp, orders, slices, dense, x_ref, pass_ref, out_ref, passed_ref, send_sem, recv_sem,
                  local_sem, pass_send, pass_recv):
    place = Place(n_dp, n_exp)

    def piece(n):
        rows = pl.ds(n * PIECE, PIECE)
        return pltpu.make_async_remote_copy(
            src_ref=pass_ref.at[rows], dst_ref=passed_ref.at[rows], send_sem=pass_send.at[n], recv_sem=pass_recv.at[n],
            device_id=place.device(place.moved(Y=1)), device_id_type=MESH)

    pieces = pass_ref.shape[0] // PIECE if n_dp == 2 else 0
    block_of = place.flat if dense else place.expert
    place.greet(orders[0], False)
    own = pltpu.make_async_copy(x_ref, out_ref.at[block_of(place.pos)], local_sem)
    own.start()
    gather_body(place, orders, slices, x_ref, out_ref, block_of, send_sem, recv_sem,
                [lambda n=n: piece(n).start() for n in range(pieces)])
    own.wait()
    for n in range(pieces):
        piece(n).wait()


def gather(x, passed, n_dp, n_exp, dense, cid, parts=None):
    size = sizes(n_dp, n_exp)
    rows, cols = x.shape
    if dense:
        orders = ("ABYC", "AYBC")
        half = cols // 256 * 128
        slices = ((0, half), (half, cols - half))
    else:
        orders = parts or ("ABC",)
        w = cols // len(orders)
        slices = tuple((i * w, w) for i in range(len(orders)))
    blocks = n_exp * (n_dp if dense else 1)
    return pl.pallas_call(
        functools.partial(gather_kernel, n_dp, n_exp, orders, slices, dense),
        out_shape=[
            jax.ShapeDtypeStruct((blocks, rows, cols), x.dtype), jax.ShapeDtypeStruct(passed.shape, passed.dtype)],
        in_specs=[pl.BlockSpec(memory_space=pl.ANY)] * 2,
        out_specs=[pl.BlockSpec(memory_space=pl.ANY)] * 2,
        scratch_shapes=[
            pltpu.SemaphoreType.DMA((count_gather(size, orders),)),
            pltpu.SemaphoreType.DMA((len(orders), blocks)),
            pltpu.SemaphoreType.DMA(()),
            pltpu.SemaphoreType.DMA((max(1, passed.shape[0] // PIECE),)),
            pltpu.SemaphoreType.DMA((max(1, passed.shape[0] // PIECE),)),
        ],
        compiler_params=pltpu.CompilerParams(collective_id=cid, has_side_effects=True),
        name="gather_dense" if dense else "gather_group",
    )(x, passed)


def line_order(n):
    out = []
    for i in range((n + 1) // 2):
        out.append(i)
        if n - 1 - i != i:
            out.append(n - 1 - i)
    return out


def stage_slots(size, order):
    slots = {}
    for i, axis in enumerate(order):
        rest = [line_order(size[x]) if x == "A" else range(size[x]) for x in order[i + 1:]]
        if axis == "A":
            for who in range(size["A"]):
                slots[(i, who, ())] = len(slots)
        else:
            for who in range(1, size[axis]):
                for r in itertools.product(*rest):
                    slots[(i, who, r)] = len(slots)
    return slots


def reduce_body(place, orders, slices, g_refs, block_of, land, base, send_sem, recv_sem, finish):
    size = place.size
    tables = [stage_slots(size, order) for order in orders]
    sends = []
    n = [0]

    def target(order, i, o, rest):
        pos = dict(place.pos)
        for axis, v in zip(order[i:], (o,) + tuple(rest)):
            if axis == "A":
                pos["A"] = v
            else:
                pos[axis] = lax.rem(pos[axis] + v, size[axis])
        return pos

    def send(conds, part, src, slot, to):
        at = n[0]
        n[0] += 1

        def copy():
            return pltpu.make_async_remote_copy(
                src_ref=src(), dst_ref=land[part].at[slot], send_sem=send_sem.at[at],
                recv_sem=recv_sem.at[base[part] + slot], device_id=place.device(to()), device_id_type=MESH)

        under(conds, lambda: copy().start())
        sends.append((conds, copy))

    def wait(part, slot):
        ref = land[part].at[slot]
        pltpu.make_async_copy(ref, ref, recv_sem.at[base[part] + slot]).wait()

    def rests(order, i):
        return list(itertools.product(*[line_order(size[x]) if x == "A" else range(size[x]) for x in order[i:]]))

    def far_first(items):
        return sorted(items, key=lambda r: tuple(0 if (isinstance(v, int) and v) else 1 for v in r[:-1]))

    for part, order in enumerate(orders):
        g_ref, lo, w = g_refs[slices[part][0]], slices[part][1], slices[part][2]
        axis = order[0]
        for t in range(1, size[axis]):
            for r in far_first(rests(order, 1)):
                def src(order=order, t=t, r=r, lo=lo, w=w, g_ref=g_ref):
                    return g_ref.at[block_of(target(order, 0, t, r)), :, pl.ds(lo, w)]
                send([], part, src, tables[part][(0, t, r)], lambda axis=axis, t=t: place.moved(**{axis: t}))
    for i in range(1, len(orders[0])):
        for pick in far_first(rests(orders[0], i)):
            for part, order in enumerate(orders):
                g_ref, lo, w = g_refs[slices[part][0]], slices[part][1], slices[part][2]
                axis = order[i]
                before = order[i - 1]
                r = pick
                got = [tables[part][(i - 1, t, r)] for t in range(1, size[before])]
                for slot in got:
                    wait(part, slot)
                if i == 1:
                    total = g_ref[block_of(target(order, 1, r[0], r[1:])), :, lo:lo + w].astype(jnp.float32)
                else:
                    total = land[part][tables[part][(i - 2, 1, (0,) + r)]].astype(jnp.float32)
                for slot in got:
                    total = total + land[part][slot].astype(jnp.float32)
                land[part][got[0]] = total.astype(land[part].dtype)
                o, later = r[0], r[1:]
                def src(part=part, slot=got[0]):
                    return land[part].at[slot]
                if axis == "A":
                    a = place.pos["A"]
                    at = n[0]
                    n[0] += 1
                    def copy(part=part, slot=got[0], o=o, at=at, i=i):
                        first = tables[part][(i, 0, ())]
                        return pltpu.make_async_remote_copy(
                            src_ref=land[part].at[slot], dst_ref=land[part].at[first + a], send_sem=send_sem.at[at],
                            recv_sem=recv_sem.at[base[part] + first + a],
                            device_id=place.device(dict(place.pos, A=o)), device_id_type=MESH)
                    away = [a != o]
                    under(away, lambda copy=copy: copy().start())
                    sends.append((away, copy))
                elif o:
                    send([], part, src, tables[part][(i, o, later)], lambda axis=axis, o=o: place.moved(**{axis: o}))
    last = len(orders[0]) - 1
    for part, order in enumerate(orders):
        own = tables[part][(last - 1, 1, (0,))]
        a = place.pos["A"]
        first = tables[part][(last, 0, ())]
        step = tables[part][(last - 1, 1, (line_order(size["A"])[1],))] - own if size["A"] > 1 else 0
        mine = own
        for k, p in enumerate(line_order(size["A"])):
            mine = jnp.where(a == p, tables[part][(last - 1, 1, (p,))], mine)
        total = land[part][mine].astype(jnp.float32)
        for d in range(1, size["A"]):
            j = lax.rem(a + d, size["A"])
            wait(part, first + j)
            total = total + land[part][first + j].astype(jnp.float32)
        finish(part, total)
    for conds, copy in sends:
        under(conds, lambda copy=copy: copy().wait_send())


def count_reduce(size, orders):
    total = 0
    for order in orders:
        for i, axis in enumerate(order):
            rest = 1
            for x in order[i + 1:]:
                rest *= size[x]
            total += size["A"] if axis == "A" else (size[axis] - 1) * rest
    return total


def norm_exchange(place, value_ref, land, send_sem, recv_sem):
    for n, axis in enumerate("CBYA"):
        mine = place.pos[axis]
        size = place.size[axis]
        land[n, mine] = value_ref[...]

        def copy(step, n=n, axis=axis, mine=mine, size=size):
            to = dict(place.pos)
            to[axis] = lax.rem(mine + step, size)
            return pltpu.make_async_remote_copy(
                src_ref=land.at[n, mine], dst_ref=land.at[n, mine], send_sem=send_sem.at[n, step],
                recv_sem=recv_sem.at[n, mine], device_id=place.device(to), device_id_type=MESH)

        for step in range(1, size):
            copy(step).start()
        for step in range(1, size):
            j = lax.rem(mine + step, size)
            pltpu.make_async_copy(land.at[n, j], land.at[n, j], recv_sem.at[n, j]).wait()
        total = land[n, 0]
        for j in range(1, size):
            total = total + land[n, j]
        for step in range(1, size):
            copy(step).wait_send()
        value_ref[...] = total


def reduce_kernel(n_dp, n_exp, orders, slices, dense, arrays, *refs):
    g_refs, out_refs, scratch = refs[:arrays], refs[arrays:2 * arrays], refs[2 * arrays + 1:]
    norm_ref = refs[2 * arrays]
    land, (send_sem, recv_sem) = scratch[:-2], scratch[-2:]
    place = Place(n_dp, n_exp)
    place.greet(orders[0], True)
    base = [0]
    for order in orders:
        base.append(base[-1] + len(stage_slots(place.size, order)))

    def finish(part, total):
        which, lo, w = slices[part]
        out_refs[which][:, lo:lo + w] = total

    reduce_body(place, orders, slices, g_refs, place.flat if dense else place.expert, land, base, send_sem, recv_sem, finish)
    total = jnp.zeros((8, 128), jnp.float32)
    for out in out_refs:
        total = total + jnp.sum(out[...] * out[...])
    norm_ref[...] = total


def reduce_dense(arrays, n_dp, n_exp, cid):
    size = sizes(n_dp, n_exp)
    blocks, rows = arrays[0].shape[:2]
    orders, slices = [], []
    for which, g in enumerate(arrays):
        cols = g.shape[2]
        half = cols // 128 * SHARE_BACK // 16 * 128
        for order, lo, w in (("CBYA", 0, half), ("CYBA", half, cols - half)):
            if w:
                orders.append(order)
                slices.append((which, lo, w))
    slots = [len(stage_slots(size, order)) for order in orders]
    return pl.pallas_call(
        functools.partial(reduce_kernel, n_dp, n_exp, orders, slices, True, len(arrays)),
        out_shape=[jax.ShapeDtypeStruct((rows, g.shape[2]), jnp.float32) for g in arrays] + [
            jax.ShapeDtypeStruct((8, 128), jnp.float32)],
        in_specs=[pl.BlockSpec(memory_space=pltpu.VMEM)] * len(arrays),
        out_specs=[pl.BlockSpec(memory_space=pltpu.VMEM)] * (len(arrays) + 1),
        scratch_shapes=[pltpu.VMEM((k, rows, s[2]), g.dtype) for k, s in zip(slots, slices)] + [
            pltpu.SemaphoreType.DMA((count_reduce(size, orders),)),
            pltpu.SemaphoreType.DMA((sum(slots),)),
        ],
        compiler_params=pltpu.CompilerParams(collective_id=cid, has_side_effects=True, vmem_limit_bytes=60 * 1024 * 1024),
        name="reduce_dense",
    )(*arrays)


def mm(a, b):
    return jnp.dot(a, b, preferred_element_type=jnp.float32)


def mm_nt(a, b):
    return lax.dot_general(a, b, (((1,), (1,)), ((), ())), preferred_element_type=jnp.float32)


def mm_tn(a, b):
    return lax.dot_general(a, b, (((0,), (0,)), ((), ())), preferred_element_type=jnp.float32)


def sig(v):
    return 1.0 / (1.0 + jnp.exp(-v))


def near_first(na):
    table = []
    for a in range(na):
        row = [a]
        for d in range(1, na):
            row += [p for p in ((a - d, a + d) if a < na // 2 else (a + d, a - d)) if 0 <= p < na]
        table.append(row)
    return table


def pair_order(na, nb):
    order = [(0, 0), (1, 0)]
    if na > 2:
        order += [(2, 0)] + [(2, t) for t in range(1, nb)]
    for i in range(3, na):
        order += [(i, t) for t in range(1, nb)] + [(i, 0)]
    return order + [(1, t) for t in range(1, nb)] + [(0, t) for t in range(1, nb)]


def choose(index, values):
    out = values[-1]
    for i in range(len(values) - 1):
        out = jnp.where(index == i, values[i], out)
    return out


def fused_kernel(n_dp, n_exp, experts, cap, halves, x_ref, cot_ref, rank_own, *refs):
    win_h, wdown_h, refs = refs[:halves], refs[halves:2 * halves], refs[2 * halves:]
    wrt_h, wshin_h, wshdown_h, xall, mixed_a, mixed_b, total_out, gg_out, refs = *refs[:8], refs[8:]
    gin_out, gdown_out, refs = refs[:halves], refs[halves:2 * halves], refs[2 * halves:]
    fused_body(n_dp, n_exp, experts, cap, x_ref, cot_ref, rank_own, win_h, wdown_h, wrt_h, wshin_h, wshdown_h,
               xall, mixed_a, mixed_b, total_out, gg_out, gin_out, gdown_out, *refs)


def fused_body(n_dp, n_exp, experts, cap, x_ref, cot_ref, rank_own, win_h, wdown_h, wrt_h, wshin_h, wshdown_h,
                 xall, mixed_a, mixed_b, total_out, gg_out, gin_out, gdown_out, gshin, gshdown, core_land, b_land, a_land,
                 win, wdown, wrt, wshin, wshdown, rank_ref, xv, cv, xr_s, act_s, gr_s, dgu_s, back_s, mixed_s, held, bsrc, stage,
                 gg_s, gin_acc, gdown_acc,
                 w_sem, x_sem, c_sem, m_sem, s_sem, ag_send, ag_recv, core_send, core_recv, b_send, b_recv,
                 a_send, a_recv, g_send, g_recv, r_send, r_recv, y_send, y_recv):
    low, wide = jnp.bfloat16, jnp.float32
    place = Place(n_dp, n_exp)
    na, nb = place.size["A"], place.size["B"]
    pos = place.pos
    a, c, me = pos["A"], pos["C"], place.expert(pos)
    toks, d = x_ref.shape[0], wdown.shape[1]
    given = cot_ref.shape[2]
    hid = wshdown.shape[0]
    table = near_first(na)
    order = pair_order(na, nb)
    steps = len(order)
    ahead = min(3, steps)
    near = [choose(a, [table[p][i] for p in range(na)]) for i in range(na)]
    sib = dict(pos, C=1 - c)

    def there(i, t, own_plane=True):
        return dict(pos, A=near[i], B=lax.rem(pos["B"] + t, nb), C=c if own_plane else 1 - c)

    barrier = pltpu.get_barrier_semaphore()
    for s in range(1, n_exp):
        pl.semaphore_signal(barrier, inc=1, device_id=(pos["Y"], lax.rem(me + s, n_exp)), device_id_type=MESH)
    if len(win_h) == 2:
        pl.semaphore_signal(barrier, inc=1, device_id=place.device(place.moved(Y=1)), device_id_type=MESH)
    pl.semaphore_wait(barrier, n_exp - 1 + (len(win_h) == 2))

    def rank_copy(s):
        j = lax.rem(me + s, n_exp)
        return pltpu.make_async_remote_copy(
            src_ref=rank_own.at[j], dst_ref=rank_ref.at[me], send_sem=r_send.at[j], recv_sem=r_recv.at[me],
            device_id=(pos["Y"], j), device_id_type=MESH)

    def rank_start(s, carry):
        rank_copy(s).start()
        return carry

    def rank_landed(j):
        pltpu.make_async_copy(rank_ref.at[j], rank_ref.at[j], r_recv.at[j]).wait()

    rank_ref[me] = rank_own[me]

    counter = [0]
    ag_sends = []

    def ag(conds, src, j, to):
        at = counter[0]
        counter[0] += 1

        def copy():
            return pltpu.make_async_remote_copy(
                src_ref=src(), dst_ref=xall.at[j()], send_sem=ag_send.at[at], recv_sem=ag_recv.at[j()],
                device_id=place.device(to()), device_id_type=MESH)

        ag_sends.append((conds, copy))
        under(conds(), lambda: copy().start())

    def landed(j):
        pltpu.make_async_copy(xall.at[j], xall.at[j], ag_recv.at[j]).wait()

    def own_block():
        return x_ref

    def always():
        return []

    for way in (1, -1):
        ag(lambda way=way: [place.inside(way)], own_block, lambda: me, lambda way=way: place.moved(A=way))
    for t in range(1, nb):
        ag(always, own_block, lambda: me, lambda t=t: place.moved(B=t))
    ag(always, own_block, lambda: me, lambda: sib)

    def line_arrival(i):
        def j():
            return place.expert(there(i, 0))

        def src():
            return xall.at[j()]

        landed(j())
        ag(lambda: [near[i] < a, place.inside(1)], src, j, lambda: place.moved(A=1))
        ag(lambda: [near[i] > a, place.inside(-1)], src, j, lambda: place.moved(A=-1))
        for t in range(1, nb):
            ag(always, src, j, lambda t=t: place.moved(B=t))
        ag(always, src, j, lambda: sib)

    def side_arrival(i):
        for t in range(1, nb):
            def j(t=t):
                return place.expert(there(i, t))

            landed(j())
            ag(always, lambda j=j: xall.at[j()], j, lambda: sib)

    lax.fori_loop(1, n_exp, rank_start, 0)

    before = {k: [] for k in range(steps)}
    for i in range(1, na):
        first = min(k for k, (q, _) in enumerate(order) if q == i)
        before[min(first, i)].append(lambda i=i: line_arrival(i))
    for i in range(na):
        first = min(k for k, (q, t) in enumerate(order) if q == i and t)
        before[min(first, i + 1)].append(lambda i=i: side_arrival(i))

    moves = [(wrt_h, wrt), (wshin_h, wshin), (wshdown_h, wshdown)]
    for pieces, whole in ((win_h, win), (wdown_h, wdown)):
        for n, piece in enumerate(pieces):
            rows = piece.shape[0]
            start = lax.rem(pos["Y"] + n, len(pieces)) * rows
            moves.append((piece, whole.at[pl.ds(pl.multiple_of(start, 16), rows)]))
    wloads = [pltpu.make_async_copy(h, v, w_sem.at[i]) for i, (h, v) in enumerate(moves)]
    for load in wloads:
        load.start()

    def pair_index(k):
        i = choose(k, [q for q, _ in order])
        t = choose(k, [q for _, q in order])
        p = dict(pos, A=choose(i, near), B=lax.rem(pos["B"] + t, nb))
        return place.expert(p), place.expert(dict(p, C=1 - c))

    def cot_load(k, slot):
        one, two = pair_index(k)
        return [pltpu.make_async_copy(cot_ref.at[j], cv.at[slot, n, :, pl.ds(0, given)], c_sem.at[slot, n])
                for n, j in enumerate((one, two))]

    def x_load(src, n, slot):
        loads = [pltpu.make_async_copy(src.at[:, pl.ds(0, d)], xv.at[n], x_sem.at[n, 0])]
        if given < d:
            loads.append(pltpu.make_async_copy(
                src.at[:, pl.ds(d, d - given)], cv.at[slot, n, :, pl.ds(given, d - given)], x_sem.at[n, 1]))
        return loads

    for load in cot_load(0, 0):
        load.start()
    gin_acc[...] = jnp.zeros_like(gin_acc)
    gdown_acc[...] = jnp.zeros_like(gdown_acc)
    gshin[...] = jnp.zeros_like(gshin)
    gshdown[...] = jnp.zeros_like(gshdown)
    for load in wloads:
        load.wait()

    def core_copy(k):
        return pltpu.make_async_remote_copy(
            src_ref=back_s.at[k % 2, 1], dst_ref=core_land.at[k], send_sem=core_send.at[k], recv_sem=core_recv.at[k],
            device_id=place.device(sib), device_id_type=MESH)

    b_steps = [k for k, (_, t) in enumerate(order) if t]

    def b_copy(k):
        i, t = order[k]
        n = b_steps.index(k)
        return pltpu.make_async_remote_copy(
            src_ref=bsrc.at[n % 2], dst_ref=b_land.at[i * (nb - 1) + t - 1], send_sem=b_send.at[n],
            recv_sem=b_recv.at[i * (nb - 1) + t - 1], device_id=place.device(place.moved(B=t)), device_id_type=MESH)

    def a_copy(i):
        return pltpu.make_async_remote_copy(
            src_ref=held.at[i], dst_ref=a_land.at[a], send_sem=a_send.at[i], recv_sem=a_recv.at[a],
            device_id=place.device(dict(pos, A=near[i])), device_id_type=MESH)

    def fetch(ref, sem, n):
        pltpu.make_async_copy(ref, ref, sem).wait()
        pltpu.make_async_copy(ref, stage.at[n], s_sem.at[n]).start()

    def fetched(n):
        pltpu.make_async_copy(stage.at[n], stage.at[n], s_sem.at[n]).wait()
        return stage[n].astype(wide)

    def core_fetch(k):
        fetch(core_land.at[k], core_recv.at[k], 0)

    def side_fetch(i):
        for t in range(1, nb):
            fetch(b_land.at[i * (nb - 1) + t - 1], b_recv.at[i * (nb - 1) + t - 1], t)

    def chip_sum(k):
        i, t = order[k]
        value = (back_s[k % 2, 0].astype(wide) + fetched(0)).astype(low)
        if t:
            n = b_steps.index(k)
            if n >= 2:
                b_copy(b_steps[n - 2]).wait_send()
            bsrc[n % 2] = value
            b_copy(k).start()
        else:
            held[i] = value

    def side_sum(i):
        value = held[i].astype(wide)
        for t in range(1, nb):
            value = value + fetched(t)
        held[i] = value.astype(low)
        if i:
            a_copy(i).start()

    early = {k: [] for k in range(steps)}
    middle = {k: [] for k in range(steps)}
    after = {k: [] for k in range(steps)}
    late = []
    for k in range(steps):
        if k + 1 < steps:
            early[k + 1].append(lambda k=k: core_fetch(k))
            middle[k + 1].append(lambda k=k: chip_sum(k))
        else:
            late.append(lambda k=k: core_fetch(k))
            late.append(lambda k=k: chip_sum(k))
    for i in list(range(2, na)) + [1, 0]:
        sent = max([k for k, (q, t) in enumerate(order) if q == i and t], default=0)
        ready = max(2 * (sent + 1) + 3, 2 * (order.index((i, 0)) + 1) + 1)
        fetching, adding = (lambda i=i: side_fetch(i)), (lambda i=i: side_sum(i))
        if ready // 2 >= steps:
            late += [fetching, adding]
        elif ready % 2:
            after[ready // 2] += [fetching, adding]
        else:
            early[ready // 2].append(fetching)
            middle[ready // 2].append(adding)

    def at(k, events):
        for n in range(steps):
            if events.get(n):
                @pl.when(k == n)
                def _(n=n):
                    for run in events[n]:
                        run()

    def gg_copy(k, n, to):
        return pltpu.make_async_remote_copy(
            src_ref=gg_s.at[k, n], dst_ref=gg_out.at[me], send_sem=g_send.at[k, n], recv_sem=g_recv.at[me],
            device_id=(pos["Y"], to), device_id_type=MESH)

    cut = mixed_a.shape[2]

    def mixed_copies(slot, n, j):
        return [
            pltpu.make_async_copy(mixed_s.at[slot, n, :, pl.ds(0, cut)], mixed_a.at[j], m_sem.at[slot, n, 0]),
            pltpu.make_async_copy(mixed_s.at[slot, n, :, pl.ds(cut, d - cut)], mixed_b.at[j], m_sem.at[slot, n, 1])]

    def step(k, carry):
        slot = lax.rem(k, 2)
        one, two = pair_index(k)
        @pl.when(k < ahead)
        def _():
            at(k, {q: before[q] if q < ahead else [] for q in range(steps)})

            @pl.when(k == 0)
            def _():
                for load in x_load(x_ref, 0, slot):
                    load.start()

            @pl.when(k > 0)
            def _():
                for load in x_load(xall.at[one], 0, slot):
                    load.start()
                rank_landed(one)

            landed(two)
            for load in x_load(xall.at[two], 1, slot):
                load.start()
            rank_landed(two)

        for n, j in enumerate((one, two)):
            for load in x_load(xall.at[j], n, slot):
                load.wait()
        for load in cot_load(k, slot):
            load.wait()

        @pl.when(k + 1 < steps)
        def _():
            for load in cot_load(k + 1, 1 - slot):
                load.start()

        ranks = (rank_ref[one], rank_ref[two])
        slots = lax.broadcasted_iota(jnp.int32, (cap, toks), 0).astype(wide)
        picks = [r == slots for r in ranks]
        crs = []
        for n in range(2):
            p = picks[n].astype(low)
            xr_s[n * cap:(n + 1) * cap, :] = mm(p, xv[n]).astype(low)
            crs.append(mm(p, cv[slot, n]).astype(low))
        cr = jnp.concatenate(crs, axis=0)
        at(k, early)
        gu = mm(xr_s[...], win[...])
        logits = mm(xr_s[...], wrt[...])
        lane = lax.broadcasted_iota(jnp.int32, logits.shape, 1)
        logits = jnp.where(lane < experts, logits, -1e30)
        ex = jnp.exp(logits - jnp.max(logits, axis=1, keepdims=True))
        gate = jnp.sum(jnp.where(lane == me, ex, 0.0), axis=1, keepdims=True) / jnp.sum(ex, axis=1, keepdims=True)
        g = gu[:, :FF]
        u = gu[:, FF:2 * FF]
        s = sig(g)
        sg = g * s
        act_s[...] = (sg * u).astype(low)
        gr_s[...] = (gate * cr.astype(wide)).astype(low)
        dact = mm_nt(gr_s[...], wdown[...])
        dgu_s[:, :FF] = (dact * u * (s + sg * (1.0 - s))).astype(low)
        dgu_s[:, FF:] = (dact * sg).astype(low)
        o = mm(act_s[...], wdown[...]).astype(low)
        of = o.astype(wide)
        gg = jnp.sum(cr.astype(wide) * of, axis=1, keepdims=True)
        wtd = (gate * of).astype(low)
        ib = mm_nt(dgu_s[...], win[...]).astype(low)
        at(k, middle)

        @pl.when(k >= 2)
        def _():
            for n, j in enumerate((one, two)):
                for copy in mixed_copies(slot, n, j):
                    copy.wait()

        for n in range(2):
            x = xv[n]
            ct = cv[slot, n]
            sh = mm(x, wshin[...])
            g2 = sh[:, :hid]
            u2 = sh[:, hid:]
            s2 = sig(g2)
            sg2 = g2 * s2
            sact = (sg2 * u2).astype(low)
            dsact = mm_nt(ct, wshdown[...])
            dsh = jnp.concatenate([dsact * u2 * (s2 + sg2 * (1.0 - s2)), dsact * sg2], axis=1).astype(low)
            p = picks[n].astype(low)
            rows = slice(n * cap, (n + 1) * cap)
            mixed_s[slot, n] = (mm_tn(p, wtd[rows]) + mm(sact, wshdown[...])).astype(low)
            back_s[slot, n] = (mm_tn(p, ib[rows]) + mm_nt(dsh, wshin[...])).astype(low)
            gg_s[k, n] = jnp.sum(jnp.where(picks[n], gg[rows], 0.0), axis=0, keepdims=True)
            gshdown[...] += mm_tn(sact, ct)
            gshin[...] += mm_tn(x, dsh)
        for n, j in enumerate((one, two)):
            for copy in mixed_copies(slot, n, j):
                copy.start()
        at(k, {q: [lambda q=q: core_copy(q).start()] for q in range(steps)})

        @pl.when(k > 0)
        def _():
            gg_copy(k, 0, one).start()

        gg_copy(k, 1, two).start()
        at(k, after)

        @pl.when((k + 1 >= ahead) & (k + 1 < steps))
        def _():
            at(k, {q - 1: before[q] for q in range(ahead, steps)})
            next_one, next_two = pair_index(k + 1)
            for load in x_load(xall.at[next_one], 0, 1 - slot):
                load.start()
            landed(next_two)
            for load in x_load(xall.at[next_two], 1, 1 - slot):
                load.start()
            rank_landed(next_one)
            rank_landed(next_two)

        gdown_acc[...] += mm_tn(act_s[...], gr_s[...])
        gin_acc[...] += mm_tn(xr_s[...], dgu_s[...])
        at(k, {q: [lambda q=q: core_copy(q - 1).wait_send()] if q else [] for q in range(steps)})
        return carry

    lax.fori_loop(0, steps, step, 0)
    gg_out[me] = gg_s[0, 0]
    outs = []
    for pieces, whole, acc in ((gin_out, win, gin_acc), (gdown_out, wdown, gdown_acc)):
        whole[...] = acc[...].astype(low)
        for n, piece in enumerate(pieces):
            rows = piece.shape[0]
            start = lax.rem(pos["Y"] + n, len(pieces)) * rows
            part = whole.at[pl.ds(pl.multiple_of(start, 16), rows)]
            if n and whole is win:
                outs.append(pltpu.make_async_remote_copy(
                    src_ref=part, dst_ref=piece, send_sem=y_send, recv_sem=y_recv,
                    device_id=place.device(place.moved(Y=1)), device_id_type=MESH))
            else:
                outs.append(pltpu.make_async_copy(part, piece, w_sem.at[len(outs)]))
            outs[-1].start()
    for run in late:
        run()
    total = held[0].astype(wide)
    for s in range(1, na):
        j = lax.rem(a + s, na)
        fetch(a_land.at[j], a_recv.at[j], 0)
        total = total + fetched(0)
    gin_acc[:toks, :d] = total
    last = pltpu.make_async_copy(gin_acc.at[pl.ds(0, toks), pl.ds(0, d)], total_out, s_sem.at[0])
    last.start()
    last.wait()
    for out in outs:
        out.wait()
    core_copy(steps - 1).wait_send()
    for k in b_steps[-2:]:
        b_copy(k).wait_send()
    for i in range(1, na):
        a_copy(i).wait_send()
    for conds, copy in ag_sends:
        under(conds(), lambda copy=copy: copy().wait_send())
    for k in (steps - 2, steps - 1):
        one, two = pair_index(k)
        for n, j in enumerate((one, two)):
            for copy in mixed_copies(k % 2, n, j):
                copy.wait()

    def gg_done(k, carry):
        one, two = pair_index(k)

        @pl.when(k > 0)
        def _():
            gg_copy(k, 0, one).wait_send()

        gg_copy(k, 1, two).wait_send()
        return carry

    lax.fori_loop(0, steps, gg_done, 0)

    def gg_wait(s, carry):
        j = lax.rem(me + s, n_exp)
        pltpu.make_async_copy(gg_out.at[j], gg_out.at[j], g_recv.at[j]).wait()
        return carry

    lax.fori_loop(1, n_exp, gg_wait, 0)

    def rank_sent(s, carry):
        rank_copy(s).wait_send()
        return carry

    lax.fori_loop(1, n_exp, rank_sent, 0)


def fused(x, cot_all, rank, win, wdown, wrt, wshin, wshdown, n_dp, n_exp, experts, cap, cid):
    toks, d = x.shape[0], wshdown.shape[1]
    size = sizes(n_dp, n_exp)
    na, nb = size["A"], size["B"]
    steps = na * nb
    hid = wshdown.shape[0]
    low, wide = jnp.bfloat16, jnp.float32
    hbm = pl.BlockSpec(memory_space=pl.ANY)
    vmem = pl.BlockSpec(memory_space=pltpu.VMEM)
    rows = 2 * cap
    block = (toks, d)
    dma = pltpu.SemaphoreType.DMA
    ag_count = 2 + (nb - 1) + 1 + (na - 1) * (2 + nb) + na * (nb - 1)
    flops = 2 * n_exp * (cap * d * FF * 9 + toks * cap * d * 4 + toks * d * hid * 9)
    out = pl.pallas_call(
        functools.partial(fused_kernel, n_dp, n_exp, experts, cap, len(win)),
        in_specs=[hbm, hbm, vmem] + [hbm] * (2 * len(win) + 3),
        out_shape=[
            jax.ShapeDtypeStruct((n_exp,) + x.shape, low),
            jax.ShapeDtypeStruct((n_exp, toks, MIXED_FIRST), low),
            jax.ShapeDtypeStruct((n_exp, toks, d - MIXED_FIRST), low),
            jax.ShapeDtypeStruct(block, wide),
            jax.ShapeDtypeStruct((n_exp, 1, toks), wide),
            *[jax.ShapeDtypeStruct(w.shape, low) for w in (*win, *wdown)],
            jax.ShapeDtypeStruct((d, 2 * hid), wide),
            jax.ShapeDtypeStruct((hid, d), wide),
            jax.ShapeDtypeStruct((steps,) + block, low),
            jax.ShapeDtypeStruct((na * max(nb - 1, 1),) + block, low),
            jax.ShapeDtypeStruct((na,) + block, low),
        ],
        out_specs=[hbm, hbm, hbm, hbm, vmem] + [hbm] * (2 * len(win)) + [vmem, vmem, hbm, hbm, hbm],
        scratch_shapes=[
            pltpu.VMEM((d, 2 * FF), low), pltpu.VMEM((FF, d), low), pltpu.VMEM(wrt.shape, low),
            pltpu.VMEM(wshin.shape, low), pltpu.VMEM(wshdown.shape, low), pltpu.VMEM((n_exp, 1, toks), wide),
            pltpu.VMEM((2,) + block, low), pltpu.VMEM((2, 2) + block, low),
            pltpu.VMEM((rows, d), low), pltpu.VMEM((rows, FF), low), pltpu.VMEM((rows, d), low),
            pltpu.VMEM((rows, 2 * FF), low),
            pltpu.VMEM((2, 2) + block, low), pltpu.VMEM((2, 2) + block, low), pltpu.VMEM((na,) + block, low),
            pltpu.VMEM((2,) + block, low), pltpu.VMEM((nb,) + block, low),
            pltpu.VMEM((steps, 2, 1, toks), wide), pltpu.VMEM((d, 2 * FF), wide), pltpu.VMEM((FF, d), wide),
            dma((3 + 2 * len(win),)), dma((2, 2)), dma((2, 2)), dma((2, 2, 2)), dma((nb,)),
            dma((ag_count,)), dma((n_exp,)), dma((steps,)), dma((steps,)),
            dma((na * max(nb - 1, 1),)), dma((na * max(nb - 1, 1),)), dma((na,)), dma((na,)),
            dma((steps, 2)), dma((n_exp,)), dma((n_exp,)), dma((n_exp,)), dma(()), dma(()),
        ],
        compiler_params=pltpu.CompilerParams(collective_id=cid, has_side_effects=True, vmem_limit_bytes=63 * 1024 * 1024),
        cost_estimate=pl.CostEstimate(flops=flops, bytes_accessed=100 * 1024 * 1024, transcendentals=0),
        name="experts_fused",
    )(x, cot_all, rank, *win, *wdown, wrt, wshin, wshdown)
    n = len(win)
    return out[1], out[2], out[3], out[4], out[5:5 + n], out[5 + n:5 + 2 * n], out[5 + 2 * n], out[6 + 2 * n]


def attend_kernel(heads_n, experts, tok_ref, gains_ref, full_ref, router_ref, cos_ref, sin_ref, bias_ref,
                  q_ref, k_ref, v_ref, heads_ref, resid_ref, mlp_ref, probs_ref, attn_ref):
    low, wide = jnp.bfloat16, jnp.float32
    width = heads_n * HD
    d = mlp_ref.shape[1]
    scale = HD ** (-0.5)
    inputs = tok_ref[...].astype(wide)
    attn_ref[...] = (inputs * rms_scale(inputs) * gains_ref[0:1, :]).astype(low)
    lane = lax.broadcasted_iota(jnp.int32, (1, HD), 1)
    sign = jnp.where(lane < HD // 2, -1.0, 1.0)

    def turn(g):
        return g * cos_ref[...] + pltpu.roll(g, HD // 2, 1) * sign * sin_ref[...]

    pair = 2 * HD

    def project(j, carry):
        for part, out in ((0, q_ref), (1, k_ref), (2, v_ref)):
            y = mm(attn_ref[...], full_ref[:, pl.ds(pl.multiple_of(part * width + j * pair, HD), pair)])
            for n in range(2):
                one = y[:, n * HD : (n + 1) * HD]
                at = pl.ds(pl.multiple_of(j * pair + n * HD, HD), HD)
                out[:, at] = (turn(one) if part < 2 else one).astype(low)
        return carry

    lax.fori_loop(0, heads_n // 2, project, 0)

    def head(h, carry):
        at = pl.ds(pl.multiple_of(h * HD, HD), HD)
        s = jnp.where(bias_ref[...] > 0.0, mm_nt(q_ref[:, at], k_ref[:, at]) * scale, NEGATIVE)
        e = jnp.exp(s - jnp.max(s, axis=-1, keepdims=True))
        p = e / jnp.sum(e, axis=-1, keepdims=True)
        heads_ref[:, at] = mm(p.astype(low), v_ref[:, at]).astype(low)
        return carry

    lax.fori_loop(0, heads_n, head, 0)
    residual = inputs + mm(heads_ref[...], full_ref[:, 3 * width : 3 * width + d])
    resid_ref[...] = residual
    mlp_ref[...] = (residual * rms_scale(residual) * gains_ref[1:2, :]).astype(low)
    logits = mm_nt(router_ref[...], mlp_ref[...])
    e = jnp.exp(logits - jnp.max(logits, axis=0, keepdims=True))
    probs_ref[...] = e / jnp.sum(e, axis=0, keepdims=True)


def attend(experts, tokens, *args):
    toks, d = tokens.shape
    low, wide = jnp.bfloat16, jnp.float32
    width = H * HD
    shape = jax.ShapeDtypeStruct
    vmem = pl.BlockSpec(memory_space=pltpu.VMEM)
    return pl.pallas_call(
        functools.partial(attend_kernel, H, experts),
        in_specs=[vmem] * (len(args) + 1),
        out_specs=[vmem] * 8,
        out_shape=[shape((toks, width), low)] * 4 + [
            shape((toks, d), wide), shape((toks, d), low), shape((experts, toks), wide), shape((toks, d), low)],
        compiler_params=pltpu.CompilerParams(vmem_limit_bytes=60 * 1024 * 1024),
        cost_estimate=pl.CostEstimate(flops=7 * 10**9, bytes_accessed=24 * 1024 * 1024, transcendentals=0),
        name="attend",
    )(tokens, *args)


def attend_back_kernel(
    heads_n, experts, back_ref, gg_ref, probs_ref, router_ref, mlp_ref, resid_ref, cot_ref, tok_ref, gains_ref, full_ref,
    heads_ref, q_ref, k_ref, v_ref, attn_ref, cos_ref, sin_ref, bias_ref,
    gqkv_ref, gout_ref, gin_ref, small_ref, pg_ref, hg_ref, rl_ref
):
    low, wide = jnp.bfloat16, jnp.float32
    width = heads_n * HD
    d = mlp_ref.shape[1]
    scale = HD ** (-0.5)
    gg = gg_ref[...]
    rp = probs_ref[...]
    logit = (rp * (gg - jnp.sum(gg * rp, axis=0, keepdims=True))).astype(low)
    residual = resid_ref[...]
    r2 = rms_scale(residual)
    n2 = residual * r2
    mg = back_ref[...] + mm_tn(logit, router_ref[...])
    small_ref[...] = jnp.zeros_like(small_ref)
    small_ref[0:experts, :] = mm(logit, mlp_ref[...])
    small_ref[experts + 8 : experts + 9, :] = jnp.sum(mg * n2, axis=0, keepdims=True)
    u = mg * gains_ref[1:2, :]
    resid_grad = cot_ref[...].astype(wide) + r2 * (u - n2 * jnp.mean(u * n2, axis=-1, keepdims=True))
    gin_ref[...] = resid_grad
    rl_ref[...] = resid_grad.astype(low)
    gout_ref[...] = mm_tn(heads_ref[...], rl_ref[...]).astype(low)
    hg_ref[...] = mm_nt(rl_ref[...], full_ref[:, 3 * width : 3 * width + d]).astype(low)
    lane = lax.broadcasted_iota(jnp.int32, (1, HD), 1)
    sign = jnp.where(lane < HD // 2, 1.0, -1.0)

    def turn_back(g):
        return g * cos_ref[...] + pltpu.roll(g * sin_ref[...], HD // 2, 1) * sign

    def head(h, carry):
        at = pl.ds(pl.multiple_of(h * HD, HD), HD)
        q, k, v, hg = q_ref[:, at], k_ref[:, at], v_ref[:, at], hg_ref[:, at]
        s = jnp.where(bias_ref[...] > 0.0, mm_nt(q, k) * scale, NEGATIVE)
        e = jnp.exp(s - jnp.max(s, axis=-1, keepdims=True))
        p = e / jnp.sum(e, axis=-1, keepdims=True)
        dp = mm_nt(hg, v)
        sg = (p * (dp - jnp.sum(dp * p, axis=-1, keepdims=True))).astype(low)
        pg_ref[:, at] = turn_back(mm(sg, k) * scale).astype(low)
        pg_ref[:, pl.ds(pl.multiple_of(width + h * HD, HD), HD)] = turn_back(mm_tn(sg, q) * scale).astype(low)
        pg_ref[:, pl.ds(pl.multiple_of(2 * width + h * HD, HD), HD)] = mm_tn(p.astype(low), hg).astype(low)
        return carry

    lax.fori_loop(0, heads_n, head, 0)
    wide_cols = 640

    def columns(j, carry):
        at = pl.ds(pl.multiple_of(j * wide_cols, 128), wide_cols)
        gqkv_ref[:, at] = mm_tn(attn_ref[...], pg_ref[:, at]).astype(low)
        return carry

    lax.fori_loop(0, 3 * width // wide_cols, columns, 0)
    ag = mm_nt(pg_ref[...], full_ref[:, : 3 * width])
    inputs = tok_ref[...].astype(wide)
    r1 = rms_scale(inputs)
    n1 = inputs * r1
    small_ref[experts : experts + 1, :] = jnp.sum(ag * n1, axis=0, keepdims=True)
    u1 = ag * gains_ref[0:1, :]
    gin_ref[...] += r1 * (u1 - n1 * jnp.mean(u1 * n1, axis=-1, keepdims=True))


def attend_back(experts, *args):
    toks, d = args[4].shape
    low, wide = jnp.bfloat16, jnp.float32
    width = H * HD
    return pl.pallas_call(
        functools.partial(attend_back_kernel, H, experts),
        in_specs=[pl.BlockSpec(memory_space=pltpu.VMEM)] * len(args),
        out_specs=[pl.BlockSpec(memory_space=pltpu.VMEM)] * 4,
        out_shape=[
            jax.ShapeDtypeStruct((d, 3 * width), low),
            jax.ShapeDtypeStruct((width, d), low),
            jax.ShapeDtypeStruct((toks, d), wide),
            jax.ShapeDtypeStruct((experts + 16, d), wide),
        ],
        scratch_shapes=[pltpu.VMEM((toks, 3 * width), low), pltpu.VMEM((toks, width), low), pltpu.VMEM((toks, d), low)],
        compiler_params=pltpu.CompilerParams(vmem_limit_bytes=62 * 1024 * 1024),
        cost_estimate=pl.CostEstimate(flops=14 * 10**9, bytes_accessed=45 * 1024 * 1024, transcendentals=0),
        name="attend_back",
    )(*args)


def norm_kernel(n_dp, n_exp, counts, sq_ref, *refs):
    groups, refs = refs[: sum(counts)], refs[sum(counts) :]
    norm_ref, land, send_sem, recv_sem = refs
    place = Place(n_dp, n_exp)
    place.greet("CBYA", True)
    total = sq_ref[...]
    at = 0
    for count in counts:
        pieces = groups[at : at + count]
        at += count
        rows, cols = pieces[0].shape
        step = 32 if rows % 32 == 0 else rows

        def add(i, acc, pieces=pieces, step=step):
            part = pl.ds(pl.multiple_of(i * step, step), step)
            g = pieces[0][part, :].astype(jnp.float32)
            for piece in pieces[1:]:
                g = g + piece[part, :].astype(jnp.float32)
            return acc + jnp.sum(g * g, axis=0, keepdims=True)

        sums = lax.fori_loop(0, rows // step, add, jnp.zeros((1, cols), jnp.float32))
        total = total + jnp.sum(sums)
    norm_ref[...] = total
    norm_exchange(place, norm_ref, land, send_sem, recv_sem)


def sum_squares(groups, dense_squares, n_dp, n_exp, cid):
    top = max(sizes(n_dp, n_exp).values())
    flat = [g for group in groups for g in group]
    vmem = pl.BlockSpec(memory_space=pltpu.VMEM)
    return pl.pallas_call(
        functools.partial(norm_kernel, n_dp, n_exp, [len(group) for group in groups]),
        out_shape=jax.ShapeDtypeStruct((8, 128), jnp.float32),
        in_specs=[vmem] * (1 + len(flat)),
        out_specs=vmem,
        scratch_shapes=[
            pltpu.VMEM((4, top, 8, 128), jnp.float32),
            pltpu.SemaphoreType.DMA((4, top)),
            pltpu.SemaphoreType.DMA((4, top)),
        ],
        compiler_params=pltpu.CompilerParams(collective_id=cid, has_side_effects=True, vmem_limit_bytes=40 * 1024 * 1024),
        name="sum_squares",
    )(dense_squares, *flat)


def adam_kernel(rates, decays, big, counts, norm_ref, *refs):
    n = len(rates)
    states, grads, at = [], [], 0
    for i in range(n):
        states.append(refs[at : at + 3])
        at += 3
    for i in range(n):
        grads.append(refs[at : at + counts[i]])
        at += counts[i]
    outs = [refs[at + 3 * i : at + 3 * i + 3] for i in range(n)]
    at += 3 * n
    held = []
    for i in range(big):
        held.append((refs[at : at + 3], refs[at + 3 : at + 3 + counts[i]], refs[at + 3 + counts[i]], refs[at + 4 + counts[i]]))
        at += 5 + counts[i]

    def copies(i, j):
        state_v, grad_v, in_sem, out_sem = held[i]
        step = CHUNK if state_v[0].shape[0] % CHUNK == 0 else CHUNK // 2
        part = pl.ds(pl.multiple_of(j * step, step), step)
        pairs = list(zip(states[i] + grads[i], state_v + grad_v))
        ins = [pltpu.make_async_copy(a.at[part], b.at[part], in_sem.at[j, q]) for q, (a, b) in enumerate(pairs)]
        back = [pltpu.make_async_copy(a.at[part], b.at[part], out_sem.at[j, q]) for q, (a, b) in enumerate(zip(state_v, outs[i]))]
        return part, ins, back

    def chunks(i):
        rows = held[i][0][0].shape[0]
        return rows // (CHUNK if rows % CHUNK == 0 else CHUNK // 2)

    for i in range(big):

        def load(j, carry, i=i):
            for copy in copies(i, j)[1]:
                copy.start()
            return carry

        lax.fori_loop(0, chunks(i), load, 0)
    factor = jnp.minimum(1.0, CLIP / jnp.sqrt(norm_ref[0:1, 0:1]))

    def total(pieces, part):
        g = pieces[0][part].astype(jnp.float32)
        for piece in pieces[1:]:
            g = g + piece[part].astype(jnp.float32)
        return g

    for i in range(big, n):
        w, m, v = states[i]
        new = adam_update(w[...], m[...], v[...], total(grads[i], Ellipsis), factor, rates[i], decays[i])
        for out, value in zip(outs[i], new):
            out[...] = value
    for i in range(big):

        def work(j, carry, i=i):
            part, ins, back = copies(i, j)
            for copy in ins:
                copy.wait()
            state_v, grad_v = held[i][0], held[i][1]
            new = adam_update(
                state_v[0][part, :], state_v[1][part, :], state_v[2][part, :], total(grad_v, part), factor, rates[i], decays[i]
            )
            for ref, value in zip(state_v, new):
                ref[part, :] = value
            for copy in back:
                copy.start()
            return carry

        lax.fori_loop(0, chunks(i), work, 0)
    for i in range(big):

        def finish(j, carry, i=i):
            for copy in copies(i, j)[2]:
                copy.wait()
            return carry

        lax.fori_loop(0, chunks(i), finish, 0)


def adam(norm, states, grads, rates, decays, big):
    hbm = pl.BlockSpec(memory_space=pl.ANY)
    vmem = pl.BlockSpec(memory_space=pltpu.VMEM)
    counts = [len(g) for g in grads]
    flat = [a for s in states for a in s] + [a for g in grads for a in g]
    specs = [hbm if i < big else vmem for i in range(len(states)) for _ in range(3)]
    scratch = []
    for i in range(big):
        rows = states[i][0].shape[0]
        pieces = rows // (CHUNK if rows % CHUNK == 0 else CHUNK // 2)
        scratch += [pltpu.VMEM(a.shape, a.dtype) for a in (*states[i], *grads[i])]
        scratch += [pltpu.SemaphoreType.DMA((pieces, 3 + counts[i])), pltpu.SemaphoreType.DMA((pieces, 3))]
    out = pl.pallas_call(
        functools.partial(adam_kernel, rates, decays, big, counts),
        in_specs=[vmem] + specs + [hbm if i < big else vmem for i in range(len(grads)) for _ in range(counts[i])],
        out_specs=specs,
        out_shape=[jax.ShapeDtypeStruct(a.shape, a.dtype) for s in states for a in s],
        scratch_shapes=scratch,
        compiler_params=pltpu.CompilerParams(vmem_limit_bytes=60 * 1024 * 1024),
        name="adam",
    )(norm, *flat)
    return [tuple(out[3 * i : 3 * i + 3]) for i in range(len(states))]


def swap_rows(x, n_dp):
    if n_dp != 2:
        return [lax.all_gather(x, "dp", axis=0, tiled=True)]
    return [x, lax.ppermute(x, "dp", [(0, 1), (1, 0)])]


def in_order(pieces):
    if len(pieces) == 1:
        return pieces[0]
    first = lax.axis_index("dp") == 0
    x, other = pieces
    return jnp.concatenate([jnp.where(first, x, other), jnp.where(first, other, x)], axis=0)


def split_rows(x, n_dp):
    if n_dp != 2:
        return [x]
    rows = x.shape[0] // 2
    top, bottom = x[:rows], x[rows:]
    first = lax.axis_index("dp") == 0
    return [jnp.where(first, top, bottom), jnp.where(first, bottom, top)]


def local(
    tokens,
    lengths,
    routes,
    cotangent,
    norm_gains,
    gains_m,
    gains_v,
    w_qkv,
    m_qkv,
    v_qkv,
    w_out,
    m_out,
    v_out,
    w_shared_in,
    m_shared_in,
    v_shared_in,
    w_shared_down,
    m_shared_down,
    v_shared_down,
    w_router,
    m_router,
    v_router,
    w_expert_in,
    m_expert_in,
    v_expert_in,
    w_expert_down,
    m_expert_down,
    v_expert_down,
):
    both = ("dp", "expert")
    low = jnp.bfloat16
    wide = jnp.float32
    row_count = tokens.shape[0]
    expert_count = w_router.shape[1]
    n_dp = lax.axis_size("dp")
    n_exp = lax.axis_size("expert")
    n_all = n_dp * n_exp
    capacity = min(row_count, (5 * row_count * TOP // (4 * expert_count) + 7) // 8 * 8)
    rows_w = w_qkv.shape[0]
    unit = w_shared_down.shape[0]

    pad = jnp.zeros((rows_w, 128 - expert_count - 2), wide)
    packed = jnp.concatenate([w_qkv, w_out, w_router, norm_gains.T, pad], axis=1).astype(low)
    edown_low = w_expert_down[0].astype(low)
    full, edown_other = gather(packed, edown_low, n_dp, n_exp, True, 1)
    full = full.reshape(D, -1)
    expert_down_full = [edown_low, edown_other] if n_dp == 2 else swap_rows(edown_low, n_dp)
    full, ein_low = lax.optimization_barrier((full, w_expert_in[0].astype(low)))
    expert_in_full = swap_rows(ein_low, n_dp)
    small_full = full[:, 3 * H * HD + D :]
    router_full = small_full[:, :expert_count]
    gain_one = small_full[:, expert_count].astype(wide)
    gain_two = small_full[:, expert_count + 1].astype(wide)
    cot_all = lax.all_gather(cotangent[:, :GIVEN], "expert", axis=0, tiled=False)
    shin_send = (
        w_shared_in.astype(low)
        .reshape(rows_w, 2, n_dp, n_exp, unit)
        .transpose(3, 0, 1, 2, 4)
        .reshape(n_exp, rows_w, 2 * n_dp * unit)
    )
    shin_send = jnp.concatenate([shin_send] * n_dp, axis=0)
    shin_mine = lax.all_to_all(shin_send, both, 0, 0, tiled=True).reshape(D, 2 * n_dp * unit)
    shdown_mine = in_order(swap_rows(w_shared_down.astype(low), n_dp))
    half = n_dp * unit

    gain_rows = jnp.stack([gain_one, gain_two])
    router_rows = router_full.T
    cosine, sine_table, allowed = rotary_tables(lengths[0], row_count, HD)
    allowed = allowed.astype(wide)
    queries, keys_rot, values_low, heads_low, residual, mlp_in, probs_rows, attn_in = attend(
        expert_count, tokens, gain_rows, full, router_rows, cosine, sine_table, allowed
    )

    routed = jnp.any(routes[:, :, None] == jnp.arange(expert_count, dtype=jnp.int32), axis=1)
    rank = jnp.where(routed, jnp.cumsum(routed.astype(jnp.int32), axis=0) - 1, -1).astype(wide).T
    hid = (half + 127) // 128 * 128
    cap = (capacity + 15) // 16 * 16
    wrt = jnp.concatenate([router_full, jnp.zeros((D, 128 - expert_count), low)], axis=1)
    gap = jnp.zeros((D, hid - half), low)
    wshin = jnp.concatenate([shin_mine[:, :half], gap, shin_mine[:, half:], gap], axis=1)
    wshdown = jnp.concatenate([shdown_mine, jnp.zeros((hid - half, D), low)], axis=0)
    mixed_a, mixed_b, back_sum, gate_grad, grad_ein, grad_edown, shin_wide, shdown_wide = fused(
        jnp.concatenate([mlp_in, cotangent[:, GIVEN:]], axis=1), cot_all, rank[:, None, :], expert_in_full, expert_down_full, wrt, wshin, wshdown, n_dp, n_exp, expert_count, cap, 2
    )
    mixed_a = lax.psum_scatter(mixed_a, "expert", scatter_dimension=0, tiled=False)
    grad_shin = jnp.concatenate([shin_wide[:, :half], shin_wide[:, hid : hid + half]], axis=1)
    grad_shdown = shdown_wide[:half]
    grad_qkv, grad_out, input_grad, small_rows = attend_back(
        expert_count,
        back_sum,
        gate_grad[:, 0, :],
        probs_rows,
        router_rows,
        mlp_in,
        residual,
        cotangent,
        tokens,
        gain_rows,
        full,
        heads_low,
        queries,
        keys_rot,
        values_low,
        attn_in,
        cosine,
        sine_table,
        allowed,
    )

    shin_back = lax.all_to_all(
        grad_shin.astype(low).reshape(n_all, rows_w, 2 * half), both, 0, 0, tiled=True
    )
    shdown_halves = split_rows(grad_shdown, n_dp)
    if n_dp == 2:
        swap = [(0, 1), (1, 0)]
        came = (lax.ppermute(shdown_halves[1], "dp", swap), lax.ppermute(grad_edown[1], "dp", swap))
        grad_qkv, shin_back, came = lax.optimization_barrier((grad_qkv, shin_back, came))
        shdown_own = [shdown_halves[0], came[0]]
        edown_own = [grad_edown[0], came[1]]
        ein_own = list(grad_ein)
    else:
        shdown_own, edown_own, ein_own = (
            [lax.psum_scatter(g[0], "dp", scatter_dimension=0, tiled=True)] for g in (shdown_halves, grad_edown, grad_ein)
        )
    small_grad = jnp.concatenate(
        [small_rows.astype(low).T, jnp.zeros((D, 128 - expert_count - 16), low)], axis=1
    )
    shin_own = jnp.sum(
        shin_back.reshape(n_dp, n_exp, rows_w, 2, n_dp, unit).astype(wide), axis=0
    )
    shin_own = shin_own.transpose(1, 2, 3, 0, 4).reshape(rows_w, 2 * FF)
    qkv_own, out_own, small_own, dense_squares = reduce_dense(
        [g.reshape(n_all, rows_w, -1) for g in (grad_qkv, grad_out, small_grad)], n_dp, n_exp, 5
    )
    qkv_own, mixed_a, mixed_b = lax.optimization_barrier((qkv_own, mixed_a, mixed_b))
    mixed_b = lax.psum_scatter(mixed_b, "expert", scatter_dimension=0, tiled=False)
    norm = sum_squares([[shin_own], shdown_own, ein_own, edown_own], dense_squares, n_dp, n_exp, 6)
    grad_norm = jnp.sqrt(norm[0, 0])
    weights = (
        norm_gains,
        w_qkv,
        w_out,
        w_shared_in,
        w_shared_down,
        w_router,
        w_expert_in,
        w_expert_down,
    )
    firsts = (
        gains_m,
        m_qkv,
        m_out,
        m_shared_in,
        m_shared_down,
        m_router,
        m_expert_in,
        m_expert_down,
    )
    seconds = (
        gains_v,
        v_qkv,
        v_out,
        v_shared_in,
        v_shared_down,
        v_router,
        v_expert_in,
        v_expert_down,
    )
    rates = (
        GAIN_RATE,
        D ** (-0.5),
        (H * HD // 64) ** (-0.5),
        D ** (-0.5),
        FF ** (-0.5),
        (4 * D) ** (-0.5),
        D ** (-0.5),
        (FF // 64) ** (-0.5),
    )
    decays = (0.0, DECAY, DECAY, DECAY, DECAY, DECAY, DECAY, DECAY)
    owned = (
        [small_own[:, expert_count : expert_count + 16 : 8].T],
        [qkv_own],
        [out_own],
        [shin_own],
        shdown_own,
        [small_own[:, :expert_count]],
        ein_own,
        edown_own,
    )
    order = (6, 7, 0, 1, 2, 3, 4, 5)
    states = [
        tuple(a.reshape(a.shape[-2:]) for a in (weights[i], firsts[i], seconds[i])) for i in order
    ]
    fresh = adam(norm, states, [owned[i] for i in order], [rates[i] for i in order], [decays[i] for i in order], 2)
    new = dict(zip(order, fresh))
    updated = [a.reshape(b.shape) for i in range(8) for a, b in zip(new[i], (weights[i], firsts[i], seconds[i]))]
    mixed_b, *updated = lax.optimization_barrier((mixed_b, *updated))
    mixed = (residual + jnp.concatenate([mixed_a, mixed_b], axis=1).astype(wide)).astype(low)
    return (
        mixed,
        input_grad,
        updated[0],
        updated[1],
        updated[2],
        updated[3],
        updated[4],
        updated[5],
        updated[6],
        updated[7],
        updated[8],
        updated[9],
        updated[10],
        updated[11],
        updated[12],
        updated[13],
        updated[14],
        updated[15],
        updated[16],
        updated[17],
        updated[18],
        updated[19],
        updated[20],
        updated[21],
        updated[22],
        updated[23],
        grad_norm,
    )


def solution(mesh):
    placed = (
        P(("dp", "expert"), None),
        P(("dp", "expert"), None),
        P(("dp", "expert"), None),
        P(("dp", "expert"), None),
        P(None, ("dp", "expert")),
        P(None, ("dp", "expert")),
        P(None, ("dp", "expert")),
        P(("dp", "expert"), None),
        P(("dp", "expert"), None),
        P(("dp", "expert"), None),
        P(("dp", "expert"), None),
        P(("dp", "expert"), None),
        P(("dp", "expert"), None),
        P(("dp", "expert"), None),
        P(("dp", "expert"), None),
        P(("dp", "expert"), None),
        P(("dp", "expert"), None),
        P(("dp", "expert"), None),
        P(("dp", "expert"), None),
        P(("dp", "expert"), None),
        P(("dp", "expert"), None),
        P(("dp", "expert"), None),
        P("expert", "dp", None),
        P("expert", "dp", None),
        P("expert", "dp", None),
        P("expert", "dp", None),
        P("expert", "dp", None),
        P("expert", "dp", None),
    )
    return jax.shard_map(
        local,
        mesh=mesh,
        in_specs=placed,
        out_specs=(
            P(("dp", "expert"), None),
            P(("dp", "expert"), None),
            P(None, ("dp", "expert")),
            P(None, ("dp", "expert")),
            P(None, ("dp", "expert")),
            P(("dp", "expert"), None),
            P(("dp", "expert"), None),
            P(("dp", "expert"), None),
            P(("dp", "expert"), None),
            P(("dp", "expert"), None),
            P(("dp", "expert"), None),
            P(("dp", "expert"), None),
            P(("dp", "expert"), None),
            P(("dp", "expert"), None),
            P(("dp", "expert"), None),
            P(("dp", "expert"), None),
            P(("dp", "expert"), None),
            P(("dp", "expert"), None),
            P(("dp", "expert"), None),
            P(("dp", "expert"), None),
            P("expert", "dp", None),
            P("expert", "dp", None),
            P("expert", "dp", None),
            P("expert", "dp", None),
            P("expert", "dp", None),
            P("expert", "dp", None),
            P(),
        ),
        check_vma=False,
    )
```

```python
import functools
import itertools

import jax
import jax.numpy as jnp
from jax import lax
from jax.experimental import pallas as pl
from jax.experimental.pallas import tpu as pltpu
from jax.sharding import PartitionSpec as P

D = 1280
H = 10
HD = 128
FF = 896
TOP = 6
ADAM_STEP = 5
HEAD = 192
MIXED_FIRST = 896
GIVEN = 1280


EPS = 1e-06
ROPE_BASE = 10000.0
BETA_ONE = 0.9
BETA_TWO = 0.95
ADAM_EPS = 1e-08
DECAY = 0.1
CLIP = 1.0
GAIN_RATE = 0.5
NEGATIVE = -1e30


def rms_scale(values):
    return lax.rsqrt(jnp.mean(values * values, axis=-1, keepdims=True) + EPS)


def rotary_tables(seq_lengths, row_count, head_width):
    position = jnp.arange(row_count, dtype=jnp.int32)
    seq_ends = jnp.cumsum(seq_lengths)
    segment = jnp.sum((position[:, None] >= seq_ends[None, :]).astype(jnp.int32), axis=1)
    starts = seq_ends - seq_lengths
    slot_ids = jnp.arange(seq_lengths.shape[0], dtype=jnp.int32)
    first_row = jnp.sum(
        jnp.where(segment[:, None] == slot_ids[None, :], starts[None, :], 0), axis=1
    )
    seq_place = (position - first_row).astype(jnp.float32)
    inv_freq = ROPE_BASE ** (-jnp.arange(head_width // 2, dtype=jnp.float32) * 2.0 / head_width)
    phase_angle = seq_place[:, None] * inv_freq[None, :]
    cosine = jnp.concatenate([jnp.cos(phase_angle), jnp.cos(phase_angle)], axis=1)
    sine_table = jnp.concatenate([jnp.sin(phase_angle), jnp.sin(phase_angle)], axis=1)
    allowed = (segment[:, None] == segment[None, :]) & (position[None, :] <= position[:, None])
    return (cosine, sine_table, allowed)


def adam_update(weight, first_moment, second_moment, gradient, factor, step_rate, decay_rate):
    clipped = gradient * factor
    first_new = BETA_ONE * first_moment + (1.0 - BETA_ONE) * clipped
    second_new = BETA_TWO * second_moment + (1.0 - BETA_TWO) * clipped * clipped
    first_hat = first_new / (1.0 - BETA_ONE**ADAM_STEP)
    second_hat = second_new / (1.0 - BETA_TWO**ADAM_STEP)
    weight_new = weight - step_rate * (
        first_hat / (jnp.sqrt(second_hat) + ADAM_EPS) + decay_rate * weight
    )
    return (weight_new, first_new, second_new)


MESH = pl.DeviceIdType.MESH


PIECE = 64
CHUNK = 64
SHARE_BACK = 6


class Place:
    def __init__(self, n_dp, n_exp):
        rest = n_exp // 2
        na = 4 if rest % 4 == 0 else rest
        self.size = {"A": na, "B": rest // na, "C": 2, "Y": n_dp}
        e = lax.axis_index("expert")
        nb = self.size["B"]
        self.pos = {"A": e // (2 * nb), "B": (e // 2) % nb, "C": e % 2, "Y": lax.axis_index("dp")}

    def expert(self, pos):
        return (pos["A"] * self.size["B"] + pos["B"]) * 2 + pos["C"]

    def flat(self, pos):
        return pos["Y"] * (2 * self.size["A"] * self.size["B"]) + self.expert(pos)

    def device(self, pos):
        return (pos["Y"], self.expert(pos))

    def moved(self, **steps):
        pos = dict(self.pos)
        for axis, step in steps.items():
            if axis == "A":
                pos[axis] = pos[axis] + step
            else:
                pos[axis] = lax.rem(pos[axis] + step, self.size[axis])
        return pos

    def inside(self, step):
        there = self.pos["A"] + step
        return (there >= 0) & (there < self.size["A"])

    def greet(self, axes, line_all):
        barrier = pltpu.get_barrier_semaphore()
        total = 0
        for axis in axes:
            if axis == "A":
                reach = range(1, self.size["A"]) if line_all else (1,)
                for step in [s * d for d in reach for s in (1, -1)]:
                    near = self.inside(step)

                    @pl.when(near)
                    def _(step=step):
                        pl.semaphore_signal(barrier, inc=1, device_id=self.device(self.moved(A=step)), device_id_type=MESH)

                    total = total + jnp.where(near, 1, 0)
            else:
                for step in range(1, self.size[axis]):
                    pl.semaphore_signal(barrier, inc=1, device_id=self.device(self.moved(**{axis: step})), device_id_type=MESH)
                    total = total + 1
        pl.semaphore_wait(barrier, total)


def under(conds, body):
    if conds:
        both = conds[0]
        for c in conds[1:]:
            both = both & c
        pl.when(both)(body)
    else:
        body()


PACE = {"A": 4, "B": 5, "Y": 5, "C": 1}


def plan_gather(size, orders):
    events = []
    for part, order in enumerate(orders):
        spans = []
        for axis in order:
            n = size[axis]
            spans.append(range(1 - n, n) if axis == "A" else range(n))
        for offs in itertools.product(*spans):
            when = 0
            for axis, o in zip(order, offs):
                when += PACE[axis] * (abs(o) if axis == "A" else (1 if o else 0))
            events.append((when, part, offs))
    events.sort(key=lambda ev: ev[0])
    return events


def gather_body(place, orders, slices, own_ref, out_ref, block_of, send_sem, recv_sem, fill=()):
    size = place.size
    sends = []
    count = [0]

    def send(conds, part, src_block, src, to):
        slot = count[0]
        count[0] += 1
        lo, n = slices[part]

        def copy():
            j = src_block()
            return pltpu.make_async_remote_copy(
                src_ref=(own_ref if src is None else out_ref.at[j]).at[:, pl.ds(lo, n)],
                dst_ref=out_ref.at[j].at[:, pl.ds(lo, n)],
                send_sem=send_sem.at[slot],
                recv_sem=recv_sem.at[part, j],
                device_id=place.device(to()),
                device_id_type=MESH,
            )

        under(conds, lambda: copy().start())
        sends.append((conds, copy))

    fill = list(fill)
    plan = plan_gather(size, orders)
    every = max(1, len(plan) // (len(fill) + 1))
    for number, (_, part, offs) in enumerate(plan):
        if fill and number % every == every - 1:
            fill.pop(0)()
        order = orders[part]
        steps = dict(zip(order, offs))
        last = max([i for i, o in enumerate(offs) if o], default=-1)
        conds = []
        if steps["A"]:
            conds.append(place.inside(steps["A"]))

        def block(steps=steps):
            return block_of(place.moved(**{k: o for k, o in steps.items() if o}))

        if last >= 0:
            lo, n = slices[part]

            def wait(block=block, part=part, lo=lo, n=n):
                j = block()
                pltpu.make_async_copy(
                    out_ref.at[j].at[:, pl.ds(lo, n)], out_ref.at[j].at[:, pl.ds(lo, n)], recv_sem.at[part, j]
                ).wait()

            under(conds, wait)
        src = None if last < 0 else out_ref
        for i in range(max(last, 0), len(order)):
            axis = order[i]
            if axis == "A":
                ways = (1, -1) if i > last else ((1,) if steps["A"] < 0 else (-1,))
                for way in ways:
                    send(conds + [place.inside(way)], part, block, src, lambda way=way: place.moved(A=way))
            elif i > last:
                for t in range(1, size[axis]):
                    send(conds, part, block, src, lambda axis=axis, t=t: place.moved(**{axis: t}))
    for run in fill:
        run()
    for conds, copy in sends:
        under(conds, lambda copy=copy: copy().wait_send())


def count_gather(size, orders):
    total = 0
    for _, part, offs in plan_gather(size, orders):
        order = orders[part]
        last = max([i for i, o in enumerate(offs) if o], default=-1)
        for i in range(max(last, 0), len(order)):
            if order[i] == "A":
                total += 2 if i > last else 1
            elif i > last:
                total += size[order[i]] - 1
    return total


def sizes(n_dp, n_exp):
    rest = n_exp // 2
    na = 4 if rest % 4 == 0 else rest
    return {"A": na, "B": rest // na, "C": 2, "Y": n_dp}


def gather_kernel(n_dp, n_exp, orders, slices, dense, n_pass, x_ref, *refs):
    pass_refs, out_ref, passed_refs = refs[:n_pass], refs[n_pass], refs[n_pass + 1:2 * n_pass + 1]
    send_sem, recv_sem, local_sem, pass_send, pass_recv = refs[2 * n_pass + 1:]
    place = Place(n_dp, n_exp)
    pieces = [(q, r) for q in range(n_pass) for r in range(pass_refs[q].shape[0] // PIECE)] if n_dp == 2 else []

    def piece(n):
        q, r = pieces[n]
        rows = pl.ds(r * PIECE, PIECE)
        return pltpu.make_async_remote_copy(
            src_ref=pass_refs[q].at[rows], dst_ref=passed_refs[q].at[rows], send_sem=pass_send.at[n], recv_sem=pass_recv.at[n],
            device_id=place.device(place.moved(Y=1)), device_id_type=MESH)

    block_of = place.flat if dense else place.expert
    place.greet(orders[0], False)
    own = pltpu.make_async_copy(x_ref, out_ref.at[block_of(place.pos)], local_sem)
    own.start()
    gather_body(place, orders, slices, x_ref, out_ref, block_of, send_sem, recv_sem,
                [lambda n=n: piece(n).start() for n in range(len(pieces))])
    own.wait()
    for n in range(len(pieces)):
        piece(n).wait()


def gather(x, passed, n_dp, n_exp, dense, cid, parts=None):
    size = sizes(n_dp, n_exp)
    rows, cols = x.shape
    if dense:
        orders = ("ABYC", "AYBC")
        half = cols // 256 * 128
        slices = ((0, half), (half, cols - half))
    else:
        orders = parts or ("ABC",)
        w = cols // len(orders)
        slices = tuple((i * w, w) for i in range(len(orders)))
    blocks = n_exp * (n_dp if dense else 1)
    return pl.pallas_call(
        functools.partial(gather_kernel, n_dp, n_exp, orders, slices, dense, len(passed)),
        out_shape=[jax.ShapeDtypeStruct((blocks, rows, cols), x.dtype)] + [
            jax.ShapeDtypeStruct(p.shape, p.dtype) for p in passed],
        in_specs=[pl.BlockSpec(memory_space=pl.ANY)] * (1 + len(passed)),
        out_specs=[pl.BlockSpec(memory_space=pl.ANY)] * (1 + len(passed)),
        scratch_shapes=[
            pltpu.SemaphoreType.DMA((count_gather(size, orders),)),
            pltpu.SemaphoreType.DMA((len(orders), blocks)),
            pltpu.SemaphoreType.DMA(()),
            pltpu.SemaphoreType.DMA((max(1, sum(p.shape[0] // PIECE for p in passed)),)),
            pltpu.SemaphoreType.DMA((max(1, sum(p.shape[0] // PIECE for p in passed)),)),
        ],
        compiler_params=pltpu.CompilerParams(collective_id=cid, has_side_effects=True),
        name="gather_dense" if dense else "gather_group",
    )(x, *passed)


def line_order(n):
    out = []
    for i in range((n + 1) // 2):
        out.append(i)
        if n - 1 - i != i:
            out.append(n - 1 - i)
    return out


def stage_slots(size, order):
    slots = {}
    for i, axis in enumerate(order):
        rest = [line_order(size[x]) if x == "A" else range(size[x]) for x in order[i + 1:]]
        if axis == "A":
            for who in range(size["A"]):
                slots[(i, who, ())] = len(slots)
        else:
            for who in range(1, size[axis]):
                for r in itertools.product(*rest):
                    slots[(i, who, r)] = len(slots)
    return slots


def reduce_body(place, orders, slices, g_refs, block_of, land, base, send_sem, recv_sem, finish):
    size = place.size
    tables = [stage_slots(size, order) for order in orders]
    sends = []
    n = [0]

    def target(order, i, o, rest):
        pos = dict(place.pos)
        for axis, v in zip(order[i:], (o,) + tuple(rest)):
            if axis == "A":
                pos["A"] = v
            else:
                pos[axis] = lax.rem(pos[axis] + v, size[axis])
        return pos

    def send(conds, part, src, slot, to):
        at = n[0]
        n[0] += 1

        def copy():
            return pltpu.make_async_remote_copy(
                src_ref=src(), dst_ref=land[part].at[slot], send_sem=send_sem.at[at],
                recv_sem=recv_sem.at[base[part] + slot], device_id=place.device(to()), device_id_type=MESH)

        under(conds, lambda: copy().start())
        sends.append((conds, copy))

    def wait(part, slot):
        ref = land[part].at[slot]
        pltpu.make_async_copy(ref, ref, recv_sem.at[base[part] + slot]).wait()

    def rests(order, i):
        return list(itertools.product(*[line_order(size[x]) if x == "A" else range(size[x]) for x in order[i:]]))

    def far_first(items):
        return sorted(items, key=lambda r: tuple(0 if (isinstance(v, int) and v) else 1 for v in r[:-1]))

    for part, order in enumerate(orders):
        g_ref, lo, w = g_refs[slices[part][0]], slices[part][1], slices[part][2]
        axis = order[0]
        for t in range(1, size[axis]):
            for r in far_first(rests(order, 1)):
                def src(order=order, t=t, r=r, lo=lo, w=w, g_ref=g_ref):
                    return g_ref.at[block_of(target(order, 0, t, r)), :, pl.ds(lo, w)]
                send([], part, src, tables[part][(0, t, r)], lambda axis=axis, t=t: place.moved(**{axis: t}))
    for i in range(1, len(orders[0])):
        for pick in far_first(rests(orders[0], i)):
            for part, order in enumerate(orders):
                g_ref, lo, w = g_refs[slices[part][0]], slices[part][1], slices[part][2]
                axis = order[i]
                before = order[i - 1]
                r = pick
                got = [tables[part][(i - 1, t, r)] for t in range(1, size[before])]
                for slot in got:
                    wait(part, slot)
                if i == 1:
                    total = g_ref[block_of(target(order, 1, r[0], r[1:])), :, lo:lo + w].astype(jnp.float32)
                else:
                    total = land[part][tables[part][(i - 2, 1, (0,) + r)]].astype(jnp.float32)
                for slot in got:
                    total = total + land[part][slot].astype(jnp.float32)
                land[part][got[0]] = total.astype(land[part].dtype)
                o, later = r[0], r[1:]
                def src(part=part, slot=got[0]):
                    return land[part].at[slot]
                if axis == "A":
                    a = place.pos["A"]
                    at = n[0]
                    n[0] += 1
                    def copy(part=part, slot=got[0], o=o, at=at, i=i):
                        first = tables[part][(i, 0, ())]
                        return pltpu.make_async_remote_copy(
                            src_ref=land[part].at[slot], dst_ref=land[part].at[first + a], send_sem=send_sem.at[at],
                            recv_sem=recv_sem.at[base[part] + first + a],
                            device_id=place.device(dict(place.pos, A=o)), device_id_type=MESH)
                    away = [a != o]
                    under(away, lambda copy=copy: copy().start())
                    sends.append((away, copy))
                elif o:
                    send([], part, src, tables[part][(i, o, later)], lambda axis=axis, o=o: place.moved(**{axis: o}))
    last = len(orders[0]) - 1
    for part, order in enumerate(orders):
        own = tables[part][(last - 1, 1, (0,))]
        a = place.pos["A"]
        first = tables[part][(last, 0, ())]
        step = tables[part][(last - 1, 1, (line_order(size["A"])[1],))] - own if size["A"] > 1 else 0
        mine = own
        for k, p in enumerate(line_order(size["A"])):
            mine = jnp.where(a == p, tables[part][(last - 1, 1, (p,))], mine)
        total = land[part][mine].astype(jnp.float32)
        for d in range(1, size["A"]):
            j = lax.rem(a + d, size["A"])
            wait(part, first + j)
            total = total + land[part][first + j].astype(jnp.float32)
        finish(part, total)
    for conds, copy in sends:
        under(conds, lambda copy=copy: copy().wait_send())


def count_reduce(size, orders):
    total = 0
    for order in orders:
        for i, axis in enumerate(order):
            rest = 1
            for x in order[i + 1:]:
                rest *= size[x]
            total += size["A"] if axis == "A" else (size[axis] - 1) * rest
    return total


def norm_exchange(place, value_ref, land, send_sem, recv_sem):
    for n, axis in enumerate("CBYA"):
        mine = place.pos[axis]
        size = place.size[axis]
        land[n, mine] = value_ref[...]

        def copy(step, n=n, axis=axis, mine=mine, size=size):
            to = dict(place.pos)
            to[axis] = lax.rem(mine + step, size)
            return pltpu.make_async_remote_copy(
                src_ref=land.at[n, mine], dst_ref=land.at[n, mine], send_sem=send_sem.at[n, step],
                recv_sem=recv_sem.at[n, mine], device_id=place.device(to), device_id_type=MESH)

        for step in range(1, size):
            copy(step).start()
        for step in range(1, size):
            j = lax.rem(mine + step, size)
            pltpu.make_async_copy(land.at[n, j], land.at[n, j], recv_sem.at[n, j]).wait()
        total = land[n, 0]
        for j in range(1, size):
            total = total + land[n, j]
        for step in range(1, size):
            copy(step).wait_send()
        value_ref[...] = total


def reduce_kernel(n_dp, n_exp, orders, slices, dense, arrays, *refs):
    g_refs, out_refs, scratch = refs[:arrays], refs[arrays:2 * arrays], refs[2 * arrays + 1:]
    norm_ref = refs[2 * arrays]
    land, (send_sem, recv_sem) = scratch[:-2], scratch[-2:]
    place = Place(n_dp, n_exp)
    place.greet(orders[0], True)
    base = [0]
    for order in orders:
        base.append(base[-1] + len(stage_slots(place.size, order)))

    def finish(part, total):
        which, lo, w = slices[part]
        out_refs[which][:, lo:lo + w] = total

    reduce_body(place, orders, slices, g_refs, place.flat if dense else place.expert, land, base, send_sem, recv_sem, finish)
    total = jnp.zeros((8, 128), jnp.float32)
    for out in out_refs:
        total = total + jnp.sum(out[...] * out[...])
    norm_ref[...] = total


def reduce_dense(arrays, n_dp, n_exp, cid):
    size = sizes(n_dp, n_exp)
    blocks, rows = arrays[0].shape[:2]
    orders, slices = [], []
    for which, g in enumerate(arrays):
        cols = g.shape[2]
        half = cols // 128 * SHARE_BACK // 16 * 128
        for order, lo, w in (("CBYA", 0, half), ("CYBA", half, cols - half)):
            if w:
                orders.append(order)
                slices.append((which, lo, w))
    slots = [len(stage_slots(size, order)) for order in orders]
    return pl.pallas_call(
        functools.partial(reduce_kernel, n_dp, n_exp, orders, slices, True, len(arrays)),
        out_shape=[jax.ShapeDtypeStruct((rows, g.shape[2]), jnp.float32) for g in arrays] + [
            jax.ShapeDtypeStruct((8, 128), jnp.float32)],
        in_specs=[pl.BlockSpec(memory_space=pltpu.VMEM)] * len(arrays),
        out_specs=[pl.BlockSpec(memory_space=pltpu.VMEM)] * (len(arrays) + 1),
        scratch_shapes=[pltpu.VMEM((k, rows, s[2]), g.dtype) for k, s in zip(slots, slices)] + [
            pltpu.SemaphoreType.DMA((count_reduce(size, orders),)),
            pltpu.SemaphoreType.DMA((sum(slots),)),
        ],
        compiler_params=pltpu.CompilerParams(collective_id=cid, has_side_effects=True, vmem_limit_bytes=60 * 1024 * 1024),
        name="reduce_dense",
    )(*arrays)


def mm(a, b):
    return jnp.dot(a, b, preferred_element_type=jnp.float32)


def mm_nt(a, b):
    return lax.dot_general(a, b, (((1,), (1,)), ((), ())), preferred_element_type=jnp.float32)


def mm_tn(a, b):
    return lax.dot_general(a, b, (((0,), (0,)), ((), ())), preferred_element_type=jnp.float32)


def sig(v):
    return 1.0 / (1.0 + jnp.exp(-v))


def near_first(na):
    table = []
    for a in range(na):
        row = [a]
        for d in range(1, na):
            row += [p for p in ((a - d, a + d) if a < na // 2 else (a + d, a - d)) if 0 <= p < na]
        table.append(row)
    return table


def pair_order(na, nb):
    order = [(0, 0), (1, 0)]
    if na > 2:
        order += [(2, 0)] + [(2, t) for t in range(1, nb)]
    for i in range(3, na):
        order += [(i, t) for t in range(1, nb)] + [(i, 0)]
    return order + [(1, t) for t in range(1, nb)] + [(0, t) for t in range(1, nb)]


def choose(index, values):
    out = values[-1]
    for i in range(len(values) - 1):
        out = jnp.where(index == i, values[i], out)
    return out


def fused_kernel(n_dp, n_exp, experts, cap, n_in, halves, x_ref, cot_ref, rank_own, *refs):
    win_h, wdown_h, refs = refs[:n_in], refs[n_in:n_in + halves], refs[n_in + halves:]
    wrt_h, wshin_h, wshdown_h, xall, mixed_a, mixed_b, total_out, gg_out, refs = *refs[:8], refs[8:]
    gin_out, gdown_out, refs = refs[:halves], refs[halves:2 * halves], refs[2 * halves:]
    fused_body(n_dp, n_exp, experts, cap, x_ref, cot_ref, rank_own, win_h, wdown_h, wrt_h, wshin_h, wshdown_h,
               xall, mixed_a, mixed_b, total_out, gg_out, gin_out, gdown_out, *refs)


def fused_body(n_dp, n_exp, experts, cap, x_ref, cot_ref, rank_own, win_h, wdown_h, wrt_h, wshin_h, wshdown_h,
                 xall, mixed_a, mixed_b, total_out, gg_out, gin_out, gdown_out, gshin, gshdown, core_land, b_land, a_land,
                 win, wdown, wrt, wshin, wshdown, rank_ref, xv, cv, xr_s, act_s, gr_s, dgu_s, back_s, mixed_s, held, bsrc, stage,
                 gg_s, gin_acc, gdown_acc,
                 w_sem, x_sem, c_sem, m_sem, s_sem, ag_send, ag_recv, core_send, core_recv, b_send, b_recv,
                 a_send, a_recv, g_send, g_recv, r_send, r_recv, y_send, y_recv):
    low, wide = jnp.bfloat16, jnp.float32
    place = Place(n_dp, n_exp)
    na, nb = place.size["A"], place.size["B"]
    pos = place.pos
    a, c, me = pos["A"], pos["C"], place.expert(pos)
    toks, d = x_ref.shape[0], wdown.shape[1]
    given = cot_ref.shape[2]
    hid = wshdown.shape[0]
    table = near_first(na)
    order = pair_order(na, nb)
    steps = len(order)
    ahead = min(3, steps)
    near = [choose(a, [table[p][i] for p in range(na)]) for i in range(na)]
    sib = dict(pos, C=1 - c)

    def there(i, t, own_plane=True):
        return dict(pos, A=near[i], B=lax.rem(pos["B"] + t, nb), C=c if own_plane else 1 - c)

    barrier = pltpu.get_barrier_semaphore()
    for s in range(1, n_exp):
        pl.semaphore_signal(barrier, inc=1, device_id=(pos["Y"], lax.rem(me + s, n_exp)), device_id_type=MESH)
    if len(wdown_h) == 2:
        pl.semaphore_signal(barrier, inc=1, device_id=place.device(place.moved(Y=1)), device_id_type=MESH)
    pl.semaphore_wait(barrier, n_exp - 1 + (len(wdown_h) == 2))

    def rank_copy(s):
        j = lax.rem(me + s, n_exp)
        return pltpu.make_async_remote_copy(
            src_ref=rank_own.at[j], dst_ref=rank_ref.at[me], send_sem=r_send.at[j], recv_sem=r_recv.at[me],
            device_id=(pos["Y"], j), device_id_type=MESH)

    def rank_start(s, carry):
        rank_copy(s).start()
        return carry

    def rank_landed(j):
        pltpu.make_async_copy(rank_ref.at[j], rank_ref.at[j], r_recv.at[j]).wait()

    rank_ref[me] = rank_own[me]

    counter = [0]
    ag_sends = []

    def ag(conds, src, j, to):
        at = counter[0]
        counter[0] += 1

        def copy():
            return pltpu.make_async_remote_copy(
                src_ref=src(), dst_ref=xall.at[j()], send_sem=ag_send.at[at], recv_sem=ag_recv.at[j()],
                device_id=place.device(to()), device_id_type=MESH)

        ag_sends.append((conds, copy))
        under(conds(), lambda: copy().start())

    def landed(j):
        pltpu.make_async_copy(xall.at[j], xall.at[j], ag_recv.at[j]).wait()

    def own_block():
        return x_ref

    def always():
        return []

    for way in (1, -1):
        ag(lambda way=way: [place.inside(way)], own_block, lambda: me, lambda way=way: place.moved(A=way))
    for t in range(1, nb):
        ag(always, own_block, lambda: me, lambda t=t: place.moved(B=t))
    ag(always, own_block, lambda: me, lambda: sib)

    def line_arrival(i):
        def j():
            return place.expert(there(i, 0))

        def src():
            return xall.at[j()]

        landed(j())
        ag(lambda: [near[i] < a, place.inside(1)], src, j, lambda: place.moved(A=1))
        ag(lambda: [near[i] > a, place.inside(-1)], src, j, lambda: place.moved(A=-1))
        for t in range(1, nb):
            ag(always, src, j, lambda t=t: place.moved(B=t))
        ag(always, src, j, lambda: sib)

    def side_arrival(i):
        for t in range(1, nb):
            def j(t=t):
                return place.expert(there(i, t))

            landed(j())
            ag(always, lambda j=j: xall.at[j()], j, lambda: sib)

    lax.fori_loop(1, n_exp, rank_start, 0)

    before = {k: [] for k in range(steps)}
    for i in range(1, na):
        first = min(k for k, (q, _) in enumerate(order) if q == i)
        before[min(first, i)].append(lambda i=i: line_arrival(i))
    for i in range(na):
        first = min(k for k, (q, t) in enumerate(order) if q == i and t)
        before[min(first, i + 1)].append(lambda i=i: side_arrival(i))

    moves = [(wrt_h, wrt), (wshin_h, wshin), (wshdown_h, wshdown)]
    for pieces, whole in ((win_h, win), (wdown_h, wdown)):
        here = max(len(pieces) // 2, 1)
        base = sum(piece.shape[0] for piece in pieces[:here])
        for first in range(0, len(pieces), here):
            start = lax.rem(pos["Y"] + first // here, len(pieces) // here) * base
            for piece in pieces[first:first + here]:
                moves.append((piece, whole.at[pl.ds(pl.multiple_of(start, 16), piece.shape[0])]))
                start = start + piece.shape[0]
    wloads = [pltpu.make_async_copy(h, v, w_sem.at[i]) for i, (h, v) in enumerate(moves)]
    for load in wloads:
        load.start()

    def pair_index(k):
        i = choose(k, [q for q, _ in order])
        t = choose(k, [q for _, q in order])
        p = dict(pos, A=choose(i, near), B=lax.rem(pos["B"] + t, nb))
        return place.expert(p), place.expert(dict(p, C=1 - c))

    def cot_load(k, slot):
        one, two = pair_index(k)
        return [pltpu.make_async_copy(cot_ref.at[j], cv.at[slot, n, :, pl.ds(0, given)], c_sem.at[slot, n])
                for n, j in enumerate((one, two))]

    def x_load(src, n, slot):
        loads = [pltpu.make_async_copy(src.at[:, pl.ds(0, d)], xv.at[n], x_sem.at[n, 0])]
        if given < d:
            loads.append(pltpu.make_async_copy(
                src.at[:, pl.ds(d, d - given)], cv.at[slot, n, :, pl.ds(given, d - given)], x_sem.at[n, 1]))
        return loads

    for load in cot_load(0, 0):
        load.start()
    gin_acc[...] = jnp.zeros_like(gin_acc)
    gdown_acc[...] = jnp.zeros_like(gdown_acc)
    gshin[...] = jnp.zeros_like(gshin)
    gshdown[...] = jnp.zeros_like(gshdown)
    for load in wloads:
        load.wait()

    def core_copy(k):
        return pltpu.make_async_remote_copy(
            src_ref=back_s.at[k % 2, 1], dst_ref=core_land.at[k], send_sem=core_send.at[k], recv_sem=core_recv.at[k],
            device_id=place.device(sib), device_id_type=MESH)

    b_steps = [k for k, (_, t) in enumerate(order) if t]

    def b_copy(k):
        i, t = order[k]
        n = b_steps.index(k)
        return pltpu.make_async_remote_copy(
            src_ref=bsrc.at[n % 2], dst_ref=b_land.at[i * (nb - 1) + t - 1], send_sem=b_send.at[n],
            recv_sem=b_recv.at[i * (nb - 1) + t - 1], device_id=place.device(place.moved(B=t)), device_id_type=MESH)

    def a_copy(i):
        return pltpu.make_async_remote_copy(
            src_ref=held.at[i], dst_ref=a_land.at[a], send_sem=a_send.at[i], recv_sem=a_recv.at[a],
            device_id=place.device(dict(pos, A=near[i])), device_id_type=MESH)

    def fetch(ref, sem, n):
        pltpu.make_async_copy(ref, ref, sem).wait()
        pltpu.make_async_copy(ref, stage.at[n], s_sem.at[n]).start()

    def fetched(n):
        pltpu.make_async_copy(stage.at[n], stage.at[n], s_sem.at[n]).wait()
        return stage[n].astype(wide)

    def core_fetch(k):
        fetch(core_land.at[k], core_recv.at[k], 0)

    def side_fetch(i):
        for t in range(1, nb):
            fetch(b_land.at[i * (nb - 1) + t - 1], b_recv.at[i * (nb - 1) + t - 1], t)

    def chip_sum(k):
        i, t = order[k]
        value = (back_s[k % 2, 0].astype(wide) + fetched(0)).astype(low)
        if t:
            n = b_steps.index(k)
            if n >= 2:
                b_copy(b_steps[n - 2]).wait_send()
            bsrc[n % 2] = value
            b_copy(k).start()
        else:
            held[i] = value

    def side_sum(i):
        value = held[i].astype(wide)
        for t in range(1, nb):
            value = value + fetched(t)
        held[i] = value.astype(low)
        if i:
            a_copy(i).start()

    early = {k: [] for k in range(steps)}
    middle = {k: [] for k in range(steps)}
    after = {k: [] for k in range(steps)}
    late = []
    for k in range(steps):
        if k + 1 < steps:
            early[k + 1].append(lambda k=k: core_fetch(k))
            middle[k + 1].append(lambda k=k: chip_sum(k))
        else:
            late.append(lambda k=k: core_fetch(k))
            late.append(lambda k=k: chip_sum(k))
    for i in list(range(2, na)) + [1, 0]:
        sent = max([k for k, (q, t) in enumerate(order) if q == i and t], default=0)
        ready = max(2 * (sent + 1) + 3, 2 * (order.index((i, 0)) + 1) + 1)
        fetching, adding = (lambda i=i: side_fetch(i)), (lambda i=i: side_sum(i))
        if ready // 2 >= steps:
            late += [fetching, adding]
        elif ready % 2:
            after[ready // 2] += [fetching, adding]
        else:
            early[ready // 2].append(fetching)
            middle[ready // 2].append(adding)

    def at(k, events):
        for n in range(steps):
            if events.get(n):
                @pl.when(k == n)
                def _(n=n):
                    for run in events[n]:
                        run()

    def gg_copy(k, n, to):
        return pltpu.make_async_remote_copy(
            src_ref=gg_s.at[k, n], dst_ref=gg_out.at[me], send_sem=g_send.at[k, n], recv_sem=g_recv.at[me],
            device_id=(pos["Y"], to), device_id_type=MESH)

    cut = mixed_a.shape[2]

    def mixed_copies(slot, n, j):
        return [
            pltpu.make_async_copy(mixed_s.at[slot, n, :, pl.ds(0, cut)], mixed_a.at[j], m_sem.at[slot, n, 0]),
            pltpu.make_async_copy(mixed_s.at[slot, n, :, pl.ds(cut, d - cut)], mixed_b.at[j], m_sem.at[slot, n, 1])]

    def step(k, carry):
        slot = lax.rem(k, 2)
        one, two = pair_index(k)
        @pl.when(k < ahead)
        def _():
            at(k, {q: before[q] if q < ahead else [] for q in range(steps)})

            @pl.when(k == 0)
            def _():
                for load in x_load(x_ref, 0, slot):
                    load.start()

            @pl.when(k > 0)
            def _():
                for load in x_load(xall.at[one], 0, slot):
                    load.start()
                rank_landed(one)

            landed(two)
            for load in x_load(xall.at[two], 1, slot):
                load.start()
            rank_landed(two)

        for n, j in enumerate((one, two)):
            for load in x_load(xall.at[j], n, slot):
                load.wait()
        for load in cot_load(k, slot):
            load.wait()

        @pl.when(k + 1 < steps)
        def _():
            for load in cot_load(k + 1, 1 - slot):
                load.start()

        ranks = (rank_ref[one], rank_ref[two])
        slots = lax.broadcasted_iota(jnp.int32, (cap, toks), 0).astype(wide)
        picks = [r == slots for r in ranks]
        crs = []
        for n in range(2):
            p = picks[n].astype(low)
            xr_s[n * cap:(n + 1) * cap, :] = mm(p, xv[n]).astype(low)
            crs.append(mm(p, cv[slot, n]).astype(low))
        cr = jnp.concatenate(crs, axis=0)
        at(k, early)
        gu = mm(xr_s[...], win[...])
        logits = mm(xr_s[...], wrt[...])
        lane = lax.broadcasted_iota(jnp.int32, logits.shape, 1)
        logits = jnp.where(lane < experts, logits, -1e30)
        ex = jnp.exp(logits - jnp.max(logits, axis=1, keepdims=True))
        gate = jnp.sum(jnp.where(lane == me, ex, 0.0), axis=1, keepdims=True) / jnp.sum(ex, axis=1, keepdims=True)
        g = gu[:, :FF]
        u = gu[:, FF:2 * FF]
        s = sig(g)
        sg = g * s
        act_s[...] = (sg * u).astype(low)
        gr_s[...] = (gate * cr.astype(wide)).astype(low)
        dact = mm_nt(gr_s[...], wdown[...])
        dgu_s[:, :FF] = (dact * u * (s + sg * (1.0 - s))).astype(low)
        dgu_s[:, FF:] = (dact * sg).astype(low)
        o = mm(act_s[...], wdown[...]).astype(low)
        of = o.astype(wide)
        gg = jnp.sum(cr.astype(wide) * of, axis=1, keepdims=True)
        wtd = (gate * of).astype(low)
        ib = mm_nt(dgu_s[...], win[...]).astype(low)
        at(k, middle)

        @pl.when(k >= 2)
        def _():
            for n, j in enumerate((one, two)):
                for copy in mixed_copies(slot, n, j):
                    copy.wait()

        for n in range(2):
            x = xv[n]
            ct = cv[slot, n]
            sh = mm(x, wshin[...])
            g2 = sh[:, :hid]
            u2 = sh[:, hid:]
            s2 = sig(g2)
            sg2 = g2 * s2
            sact = (sg2 * u2).astype(low)
            dsact = mm_nt(ct, wshdown[...])
            dsh = jnp.concatenate([dsact * u2 * (s2 + sg2 * (1.0 - s2)), dsact * sg2], axis=1).astype(low)
            p = picks[n].astype(low)
            rows = slice(n * cap, (n + 1) * cap)
            mixed_s[slot, n] = (mm_tn(p, wtd[rows]) + mm(sact, wshdown[...])).astype(low)
            back_s[slot, n] = (mm_tn(p, ib[rows]) + mm_nt(dsh, wshin[...])).astype(low)
            gg_s[k, n] = jnp.sum(jnp.where(picks[n], gg[rows], 0.0), axis=0, keepdims=True)
            gshdown[...] += mm_tn(sact, ct)
            gshin[...] += mm_tn(x, dsh)
        for n, j in enumerate((one, two)):
            for copy in mixed_copies(slot, n, j):
                copy.start()
        at(k, {q: [lambda q=q: core_copy(q).start()] for q in range(steps)})

        @pl.when(k > 0)
        def _():
            gg_copy(k, 0, one).start()

        gg_copy(k, 1, two).start()
        at(k, after)

        @pl.when((k + 1 >= ahead) & (k + 1 < steps))
        def _():
            at(k, {q - 1: before[q] for q in range(ahead, steps)})
            next_one, next_two = pair_index(k + 1)
            for load in x_load(xall.at[next_one], 0, 1 - slot):
                load.start()
            landed(next_two)
            for load in x_load(xall.at[next_two], 1, 1 - slot):
                load.start()
            rank_landed(next_one)
            rank_landed(next_two)

        gdown_acc[...] += mm_tn(act_s[...], gr_s[...])
        gin_acc[...] += mm_tn(xr_s[...], dgu_s[...])
        at(k, {q: [lambda q=q: core_copy(q - 1).wait_send()] if q else [] for q in range(steps)})
        return carry

    lax.fori_loop(0, steps, step, 0)
    gg_out[me] = gg_s[0, 0]
    outs = []
    for pieces, whole, acc in ((gin_out, win, gin_acc), (gdown_out, wdown, gdown_acc)):
        whole[...] = acc[...].astype(low)
        for n, piece in enumerate(pieces):
            rows = piece.shape[0]
            start = lax.rem(pos["Y"] + n, len(pieces)) * rows
            part = whole.at[pl.ds(pl.multiple_of(start, 16), rows)]
            if n and whole is win:
                outs.append(pltpu.make_async_remote_copy(
                    src_ref=part, dst_ref=piece, send_sem=y_send, recv_sem=y_recv,
                    device_id=place.device(place.moved(Y=1)), device_id_type=MESH))
            else:
                outs.append(pltpu.make_async_copy(part, piece, w_sem.at[len(outs)]))
            outs[-1].start()
    for run in late:
        run()
    total = held[0].astype(wide)
    for s in range(1, na):
        j = lax.rem(a + s, na)
        fetch(a_land.at[j], a_recv.at[j], 0)
        total = total + fetched(0)
    gin_acc[:toks, :d] = total
    last = pltpu.make_async_copy(gin_acc.at[pl.ds(0, toks), pl.ds(0, d)], total_out, s_sem.at[0])
    last.start()
    last.wait()
    for out in outs:
        out.wait()
    core_copy(steps - 1).wait_send()
    for k in b_steps[-2:]:
        b_copy(k).wait_send()
    for i in range(1, na):
        a_copy(i).wait_send()
    for conds, copy in ag_sends:
        under(conds(), lambda copy=copy: copy().wait_send())
    for k in (steps - 2, steps - 1):
        one, two = pair_index(k)
        for n, j in enumerate((one, two)):
            for copy in mixed_copies(k % 2, n, j):
                copy.wait()

    def gg_done(k, carry):
        one, two = pair_index(k)

        @pl.when(k > 0)
        def _():
            gg_copy(k, 0, one).wait_send()

        gg_copy(k, 1, two).wait_send()
        return carry

    lax.fori_loop(0, steps, gg_done, 0)

    def gg_wait(s, carry):
        j = lax.rem(me + s, n_exp)
        pltpu.make_async_copy(gg_out.at[j], gg_out.at[j], g_recv.at[j]).wait()
        return carry

    lax.fori_loop(1, n_exp, gg_wait, 0)

    def rank_sent(s, carry):
        rank_copy(s).wait_send()
        return carry

    lax.fori_loop(1, n_exp, rank_sent, 0)


def fused(x, cot_all, rank, win, wdown, wrt, wshin, wshdown, n_dp, n_exp, experts, cap, cid):
    toks, d = x.shape[0], wshdown.shape[1]
    size = sizes(n_dp, n_exp)
    na, nb = size["A"], size["B"]
    steps = na * nb
    hid = wshdown.shape[0]
    low, wide = jnp.bfloat16, jnp.float32
    hbm = pl.BlockSpec(memory_space=pl.ANY)
    vmem = pl.BlockSpec(memory_space=pltpu.VMEM)
    rows = 2 * cap
    block = (toks, d)
    dma = pltpu.SemaphoreType.DMA
    ag_count = 2 + (nb - 1) + 1 + (na - 1) * (2 + nb) + na * (nb - 1)
    flops = 2 * n_exp * (cap * d * FF * 9 + toks * cap * d * 4 + toks * d * hid * 9)
    out = pl.pallas_call(
        functools.partial(fused_kernel, n_dp, n_exp, experts, cap, len(win), len(wdown)),
        in_specs=[hbm, hbm, vmem] + [hbm] * (len(win) + len(wdown) + 3),
        out_shape=[
            jax.ShapeDtypeStruct((n_exp,) + x.shape, low),
            jax.ShapeDtypeStruct((n_exp, toks, MIXED_FIRST), low),
            jax.ShapeDtypeStruct((n_exp, toks, d - MIXED_FIRST), low),
            jax.ShapeDtypeStruct(block, wide),
            jax.ShapeDtypeStruct((n_exp, 1, toks), wide),
            *[jax.ShapeDtypeStruct((d // len(wdown), 2 * FF), low) for _ in wdown],
            *[jax.ShapeDtypeStruct(w.shape, low) for w in wdown],
            jax.ShapeDtypeStruct((d, 2 * hid), wide),
            jax.ShapeDtypeStruct((hid, d), wide),
            jax.ShapeDtypeStruct((steps,) + block, low),
            jax.ShapeDtypeStruct((na * max(nb - 1, 1),) + block, low),
            jax.ShapeDtypeStruct((na,) + block, low),
        ],
        out_specs=[hbm, hbm, hbm, hbm, vmem] + [hbm] * (2 * len(wdown)) + [vmem, vmem, hbm, hbm, hbm],
        scratch_shapes=[
            pltpu.VMEM((d, 2 * FF), low), pltpu.VMEM((FF, d), low), pltpu.VMEM(wrt.shape, low),
            pltpu.VMEM(wshin.shape, low), pltpu.VMEM(wshdown.shape, low), pltpu.VMEM((n_exp, 1, toks), wide),
            pltpu.VMEM((2,) + block, low), pltpu.VMEM((2, 2) + block, low),
            pltpu.VMEM((rows, d), low), pltpu.VMEM((rows, FF), low), pltpu.VMEM((rows, d), low),
            pltpu.VMEM((rows, 2 * FF), low),
            pltpu.VMEM((2, 2) + block, low), pltpu.VMEM((2, 2) + block, low), pltpu.VMEM((na,) + block, low),
            pltpu.VMEM((2,) + block, low), pltpu.VMEM((nb,) + block, low),
            pltpu.VMEM((steps, 2, 1, toks), wide), pltpu.VMEM((d, 2 * FF), wide), pltpu.VMEM((FF, d), wide),
            dma((3 + len(win) + len(wdown),)), dma((2, 2)), dma((2, 2)), dma((2, 2, 2)), dma((nb,)),
            dma((ag_count,)), dma((n_exp,)), dma((steps,)), dma((steps,)),
            dma((na * max(nb - 1, 1),)), dma((na * max(nb - 1, 1),)), dma((na,)), dma((na,)),
            dma((steps, 2)), dma((n_exp,)), dma((n_exp,)), dma((n_exp,)), dma(()), dma(()),
        ],
        compiler_params=pltpu.CompilerParams(collective_id=cid, has_side_effects=True, vmem_limit_bytes=63 * 1024 * 1024),
        cost_estimate=pl.CostEstimate(flops=flops, bytes_accessed=100 * 1024 * 1024, transcendentals=0),
        name="experts_fused",
    )(x, cot_all, rank, *win, *wdown, wrt, wshin, wshdown)
    n = len(wdown)
    return out[1], out[2], out[3], out[4], out[5:5 + n], out[5 + n:5 + 2 * n], out[5 + 2 * n], out[6 + 2 * n]


def attend_kernel(heads_n, experts, tok_ref, gains_ref, full_ref, router_ref, cos_ref, sin_ref, bias_ref,
                  q_ref, k_ref, v_ref, heads_ref, resid_ref, mlp_ref, probs_ref, attn_ref):
    low, wide = jnp.bfloat16, jnp.float32
    width = heads_n * HD
    d = mlp_ref.shape[1]
    scale = HD ** (-0.5)
    inputs = tok_ref[...].astype(wide)
    attn_ref[...] = (inputs * rms_scale(inputs) * gains_ref[0:1, :]).astype(low)
    lane = lax.broadcasted_iota(jnp.int32, (1, HD), 1)
    sign = jnp.where(lane < HD // 2, -1.0, 1.0)

    def turn(g):
        return g * cos_ref[...] + pltpu.roll(g, HD // 2, 1) * sign * sin_ref[...]

    pair = 2 * HD

    def project(j, carry):
        for part, out in ((0, q_ref), (1, k_ref), (2, v_ref)):
            y = mm(attn_ref[...], full_ref[:, pl.ds(pl.multiple_of(part * width + j * pair, HD), pair)])
            for n in range(2):
                one = y[:, n * HD : (n + 1) * HD]
                at = pl.ds(pl.multiple_of(j * pair + n * HD, HD), HD)
                out[:, at] = (turn(one) if part < 2 else one).astype(low)
        return carry

    lax.fori_loop(0, heads_n // 2, project, 0)

    def head(h, carry):
        at = pl.ds(pl.multiple_of(h * HD, HD), HD)
        s = jnp.where(bias_ref[...] > 0.0, mm_nt(q_ref[:, at], k_ref[:, at]) * scale, NEGATIVE)
        e = jnp.exp(s - jnp.max(s, axis=-1, keepdims=True))
        p = e / jnp.sum(e, axis=-1, keepdims=True)
        heads_ref[:, at] = mm(p.astype(low), v_ref[:, at]).astype(low)
        return carry

    lax.fori_loop(0, heads_n, head, 0)
    residual = inputs + mm(heads_ref[...], full_ref[:, 3 * width : 3 * width + d])
    resid_ref[...] = residual
    mlp_ref[...] = (residual * rms_scale(residual) * gains_ref[1:2, :]).astype(low)
    logits = mm_nt(router_ref[...], mlp_ref[...])
    e = jnp.exp(logits - jnp.max(logits, axis=0, keepdims=True))
    probs_ref[...] = e / jnp.sum(e, axis=0, keepdims=True)


def attend(experts, tokens, *args):
    toks, d = tokens.shape
    low, wide = jnp.bfloat16, jnp.float32
    width = H * HD
    shape = jax.ShapeDtypeStruct
    vmem = pl.BlockSpec(memory_space=pltpu.VMEM)
    return pl.pallas_call(
        functools.partial(attend_kernel, H, experts),
        in_specs=[vmem] * (len(args) + 1),
        out_specs=[vmem] * 8,
        out_shape=[shape((toks, width), low)] * 4 + [
            shape((toks, d), wide), shape((toks, d), low), shape((experts, toks), wide), shape((toks, d), low)],
        compiler_params=pltpu.CompilerParams(vmem_limit_bytes=60 * 1024 * 1024),
        cost_estimate=pl.CostEstimate(flops=7 * 10**9, bytes_accessed=24 * 1024 * 1024, transcendentals=0),
        name="attend",
    )(tokens, *args)


def attend_back_kernel(
    heads_n, experts, back_ref, gg_ref, probs_ref, router_ref, mlp_ref, resid_ref, cot_ref, tok_ref, gains_ref, full_ref,
    heads_ref, q_ref, k_ref, v_ref, attn_ref, cos_ref, sin_ref, bias_ref,
    gqkv_ref, gout_ref, gin_ref, small_ref, pg_ref, hg_ref, rl_ref
):
    low, wide = jnp.bfloat16, jnp.float32
    width = heads_n * HD
    d = mlp_ref.shape[1]
    scale = HD ** (-0.5)
    gg = gg_ref[...]
    rp = probs_ref[...]
    logit = (rp * (gg - jnp.sum(gg * rp, axis=0, keepdims=True))).astype(low)
    residual = resid_ref[...]
    r2 = rms_scale(residual)
    n2 = residual * r2
    mg = back_ref[...] + mm_tn(logit, router_ref[...])
    small_ref[...] = jnp.zeros_like(small_ref)
    small_ref[0:experts, :] = mm(logit, mlp_ref[...])
    small_ref[experts + 8 : experts + 9, :] = jnp.sum(mg * n2, axis=0, keepdims=True)
    u = mg * gains_ref[1:2, :]
    resid_grad = cot_ref[...].astype(wide) + r2 * (u - n2 * jnp.mean(u * n2, axis=-1, keepdims=True))
    gin_ref[...] = resid_grad
    rl_ref[...] = resid_grad.astype(low)
    gout_ref[...] = mm_tn(heads_ref[...], rl_ref[...]).astype(low)
    hg_ref[...] = mm_nt(rl_ref[...], full_ref[:, 3 * width : 3 * width + d]).astype(low)
    lane = lax.broadcasted_iota(jnp.int32, (1, HD), 1)
    sign = jnp.where(lane < HD // 2, 1.0, -1.0)

    def turn_back(g):
        return g * cos_ref[...] + pltpu.roll(g * sin_ref[...], HD // 2, 1) * sign

    def head(h, carry):
        at = pl.ds(pl.multiple_of(h * HD, HD), HD)
        q, k, v, hg = q_ref[:, at], k_ref[:, at], v_ref[:, at], hg_ref[:, at]
        s = jnp.where(bias_ref[...] > 0.0, mm_nt(q, k) * scale, NEGATIVE)
        e = jnp.exp(s - jnp.max(s, axis=-1, keepdims=True))
        p = e / jnp.sum(e, axis=-1, keepdims=True)
        dp = mm_nt(hg, v)
        sg = (p * (dp - jnp.sum(dp * p, axis=-1, keepdims=True))).astype(low)
        pg_ref[:, at] = turn_back(mm(sg, k) * scale).astype(low)
        pg_ref[:, pl.ds(pl.multiple_of(width + h * HD, HD), HD)] = turn_back(mm_tn(sg, q) * scale).astype(low)
        pg_ref[:, pl.ds(pl.multiple_of(2 * width + h * HD, HD), HD)] = mm_tn(p.astype(low), hg).astype(low)
        return carry

    lax.fori_loop(0, heads_n, head, 0)
    wide_cols = 640

    def columns(j, carry):
        at = pl.ds(pl.multiple_of(j * wide_cols, 128), wide_cols)
        gqkv_ref[:, at] = mm_tn(attn_ref[...], pg_ref[:, at]).astype(low)
        return carry

    lax.fori_loop(0, 3 * width // wide_cols, columns, 0)
    ag = mm_nt(pg_ref[...], full_ref[:, : 3 * width])
    inputs = tok_ref[...].astype(wide)
    r1 = rms_scale(inputs)
    n1 = inputs * r1
    small_ref[experts : experts + 1, :] = jnp.sum(ag * n1, axis=0, keepdims=True)
    u1 = ag * gains_ref[0:1, :]
    gin_ref[...] += r1 * (u1 - n1 * jnp.mean(u1 * n1, axis=-1, keepdims=True))


def attend_back(experts, *args):
    toks, d = args[4].shape
    low, wide = jnp.bfloat16, jnp.float32
    width = H * HD
    return pl.pallas_call(
        functools.partial(attend_back_kernel, H, experts),
        in_specs=[pl.BlockSpec(memory_space=pltpu.VMEM)] * len(args),
        out_specs=[pl.BlockSpec(memory_space=pltpu.VMEM)] * 4,
        out_shape=[
            jax.ShapeDtypeStruct((d, 3 * width), low),
            jax.ShapeDtypeStruct((width, d), low),
            jax.ShapeDtypeStruct((toks, d), wide),
            jax.ShapeDtypeStruct((experts + 16, d), wide),
        ],
        scratch_shapes=[pltpu.VMEM((toks, 3 * width), low), pltpu.VMEM((toks, width), low), pltpu.VMEM((toks, d), low)],
        compiler_params=pltpu.CompilerParams(vmem_limit_bytes=62 * 1024 * 1024),
        cost_estimate=pl.CostEstimate(flops=14 * 10**9, bytes_accessed=45 * 1024 * 1024, transcendentals=0),
        name="attend_back",
    )(*args)


def norm_kernel(n_dp, n_exp, counts, sq_ref, *refs):
    groups, refs = refs[: sum(counts)], refs[sum(counts) :]
    norm_ref, land, send_sem, recv_sem = refs
    place = Place(n_dp, n_exp)
    place.greet("CBYA", True)
    total = sq_ref[...]
    at = 0
    for count in counts:
        pieces = groups[at : at + count]
        at += count
        rows, cols = pieces[0].shape
        step = 32 if rows % 32 == 0 else rows

        def add(i, acc, pieces=pieces, step=step):
            part = pl.ds(pl.multiple_of(i * step, step), step)
            g = pieces[0][part, :].astype(jnp.float32)
            for piece in pieces[1:]:
                g = g + piece[part, :].astype(jnp.float32)
            return acc + jnp.sum(g * g, axis=0, keepdims=True)

        sums = lax.fori_loop(0, rows // step, add, jnp.zeros((1, cols), jnp.float32))
        total = total + jnp.sum(sums)
    norm_ref[...] = total
    norm_exchange(place, norm_ref, land, send_sem, recv_sem)


def sum_squares(groups, dense_squares, n_dp, n_exp, cid):
    top = max(sizes(n_dp, n_exp).values())
    flat = [g for group in groups for g in group]
    vmem = pl.BlockSpec(memory_space=pltpu.VMEM)
    return pl.pallas_call(
        functools.partial(norm_kernel, n_dp, n_exp, [len(group) for group in groups]),
        out_shape=jax.ShapeDtypeStruct((8, 128), jnp.float32),
        in_specs=[vmem] * (1 + len(flat)),
        out_specs=vmem,
        scratch_shapes=[
            pltpu.VMEM((4, top, 8, 128), jnp.float32),
            pltpu.SemaphoreType.DMA((4, top)),
            pltpu.SemaphoreType.DMA((4, top)),
        ],
        compiler_params=pltpu.CompilerParams(collective_id=cid, has_side_effects=True, vmem_limit_bytes=40 * 1024 * 1024),
        name="sum_squares",
    )(dense_squares, *flat)


def adam_kernel(rates, decays, big, counts, norm_ref, *refs):
    n = len(rates)
    states, grads, at = [], [], 0
    for i in range(n):
        states.append(refs[at : at + 3])
        at += 3
    for i in range(n):
        grads.append(refs[at : at + counts[i]])
        at += counts[i]
    outs = [refs[at + 3 * i : at + 3 * i + 3] for i in range(n)]
    at += 3 * n
    held = []
    for i in range(big):
        held.append((refs[at : at + 3], refs[at + 3 : at + 3 + counts[i]], refs[at + 3 + counts[i]], refs[at + 4 + counts[i]]))
        at += 5 + counts[i]

    def copies(i, j):
        state_v, grad_v, in_sem, out_sem = held[i]
        step = CHUNK if state_v[0].shape[0] % CHUNK == 0 else CHUNK // 2
        part = pl.ds(pl.multiple_of(j * step, step), step)
        pairs = list(zip(states[i] + grads[i], state_v + grad_v))
        ins = [pltpu.make_async_copy(a.at[part], b.at[part], in_sem.at[j, q]) for q, (a, b) in enumerate(pairs)]
        back = [pltpu.make_async_copy(a.at[part], b.at[part], out_sem.at[j, q]) for q, (a, b) in enumerate(zip(state_v, outs[i]))]
        return part, ins, back

    def chunks(i):
        rows = held[i][0][0].shape[0]
        return rows // (CHUNK if rows % CHUNK == 0 else CHUNK // 2)

    for i in range(big):

        def load(j, carry, i=i):
            for copy in copies(i, j)[1]:
                copy.start()
            return carry

        lax.fori_loop(0, chunks(i), load, 0)
    factor = jnp.minimum(1.0, CLIP / jnp.sqrt(norm_ref[0:1, 0:1]))

    def total(pieces, part):
        g = pieces[0][part].astype(jnp.float32)
        for piece in pieces[1:]:
            g = g + piece[part].astype(jnp.float32)
        return g

    for i in range(big, n):
        w, m, v = states[i]
        new = adam_update(w[...], m[...], v[...], total(grads[i], Ellipsis), factor, rates[i], decays[i])
        for out, value in zip(outs[i], new):
            out[...] = value
    for i in range(big):

        def work(j, carry, i=i):
            part, ins, back = copies(i, j)
            for copy in ins:
                copy.wait()
            state_v, grad_v = held[i][0], held[i][1]
            new = adam_update(
                state_v[0][part, :], state_v[1][part, :], state_v[2][part, :], total(grad_v, part), factor, rates[i], decays[i]
            )
            for ref, value in zip(state_v, new):
                ref[part, :] = value
            for copy in back:
                copy.start()
            return carry

        lax.fori_loop(0, chunks(i), work, 0)
    for i in range(big):

        def finish(j, carry, i=i):
            for copy in copies(i, j)[2]:
                copy.wait()
            return carry

        lax.fori_loop(0, chunks(i), finish, 0)


def adam(norm, states, grads, rates, decays, big):
    hbm = pl.BlockSpec(memory_space=pl.ANY)
    vmem = pl.BlockSpec(memory_space=pltpu.VMEM)
    counts = [len(g) for g in grads]
    flat = [a for s in states for a in s] + [a for g in grads for a in g]
    specs = [hbm if i < big else vmem for i in range(len(states)) for _ in range(3)]
    scratch = []
    for i in range(big):
        rows = states[i][0].shape[0]
        pieces = rows // (CHUNK if rows % CHUNK == 0 else CHUNK // 2)
        scratch += [pltpu.VMEM(a.shape, a.dtype) for a in (*states[i], *grads[i])]
        scratch += [pltpu.SemaphoreType.DMA((pieces, 3 + counts[i])), pltpu.SemaphoreType.DMA((pieces, 3))]
    out = pl.pallas_call(
        functools.partial(adam_kernel, rates, decays, big, counts),
        in_specs=[vmem] + specs + [hbm if i < big else vmem for i in range(len(grads)) for _ in range(counts[i])],
        out_specs=specs,
        out_shape=[jax.ShapeDtypeStruct(a.shape, a.dtype) for s in states for a in s],
        scratch_shapes=scratch,
        compiler_params=pltpu.CompilerParams(vmem_limit_bytes=60 * 1024 * 1024),
        name="adam",
    )(norm, *flat)
    return [tuple(out[3 * i : 3 * i + 3]) for i in range(len(states))]


def swap_rows(x, n_dp):
    if n_dp != 2:
        return [lax.all_gather(x, "dp", axis=0, tiled=True)]
    return [x, lax.ppermute(x, "dp", [(0, 1), (1, 0)])]


def in_order(pieces):
    if len(pieces) == 1:
        return pieces[0]
    first = lax.axis_index("dp") == 0
    x, other = pieces
    return jnp.concatenate([jnp.where(first, x, other), jnp.where(first, other, x)], axis=0)


def split_rows(x, n_dp):
    if n_dp != 2:
        return [x]
    rows = x.shape[0] // 2
    top, bottom = x[:rows], x[rows:]
    first = lax.axis_index("dp") == 0
    return [jnp.where(first, top, bottom), jnp.where(first, bottom, top)]


def local(
    tokens,
    lengths,
    routes,
    cotangent,
    norm_gains,
    gains_m,
    gains_v,
    w_qkv,
    m_qkv,
    v_qkv,
    w_out,
    m_out,
    v_out,
    w_shared_in,
    m_shared_in,
    v_shared_in,
    w_shared_down,
    m_shared_down,
    v_shared_down,
    w_router,
    m_router,
    v_router,
    w_expert_in,
    m_expert_in,
    v_expert_in,
    w_expert_down,
    m_expert_down,
    v_expert_down,
):
    both = ("dp", "expert")
    low = jnp.bfloat16
    wide = jnp.float32
    row_count = tokens.shape[0]
    expert_count = w_router.shape[1]
    n_dp = lax.axis_size("dp")
    n_exp = lax.axis_size("expert")
    n_all = n_dp * n_exp
    capacity = min(row_count, (5 * row_count * TOP // (4 * expert_count) + 7) // 8 * 8)
    rows_w = w_qkv.shape[0]
    unit = w_shared_down.shape[0]

    pad = jnp.zeros((rows_w, 128 - expert_count - 2), wide)
    packed = jnp.concatenate([w_qkv, w_out, w_router, norm_gains.T, pad], axis=1).astype(low)
    edown_low = w_expert_down[0].astype(low)
    passed = [edown_low]
    early = HEAD if n_dp == 2 else 0
    if n_dp == 2:
        passed.append(w_expert_in[0, :early].astype(low))
    packed, passed, cot_late = lax.optimization_barrier((packed, passed, cotangent))
    full, *others = gather(packed, passed, n_dp, n_exp, True, 1)
    full = full.reshape(D, -1)
    full, ein_rest, shin_low, shdown_low = lax.optimization_barrier(
        (full, w_expert_in[0, early:].astype(low), w_shared_in.astype(low), w_shared_down.astype(low))
    )
    if n_dp == 2:
        rest_other = lax.ppermute(ein_rest, "dp", [(0, 1), (1, 0)])
        expert_in_full = [passed[1], ein_rest, others[1], rest_other]
        expert_down_full = [passed[0], others[0]]
    else:
        expert_in_full, expert_down_full = swap_rows(ein_rest, n_dp), swap_rows(passed[0], n_dp)
    small_full = full[:, 3 * H * HD + D :]
    router_full = small_full[:, :expert_count]
    gain_one = small_full[:, expert_count].astype(wide)
    gain_two = small_full[:, expert_count + 1].astype(wide)
    cot_all = lax.all_gather(cot_late[:, :GIVEN], "expert", axis=0, tiled=False)
    shin_send = (
        shin_low
        .reshape(rows_w, 2, n_dp, n_exp, unit)
        .transpose(3, 0, 1, 2, 4)
        .reshape(n_exp, rows_w, 2 * n_dp * unit)
    )
    shin_send = jnp.concatenate([shin_send] * n_dp, axis=0)
    shin_mine = lax.all_to_all(shin_send, both, 0, 0, tiled=True).reshape(D, 2 * n_dp * unit)
    shdown_mine = in_order(swap_rows(shdown_low, n_dp))
    half = n_dp * unit

    gain_rows = jnp.stack([gain_one, gain_two])
    router_rows = router_full.T
    cosine, sine_table, allowed = rotary_tables(lengths[0], row_count, HD)
    allowed = allowed.astype(wide)
    queries, keys_rot, values_low, heads_low, residual, mlp_in, probs_rows, attn_in = attend(
        expert_count, tokens, gain_rows, full, router_rows, cosine, sine_table, allowed
    )

    routed = jnp.any(routes[:, :, None] == jnp.arange(expert_count, dtype=jnp.int32), axis=1)
    rank = jnp.where(routed, jnp.cumsum(routed.astype(jnp.int32), axis=0) - 1, -1).astype(wide).T
    hid = (half + 127) // 128 * 128
    cap = (capacity + 15) // 16 * 16
    wrt = jnp.concatenate([router_full, jnp.zeros((D, 128 - expert_count), low)], axis=1)
    gap = jnp.zeros((D, hid - half), low)
    wshin = jnp.concatenate([shin_mine[:, :half], gap, shin_mine[:, half:], gap], axis=1)
    wshdown = jnp.concatenate([shdown_mine, jnp.zeros((hid - half, D), low)], axis=0)
    mixed_a, mixed_b, back_sum, gate_grad, grad_ein, grad_edown, shin_wide, shdown_wide = fused(
        jnp.concatenate([mlp_in, cotangent[:, GIVEN:]], axis=1), cot_all, rank[:, None, :], expert_in_full, expert_down_full, wrt, wshin, wshdown, n_dp, n_exp, expert_count, cap, 2
    )
    mixed_a = lax.psum_scatter(mixed_a, "expert", scatter_dimension=0, tiled=False)
    grad_shin = jnp.concatenate([shin_wide[:, :half], shin_wide[:, hid : hid + half]], axis=1)
    grad_shdown = shdown_wide[:half]
    grad_qkv, grad_out, input_grad, small_rows = attend_back(
        expert_count,
        back_sum,
        gate_grad[:, 0, :],
        probs_rows,
        router_rows,
        mlp_in,
        residual,
        cotangent,
        tokens,
        gain_rows,
        full,
        heads_low,
        queries,
        keys_rot,
        values_low,
        attn_in,
        cosine,
        sine_table,
        allowed,
    )

    shin_back = lax.all_to_all(
        grad_shin.astype(low).reshape(n_all, rows_w, 2 * half), both, 0, 0, tiled=True
    )
    shin_own = jnp.sum(
        shin_back.reshape(n_dp, n_exp, rows_w, 2, n_dp, unit).astype(wide), axis=0
    )
    shin_own = shin_own.transpose(1, 2, 3, 0, 4).reshape(rows_w, 2 * FF)
    shdown_halves = split_rows(grad_shdown, n_dp)
    if n_dp == 2:
        swap = [(0, 1), (1, 0)]
        came = (lax.ppermute(shdown_halves[1], "dp", swap), lax.ppermute(grad_edown[1], "dp", swap))
        grad_qkv, shin_own, came = lax.optimization_barrier((grad_qkv, shin_own, came))
        shdown_own = [shdown_halves[0], came[0]]
        edown_own = [grad_edown[0], came[1]]
        ein_own = list(grad_ein)
    else:
        shdown_own, edown_own, ein_own = (
            [lax.psum_scatter(g[0], "dp", scatter_dimension=0, tiled=True)] for g in (shdown_halves, grad_edown, grad_ein)
        )
    small_grad = jnp.concatenate(
        [small_rows.astype(low).T, jnp.zeros((D, 128 - expert_count - 16), low)], axis=1
    )
    qkv_own, out_own, small_own, dense_squares = reduce_dense(
        [g.reshape(n_all, rows_w, -1) for g in (grad_qkv, grad_out, small_grad)], n_dp, n_exp, 5
    )
    qkv_own, mixed_a, mixed_b = lax.optimization_barrier((qkv_own, mixed_a, mixed_b))
    mixed_b = lax.psum_scatter(mixed_b, "expert", scatter_dimension=0, tiled=False)
    norm = sum_squares([[shin_own], shdown_own, ein_own, edown_own], dense_squares, n_dp, n_exp, 6)
    grad_norm = jnp.sqrt(norm[0, 0])
    weights = (
        norm_gains,
        w_qkv,
        w_out,
        w_shared_in,
        w_shared_down,
        w_router,
        w_expert_in,
        w_expert_down,
    )
    firsts = (
        gains_m,
        m_qkv,
        m_out,
        m_shared_in,
        m_shared_down,
        m_router,
        m_expert_in,
        m_expert_down,
    )
    seconds = (
        gains_v,
        v_qkv,
        v_out,
        v_shared_in,
        v_shared_down,
        v_router,
        v_expert_in,
        v_expert_down,
    )
    rates = (
        GAIN_RATE,
        D ** (-0.5),
        (H * HD // 64) ** (-0.5),
        D ** (-0.5),
        FF ** (-0.5),
        (4 * D) ** (-0.5),
        D ** (-0.5),
        (FF // 64) ** (-0.5),
    )
    decays = (0.0, DECAY, DECAY, DECAY, DECAY, DECAY, DECAY, DECAY)
    owned = (
        [small_own[:, expert_count : expert_count + 16 : 8].T],
        [qkv_own],
        [out_own],
        [shin_own],
        shdown_own,
        [small_own[:, :expert_count].T],
        ein_own,
        edown_own,
    )
    order = (6, 7, 0, 1, 2, 3, 4, 5)
    states = [
        tuple(a.T if i == 5 else a.reshape(a.shape[-2:]) for a in (weights[i], firsts[i], seconds[i])) for i in order
    ]
    fresh = adam(norm, states, [owned[i] for i in order], [rates[i] for i in order], [decays[i] for i in order], 2)
    new = dict(zip(order, fresh))
    updated = [a.T if i == 5 else a.reshape(b.shape) for i in range(8) for a, b in zip(new[i], (weights[i], firsts[i], seconds[i]))]
    mixed_b, *updated = lax.optimization_barrier((mixed_b, *updated))
    mixed = (residual + jnp.concatenate([mixed_a, mixed_b], axis=1).astype(wide)).astype(low)
    return (
        mixed,
        input_grad,
        updated[0],
        updated[1],
        updated[2],
        updated[3],
        updated[4],
        updated[5],
        updated[6],
        updated[7],
        updated[8],
        updated[9],
        updated[10],
        updated[11],
        updated[12],
        updated[13],
        updated[14],
        updated[15],
        updated[16],
        updated[17],
        updated[18],
        updated[19],
        updated[20],
        updated[21],
        updated[22],
        updated[23],
        grad_norm,
    )


def solution(mesh):
    placed = (
        P(("dp", "expert"), None),
        P(("dp", "expert"), None),
        P(("dp", "expert"), None),
        P(("dp", "expert"), None),
        P(None, ("dp", "expert")),
        P(None, ("dp", "expert")),
        P(None, ("dp", "expert")),
        P(("dp", "expert"), None),
        P(("dp", "expert"), None),
        P(("dp", "expert"), None),
        P(("dp", "expert"), None),
        P(("dp", "expert"), None),
        P(("dp", "expert"), None),
        P(("dp", "expert"), None),
        P(("dp", "expert"), None),
        P(("dp", "expert"), None),
        P(("dp", "expert"), None),
        P(("dp", "expert"), None),
        P(("dp", "expert"), None),
        P(("dp", "expert"), None),
        P(("dp", "expert"), None),
        P(("dp", "expert"), None),
        P("expert", "dp", None),
        P("expert", "dp", None),
        P("expert", "dp", None),
        P("expert", "dp", None),
        P("expert", "dp", None),
        P("expert", "dp", None),
    )
    return jax.shard_map(
        local,
        mesh=mesh,
        in_specs=placed,
        out_specs=(
            P(("dp", "expert"), None),
            P(("dp", "expert"), None),
            P(None, ("dp", "expert")),
            P(None, ("dp", "expert")),
            P(None, ("dp", "expert")),
            P(("dp", "expert"), None),
            P(("dp", "expert"), None),
            P(("dp", "expert"), None),
            P(("dp", "expert"), None),
            P(("dp", "expert"), None),
            P(("dp", "expert"), None),
            P(("dp", "expert"), None),
            P(("dp", "expert"), None),
            P(("dp", "expert"), None),
            P(("dp", "expert"), None),
            P(("dp", "expert"), None),
            P(("dp", "expert"), None),
            P(("dp", "expert"), None),
            P(("dp", "expert"), None),
            P(("dp", "expert"), None),
            P("expert", "dp", None),
            P("expert", "dp", None),
            P("expert", "dp", None),
            P("expert", "dp", None),
            P("expert", "dp", None),
            P("expert", "dp", None),
            P(),
        ),
        check_vma=False,
    )
```
